256 devices in a mesh: wide: 8 (over y_lo, x), narrow: 32 (over z, y_hi, core).
Axes of the slice: x: 4, y: 4 (y_hi: 2, y_lo: 2; y = y_hi * 2 + y_lo), z: 8, core: 2. Of those that a mesh axis runs over, the one named last changes fastest.
Arguments:
- iterate: bfloat16 [3584, 18432], P('wide', 'narrow'), may hold values from -0.078125 to 0.078125
Outputs:
- update: bfloat16 [3584, 18432], P('wide', 'narrow')
The draws below stay inside these ranges and needn't reach their ends.
All inputs are finite; a program needn't handle non-finite values.
Results may differ from the reference program's by a relative error of at most 0.0065.
Values may be sent and summed in bfloat16 or wider, within the bound.
No kernel may reach another device: no remote copies, remote signals or barrier semaphores. Data moves between devices by JAX's collectives and lax.ppermute only.
A program may use at most 64 MiB of HBM per device.

```python
import jax
import jax.numpy as jnp

ROWS = 3584
COLS = 18432


def steps_of(stream_key, dims, shards, smallest, top_value):
    loudness, own = 1.0, jax.random.fold_in(stream_key, 6)
    for position, shards_of in shards:
        steps = jnp.exp(jax.random.uniform(jax.random.fold_in(own, position), (shards_of,), jnp.float32, smallest / len(shards), top_value / len(shards)))
        loudness = loudness * jnp.repeat(steps, dims[position] // shards_of).reshape([-1 if axis == position else 1 for axis in range(len(dims))])
    return loudness


def normal_values(own_key, extent, spread, limit, pieces=(), kind=jnp.bfloat16):
    array = spread * jax.random.normal(own_key, extent, jnp.float32)
    if pieces:
        array = array * steps_of(own_key, extent, pieces, -0.22, 0.18)
    return jnp.clip(array, -limit, limit).astype(kind)


def setup_inputs(seed: int = 0) -> dict:
    keys = jax.random.split(jax.random.key(seed), 2)
    return {
        "iterate": normal_values(keys[0], (ROWS, COLS), (0.7 * COLS ** -0.5), 0.078125, ((0, 8), (1, 32))),
    }


coef_a = 3.4445
coef_b = -4.7750
coef_c = 2.0315


def reference(iterate):
    gram = jnp.dot(iterate, iterate.T, preferred_element_type=jnp.float32)
    gram_half = gram.astype(jnp.bfloat16)
    square = jnp.dot(gram_half, gram_half, preferred_element_type=jnp.float32)
    mixer = (coef_b * gram + coef_c * square).astype(jnp.bfloat16)
    product = jnp.dot(mixer, iterate, preferred_element_type=jnp.float32)
    scale = float(COLS) ** 0.5
    return (scale * (coef_a * iterate.astype(jnp.float32) + product)).astype(jnp.bfloat16)
```

```python
import jax
import jax.numpy as jnp
from jax import lax
from jax.sharding import PartitionSpec as P

COLS = 18432

coef_a = 3.4445
coef_b = -4.775
coef_c = 2.0315

X_SIZE, Z_SIZE = 4, 8
f32, bf16 = jnp.float32, jnp.bfloat16


def from_x(value, step):
    pairs = [(y * 4 + (x + step) % 4, y * 4 + x) for y in range(2) for x in range(4)]
    return lax.ppermute(value, "wide", pairs)


def from_y(value):
    return lax.ppermute(value, "wide", [(w, (w + 4) % 8) for w in range(8)])


def from_z(value, step):
    pairs = [(((z + step) % 8) * 4 + r, z * 4 + r) for z in range(8) for r in range(4)]
    return lax.ppermute(value, "narrow", pairs)


def from_y_hi(value):
    return lax.ppermute(value, "narrow", [(n, n ^ 2) for n in range(32)])


def from_core(value):
    return lax.ppermute(value, "narrow", [(n, n ^ 1) for n in range(32)])


def rows_of(left, right):
    return lax.dot_general(left, right, (((1,), (1,)), ((), ())), preferred_element_type=f32)


def dot(left, right):
    return jnp.dot(left, right, preferred_element_type=f32)


def gather_first(own):
    return from_x(own, 1), from_x(own, -1), from_y(own)


def gather_rest(right, left, across):
    half = right.shape[0] // 2
    via_y = from_y(jnp.concatenate([right[:half], left[:half]]))
    via_right = from_x(jnp.concatenate([across[half:], right[:half]]), 1)
    via_left = from_x(jnp.concatenate([across[half:], left[half:]]), -1)
    far = jnp.concatenate([via_right[half:], via_left[half:]])
    across_right = jnp.concatenate([via_y[:half], via_right[:half]])
    across_left = jnp.concatenate([via_y[half:], via_left[:half]])
    cut_a, cut_b = 144, 296
    part_y = from_y(far[:cut_a])
    part_right = from_x(across_right[cut_a:cut_b], 1)
    part_left = from_x(across_left[cut_b:], -1)
    across_far = jnp.concatenate([part_y, part_right, part_left])
    return far, across_right, across_left, across_far


def local(own):
    rows = own.shape[0]
    narrow_pos = lax.axis_index("narrow")
    core = narrow_pos % 2
    z_pos = narrow_pos // 4
    unit = rows // Z_SIZE

    right, left, across = gather_first(own)
    first = jnp.concatenate([own, right, left, across])
    second = jnp.concatenate(gather_rest(right, left, across))

    def core_sum(partial):
        width = partial.shape[1] // 2
        mine = lax.dynamic_slice_in_dim(partial, core * width, width, 1)
        other = lax.dynamic_slice_in_dim(partial, (1 - core) * width, width, 1)
        return mine + from_core(other.astype(bf16)).astype(f32)

    summed = jnp.concatenate([core_sum(rows_of(own, first)), core_sum(rows_of(own, second))], axis=1)
    width = summed.shape[1]
    half = width // 2

    def chunk(step):
        return lax.dynamic_slice_in_dim(summed, ((z_pos + step) % 8) * unit, unit, 0)

    near_up = from_z(chunk(1).astype(bf16), -1)
    near_down = from_z(chunk(-1).astype(bf16), 1)
    up3 = from_z(chunk(3).astype(bf16), -1)
    down3 = from_z(chunk(-3).astype(bf16), 1)
    up4 = from_z(chunk(4)[:, :half].astype(bf16), -2)
    down4 = from_z(chunk(4)[:, half:].astype(bf16), 2)
    up = chunk(2) + up3.astype(f32) + jnp.pad(up4.astype(f32), ((0, 0), (0, half)))
    down = chunk(-2) + down3.astype(f32) + jnp.pad(down4.astype(f32), ((0, 0), (half, 0)))
    far_up = from_z(up.astype(bf16), -2)
    far_down = from_z(down.astype(bf16), 2)
    total = (
        chunk(0)
        + near_up.astype(f32)
        + near_down.astype(f32)
        + far_up.astype(f32)
        + far_down.astype(f32)
    )
    sent = total.astype(bf16)
    gram = (sent.astype(f32) + from_y_hi(sent).astype(f32)).astype(bf16)

    up1, down1 = from_z(gram, 1), from_z(gram, -1)
    up2, down2 = from_z(gram, 2), from_z(gram, -2)
    up3, down3 = from_z(up2, 1), from_z(down2, -1)
    up4 = from_z(up2[:, :half], 2)
    down4 = from_z(down2[:, half:], -2)
    four = jnp.concatenate([up4, down4], axis=1)
    block = jnp.zeros((rows, width), bf16)
    for step, piece in ((0, gram), (1, up1), (-1, down1), (2, up2), (-2, down2), (3, up3), (-3, down3), (4, four)):
        block = lax.dynamic_update_slice_in_dim(block, piece, ((z_pos + step) % 8) * unit, 0)
    other = from_core(block)
    low = jnp.where(core == 0, block, other)
    high = jnp.where(core == 0, other, block)
    gram_first = jnp.concatenate([low[:, :half], high[:, :half]], axis=1)
    gram_second = jnp.concatenate([low[:, half:], high[:, half:]], axis=1)

    again = dot(gram_first, first) + dot(gram_second, second)
    inner = (coef_b * own.astype(f32) + coef_c * again).astype(bf16)
    right, left, across = gather_first(inner)
    product = dot(gram_first, jnp.concatenate([inner, right, left, across]))
    product = product + dot(gram_second, jnp.concatenate(gather_rest(right, left, across)))
    scale = float(COLS) ** 0.5
    return (scale * (coef_a * own.astype(f32) + product)).astype(bf16)


def solution(mesh):
    return jax.shard_map(
        local,
        mesh=mesh,
        in_specs=(P("wide", "narrow"),),
        out_specs=P("wide", "narrow"),
        check_vma=False,
    )
```

```python
import jax
import jax.numpy as jnp
from jax import lax
from jax.sharding import PartitionSpec as P

COLS = 18432

coef_a = 3.4445
coef_b = -4.775
coef_c = 2.0315

Z_SIZE = 8
f32, bf16 = jnp.float32, jnp.bfloat16


def from_x(value, step):
    pairs = [(y * 4 + (x + step) % 4, y * 4 + x) for y in range(2) for x in range(4)]
    return lax.ppermute(value, "wide", pairs)


def from_y(value):
    return lax.ppermute(value, "wide", [(w, (w + 4) % 8) for w in range(8)])


def from_z(value, step):
    pairs = [(((z + step) % 8) * 4 + r, z * 4 + r) for z in range(8) for r in range(4)]
    return lax.ppermute(value, "narrow", pairs)


def from_y_hi(value):
    return lax.ppermute(value, "narrow", [(n, n ^ 2) for n in range(32)])


def from_core(value):
    return lax.ppermute(value, "narrow", [(n, n ^ 1) for n in range(32)])


def rows_of(left, right):
    return lax.dot_general(left, right, (((1,), (1,)), ((), ())), preferred_element_type=f32)


def dot(left, right):
    return jnp.dot(left, right, preferred_element_type=f32)


def cat(*parts, axis=0):
    return jnp.concatenate(parts, axis=axis)


def gather_first(own):
    return from_x(own, 1), from_x(own, -1), from_y(own)


def gather_second(right, left, across):
    half = right.shape[0] // 16 * 8
    via_y = from_y(cat(right[:half], left[:half]))
    via_right = from_x(cat(across[half:], right[:half]), 1)
    via_left = from_x(cat(across[half:], left[half:]), -1)
    rest = right.shape[0] - half
    far = cat(via_right[rest:], via_left[rest:])
    return far, cat(via_y[:half], via_right[:rest]), cat(via_y[half:], via_left[:rest])


def gather_third(far, across_right, across_left):
    third = far.shape[0] // 24 * 8
    part_y = from_y(far[:third])
    part_right = from_x(across_right[third : 2 * third], 1)
    part_left = from_x(across_left[2 * third :], -1)
    return cat(part_y, part_right, part_left)


def local(own):
    rows = own.shape[0]
    narrow_pos = lax.axis_index("narrow")
    core = narrow_pos % 2
    z_pos = narrow_pos // 4
    unit = rows // Z_SIZE

    def core_sum(partial):
        width = partial.shape[1] // 2
        mine = lax.dynamic_slice_in_dim(partial, core * width, width, 1)
        other = lax.dynamic_slice_in_dim(partial, (1 - core) * width, width, 1)
        return mine + from_core(other.astype(bf16)).astype(f32)

    def z_sum(summed):
        half = summed.shape[1] // 2

        def chunk(step):
            return lax.dynamic_slice_in_dim(summed, ((z_pos + step) % 8) * unit, unit, 0)

        up3 = from_z(chunk(3).astype(bf16), -1)
        down3 = from_z(chunk(-3).astype(bf16), 1)
        up4 = from_z(chunk(4)[:, :half].astype(bf16), -2)
        down4 = from_z(chunk(4)[:, half:].astype(bf16), 2)
        near_up = from_z(chunk(1).astype(bf16), -1)
        near_down = from_z(chunk(-1).astype(bf16), 1)
        up = chunk(2) + up3.astype(f32) + jnp.pad(up4.astype(f32), ((0, 0), (0, half)))
        down = chunk(-2) + down3.astype(f32) + jnp.pad(down4.astype(f32), ((0, 0), (half, 0)))
        far_up = from_z(up.astype(bf16), -2)
        far_down = from_z(down.astype(bf16), 2)
        near = chunk(0) + near_up.astype(f32) + near_down.astype(f32)
        return near + far_up.astype(f32) + far_down.astype(f32)

    def y_hi_sum(total):
        sent = total.astype(bf16)
        return (sent.astype(f32) + from_y_hi(sent).astype(f32)).astype(bf16)

    def both_cores(block):
        other = from_core(block)
        low = jnp.where(core == 0, block, other)
        high = jnp.where(core == 0, other, block)
        half = block.shape[1] // 2
        return cat(low[:, :half], high[:, :half], axis=1), cat(low[:, half:], high[:, half:], axis=1)

    def turned(block, shift):
        return lax.dynamic_slice_in_dim(cat(block, block), (shift % 8) * unit, rows, 0)

    right, left, across = gather_first(own)
    first = cat(own, right, left, across)
    gram_a = y_hi_sum(z_sum(core_sum(rows_of(own, first))))
    far, across_right, across_left = gather_second(right, left, across)
    across_far = gather_third(far, across_right, across_left)
    second = cat(far, across_right, across_left, across_far)
    gram_b = y_hi_sum(z_sum(core_sum(rows_of(own, second))))
    gram = cat(gram_a, gram_b, axis=1)

    up1, down1 = from_z(gram, 1), from_z(gram, -1)
    up2, down2 = from_z(gram, 2), from_z(gram, -2)
    half = gram.shape[1] // 2
    up3, down3 = from_z(up2, 1), from_z(down2, -1)
    up4 = from_z(up2[:, :half], 2)
    down4 = from_z(down2[:, half:], -2)

    near_a, near_b = both_cores(cat(down2, down1, gram, up1, up2))
    y_near = dot(near_a, first) + dot(near_b, second)
    far_a, far_b = both_cores(cat(up3, cat(up4, down4, axis=1), down3))
    y_far = dot(far_a, first) + dot(far_b, second)

    near0, far0 = y_near.astype(bf16), y_far.astype(bf16)
    near1, far1 = gather_first(near0), gather_first(far0)
    near2, far2 = gather_second(*near1), gather_second(*far1)
    near3, far3 = gather_third(*near2), gather_third(*far2)
    y_first = cat(*[turned(cat(n, f), 2 - z_pos) for n, f in zip((near0, *near1), (far0, *far1))])
    y_second = cat(*[turned(cat(n, f), 2 - z_pos) for n, f in zip((*near2, near3), (*far2, far3))])
    gram_first, gram_second = cat(near_a, far_a), cat(near_b, far_b)
    product = dot(gram_first, y_first) + dot(gram_second, y_second)
    added = turned(coef_b * cat(y_near, y_far) + coef_c * product, 2 - z_pos)
    scale = float(COLS) ** 0.5
    return (scale * (coef_a * own.astype(f32) + added)).astype(bf16)


def solution(mesh):
    return jax.shard_map(
        local,
        mesh=mesh,
        in_specs=(P("wide", "narrow"),),
        out_specs=P("wide", "narrow"),
        check_vma=False,
    )
```

```python
import jax
import jax.numpy as jnp
from jax import lax
from jax.sharding import PartitionSpec as P

COLS = 18432

coef_a = 3.4445
coef_b = -4.775
coef_c = 2.0315

Z_SIZE = 8
f32, bf16 = jnp.float32, jnp.bfloat16


def from_x(value, step):
    pairs = [(y * 4 + (x + step) % 4, y * 4 + x) for y in range(2) for x in range(4)]
    return lax.ppermute(value, "wide", pairs)


def from_y(value):
    return lax.ppermute(value, "wide", [(w, (w + 4) % 8) for w in range(8)])


def from_z(value, step):
    pairs = [(((z + step) % 8) * 4 + r, z * 4 + r) for z in range(8) for r in range(4)]
    return lax.ppermute(value, "narrow", pairs)


def from_y_hi(value):
    return lax.ppermute(value, "narrow", [(n, n ^ 2) for n in range(32)])


def from_y_both(value):
    pairs = [((w, n), ((w + 4) % 8, n ^ 2)) for w in range(8) for n in range(32)]
    return lax.ppermute(value, ("wide", "narrow"), [(a * 32 + b, c * 32 + d) for (a, b), (c, d) in pairs])


def from_core(value):
    return lax.ppermute(value, "narrow", [(n, n ^ 1) for n in range(32)])


def rows_of(left, right):
    return lax.dot_general(left, right, (((1,), (1,)), ((), ())), preferred_element_type=f32)


def dot(left, right):
    return jnp.dot(left, right, preferred_element_type=f32)


def cat(*parts, axis=0):
    return jnp.concatenate(parts, axis=axis)


def gather_first(own):
    return from_x(own, 1), from_x(own, -1), from_y(own)


def gather_second(right, left, across):
    half = right.shape[0] // 16 * 8
    via_y = from_y(cat(right[:half], left[:half]))
    via_right = from_x(cat(across[half:], right[:half]), 1)
    via_left = from_x(cat(across[half:], left[half:]), -1)
    rest = right.shape[0] - half
    far = cat(via_right[rest:], via_left[rest:])
    return far, cat(via_y[:half], via_right[:rest]), cat(via_y[half:], via_left[:rest])


def gather_third(far, across_right, across_left):
    third = far.shape[0] // 24 * 8
    part_y = from_y(far[:third])
    part_right = from_x(across_right[third : 2 * third], 1)
    part_left = from_x(across_left[2 * third :], -1)
    return cat(part_y, part_right, part_left)


def local(own):
    rows = own.shape[0]
    narrow_pos = lax.axis_index("narrow")
    core = narrow_pos % 2
    z_pos = narrow_pos // 4
    unit = rows // Z_SIZE

    def turned(block, shift):
        return lax.dynamic_slice_in_dim(cat(block, block), (shift % 8) * unit, rows, 0)

    right, left, across = gather_first(own)
    half_rows = rows // 2
    far = cat(from_x(right[:half_rows], 1), from_x(left[half_rows:], -1))
    same = cat(own, right, left, far)

    def core_halves(partial):
        width = partial.shape[1] // 2
        mine = lax.dynamic_slice_in_dim(partial, core * width, width, 1)
        other = lax.dynamic_slice_in_dim(partial, (1 - core) * width, width, 1)
        return mine, other.astype(bf16)

    own_mine, own_other = core_halves(rows_of(own, same))
    across_mine, across_other = core_halves(rows_of(across, same))
    summed = cat(own_mine, across_mine, axis=1) + from_core(cat(own_other, across_other, axis=1)).astype(f32)
    width = summed.shape[1]
    half = width // 2

    def chunk(step):
        return lax.dynamic_slice_in_dim(summed, ((z_pos + step) % 8) * unit, unit, 0)

    up3 = from_z(chunk(3).astype(bf16), -1)
    down3 = from_z(chunk(-3).astype(bf16), 1)
    up4 = from_z(chunk(4)[:, :half].astype(bf16), -2)
    down4 = from_z(chunk(4)[:, half:].astype(bf16), 2)
    near_up = from_z(chunk(1).astype(bf16), -1)
    near_down = from_z(chunk(-1).astype(bf16), 1)
    up = chunk(2) + up3.astype(f32) + jnp.pad(up4.astype(f32), ((0, 0), (0, half)))
    down = chunk(-2) + down3.astype(f32) + jnp.pad(down4.astype(f32), ((0, 0), (half, 0)))
    far_up = from_z(up.astype(bf16), -2)
    far_down = from_z(down.astype(bf16), 2)
    total = chunk(0) + near_up.astype(f32) + near_down.astype(f32)
    total = (total + far_up.astype(f32) + far_down.astype(f32)).astype(bf16)

    kept, given = total[:, :half], total[:, half:]
    gram_same = kept.astype(f32) + from_y_hi(kept).astype(f32)
    gram_other = from_y(given).astype(f32) + from_y_both(given).astype(f32)
    gram = cat(gram_same, gram_other, axis=1).astype(bf16)

    up1, down1 = from_z(gram, 1), from_z(gram, -1)
    up2, down2 = from_z(gram, 2), from_z(gram, -2)
    up3, down3 = from_z(up2, 1), from_z(down2, -1)
    up4 = from_z(up2[:, :half], 2)
    down4 = from_z(down2[:, half:], -2)
    block = cat(down2, down1, gram, up1, up2, up3, cat(up4, down4, axis=1), down3)
    other = from_core(block)
    low = jnp.where(core == 0, block, other)
    high = jnp.where(core == 0, other, block)
    gram_same = cat(low[:, :half], high[:, :half], axis=1)
    gram_other = cat(low[:, half:], high[:, half:], axis=1)

    others = cat(across, from_x(across, 1), from_x(across, -1), from_y(far))
    found = dot(gram_same, same) + dot(gram_other, others)

    sent = turned(found, 2 - z_pos).astype(bf16)
    near = gather_first(sent)
    second = gather_second(*near)
    third = gather_third(*second)
    right, left, across = near
    far, across_right, across_left = second
    product = dot(gram_same, cat(sent, right, left, far))
    product = product + dot(gram_other, cat(across, across_right, across_left, third))
    added = turned(coef_b * found + coef_c * product, 2 - z_pos)
    scale = float(COLS) ** 0.5
    return (scale * (coef_a * own.astype(f32) + added)).astype(bf16)


def solution(mesh):
    return jax.shard_map(
        local,
        mesh=mesh,
        in_specs=(P("wide", "narrow"),),
        out_specs=P("wide", "narrow"),
        check_vma=False,
    )
```

```python
import jax
import jax.numpy as jnp
from jax import lax
from jax.sharding import PartitionSpec as P

COLS = 18432

coef_a = 3.4445
coef_b = -4.775
coef_c = 2.0315

Z_SIZE = 8
f32, bf16 = jnp.float32, jnp.bfloat16


def from_x(value, step):
    pairs = [(y * 4 + (x + step) % 4, y * 4 + x) for y in range(2) for x in range(4)]
    return lax.ppermute(value, "wide", pairs)


def from_y(value):
    return lax.ppermute(value, "wide", [(w, (w + 4) % 8) for w in range(8)])


def from_z(value, step):
    pairs = [(((z + step) % 8) * 4 + r, z * 4 + r) for z in range(8) for r in range(4)]
    return lax.ppermute(value, "narrow", pairs)


def from_y_hi(value):
    return lax.ppermute(value, "narrow", [(n, n ^ 2) for n in range(32)])


def from_y_both(value):
    pairs = [((w, n), ((w + 4) % 8, n ^ 2)) for w in range(8) for n in range(32)]
    return lax.ppermute(value, ("wide", "narrow"), [(a * 32 + b, c * 32 + d) for (a, b), (c, d) in pairs])


def from_core(value):
    return lax.ppermute(value, "narrow", [(n, n ^ 1) for n in range(32)])


def rows_of(left, right):
    return lax.dot_general(left, right, (((1,), (1,)), ((), ())), preferred_element_type=f32)


def dot(left, right):
    return jnp.dot(left, right, preferred_element_type=f32)


def cat(*parts, axis=0):
    return jnp.concatenate(parts, axis=axis)


def gather_first(own):
    return from_x(own, 1), from_x(own, -1), from_y(own)


def gather_second(right, left, across):
    half = right.shape[0] // 16 * 8
    via_y = from_y(cat(right[:half], left[:half]))
    via_right = from_x(cat(across[half:], right[:half]), 1)
    via_left = from_x(cat(across[half:], left[half:]), -1)
    rest = right.shape[0] - half
    far = cat(via_right[rest:], via_left[rest:])
    return far, cat(via_y[:half], via_right[:rest]), cat(via_y[half:], via_left[:rest])


def gather_third(far, across_right, across_left):
    third = far.shape[0] // 24 * 8
    part_y = from_y(far[:third])
    part_right = from_x(across_right[third : 2 * third], 1)
    part_left = from_x(across_left[2 * third :], -1)
    return cat(part_y, part_right, part_left)


def local(own):
    rows = own.shape[0]
    narrow_pos = lax.axis_index("narrow")
    core = narrow_pos % 2
    z_pos = narrow_pos // 4
    unit = rows // Z_SIZE

    right, left, across = gather_first(own)
    half_rows = rows // 2
    far = cat(from_x(right[:half_rows], 1), from_x(left[half_rows:], -1))
    same = cat(own, right, left, far)

    width = 2 * rows
    both = cat(own, across)
    given = rows_of(both, lax.dynamic_slice_in_dim(same, (1 - core) * width, width, 0)).astype(bf16)
    kept = rows_of(both, lax.dynamic_slice_in_dim(same, core * width, width, 0))
    summed = (kept + from_core(given).astype(f32)).reshape(2, rows, width)

    def chunk(step):
        return lax.dynamic_slice_in_dim(summed, ((z_pos + step) % 8) * unit, unit, 1)

    up3 = from_z(chunk(3).astype(bf16), -1)
    down3 = from_z(chunk(-3).astype(bf16), 1)
    up4 = from_z(chunk(4)[:1].astype(bf16), -2)
    down4 = from_z(chunk(4)[1:].astype(bf16), 2)
    up = chunk(2) + up3.astype(f32) + jnp.pad(up4.astype(f32), ((0, 1), (0, 0), (0, 0)))
    down = chunk(-2) + down3.astype(f32) + jnp.pad(down4.astype(f32), ((1, 0), (0, 0), (0, 0)))
    up, down, next_up, next_down = lax.optimization_barrier(
        (up.astype(bf16), down.astype(bf16), chunk(1).astype(bf16), chunk(-1).astype(bf16))
    )
    far_up, far_down = from_z(up, -2), from_z(down, 2)
    near_up, near_down = from_z(next_up, -1), from_z(next_down, 1)
    total = chunk(0) + near_up.astype(f32) + near_down.astype(f32)
    total = (total + far_up.astype(f32) + far_down.astype(f32)).astype(bf16)

    others = (from_x(across, 1), from_x(across, -1), from_y(far))
    total, *others = lax.optimization_barrier((total, *others))

    gram_same = total[0].astype(f32) + from_y_hi(total[0]).astype(f32)
    gram_other = from_y(total[1]).astype(f32) + from_y_both(total[1]).astype(f32)
    gram = jnp.stack([gram_same, gram_other]).astype(bf16)

    up1, down1 = from_z(gram, 1), from_z(gram, -1)
    up2, down2 = from_z(gram, 2), from_z(gram, -2)
    up3, down3 = from_z(up2, 1), from_z(down2, -1)
    up4, down4 = from_z(up2[:1], 2), from_z(down2[1:], -2)
    block = jnp.zeros((2, rows, width), bf16)
    pieces = ((0, gram), (1, up1), (-1, down1), (2, up2), (-2, down2), (3, up3), (-3, down3), (4, cat(up4, down4)))
    for step, piece in pieces:
        block = lax.dynamic_update_slice_in_dim(block, piece, ((z_pos + step) % 8) * unit, 1)
    other = from_core(block)
    low = jnp.where(core == 0, block, other)
    high = jnp.where(core == 0, other, block)
    gram_rows = cat(low[0], high[0], low[1], high[1], axis=1)

    found = dot(gram_rows, cat(same, across, *others))
    sent = found.astype(bf16)
    right, left, across = gather_first(sent)
    far, across_right, across_left = gather_second(right, left, across)
    across_far = gather_third(far, across_right, across_left)
    three, seven = 3 * rows, 7 * rows
    product = dot(gram_rows[:, :three], cat(sent, right, left))
    product = product + dot(gram_rows[:, three:seven], cat(far, across, across_right, across_left))
    start = coef_a * own.astype(f32) + coef_b * found + coef_c * product
    scale = float(COLS) ** 0.5
    return (scale * (start + coef_c * dot(gram_rows[:, seven:], across_far))).astype(bf16)


def solution(mesh):
    return jax.shard_map(
        local,
        mesh=mesh,
        in_specs=(P("wide", "narrow"),),
        out_specs=P("wide", "narrow"),
        check_vma=False,
    )
```

```python
import jax
import jax.numpy as jnp
from jax import lax
from jax.sharding import PartitionSpec as P

COLS = 18432

coef_a = 3.4445
coef_b = -4.775
coef_c = 2.0315

Z_SIZE = 8
f32, bf16 = jnp.float32, jnp.bfloat16


def from_x(value, step):
    pairs = [(y * 4 + (x + step) % 4, y * 4 + x) for y in range(2) for x in range(4)]
    return lax.ppermute(value, "wide", pairs)


def from_y(value):
    return lax.ppermute(value, "wide", [(w, (w + 4) % 8) for w in range(8)])


def from_z(value, step):
    pairs = [(((z + step) % 8) * 4 + r, z * 4 + r) for z in range(8) for r in range(4)]
    return lax.ppermute(value, "narrow", pairs)


def from_y_hi(value):
    return lax.ppermute(value, "narrow", [(n, n ^ 2) for n in range(32)])


def from_y_both(value):
    pairs = [((w, n), ((w + 4) % 8, n ^ 2)) for w in range(8) for n in range(32)]
    return lax.ppermute(value, ("wide", "narrow"), [(a * 32 + b, c * 32 + d) for (a, b), (c, d) in pairs])


def from_core(value):
    return lax.ppermute(value, "narrow", [(n, n ^ 1) for n in range(32)])


def rows_of(left, right):
    return lax.dot_general(left, right, (((1,), (1,)), ((), ())), preferred_element_type=f32)


def dot(left, right):
    return jnp.dot(left, right, preferred_element_type=f32)


def cat(*parts, axis=0):
    return jnp.concatenate(parts, axis=axis)


def gather_first(own):
    return from_x(own, 1), from_x(own, -1), from_y(own)


def gather_second(right, left, across):
    half = right.shape[0] // 16 * 8
    via_y = from_y(cat(right[:half], left[:half]))
    via_right = from_x(cat(across[half:], right[:half]), 1)
    via_left = from_x(cat(across[half:], left[half:]), -1)
    rest = right.shape[0] - half
    far = cat(via_right[rest:], via_left[rest:])
    return far, cat(via_y[:half], via_right[:rest]), cat(via_y[half:], via_left[:rest])


def gather_third(far, across_right, across_left):
    third = far.shape[0] // 24 * 8
    part_y = from_y(far[:third])
    part_right = from_x(across_right[third : 2 * third], 1)
    part_left = from_x(across_left[2 * third :], -1)
    return cat(part_y, part_right, part_left)


def local(own):
    rows = own.shape[0]
    narrow_pos = lax.axis_index("narrow")
    core = narrow_pos % 2
    z_pos = narrow_pos // 4
    unit = rows // Z_SIZE

    right, left, across = gather_first(own)
    half_rows = rows // 2
    far = cat(from_x(right[:half_rows], 1), from_x(left[half_rows:], -1))
    same = cat(own, right, left, far)

    width = 2 * rows
    both = cat(own, across)
    given = rows_of(both, lax.dynamic_slice_in_dim(same, (1 - core) * width, width, 0)).astype(bf16)
    kept = lax.optimization_barrier(rows_of(both, lax.dynamic_slice_in_dim(same, core * width, width, 0)))
    summed = (kept + from_core(given).astype(f32)).reshape(2, rows, width)

    def chunk(step):
        return lax.dynamic_slice_in_dim(summed, ((z_pos + step) % 8) * unit, unit, 1)

    up3 = from_z(chunk(3).astype(bf16), -1)
    down3 = from_z(chunk(-3).astype(bf16), 1)
    up4 = from_z(chunk(4)[:1].astype(bf16), -2)
    down4 = from_z(chunk(4)[1:].astype(bf16), 2)
    up = chunk(2) + up3.astype(f32) + jnp.pad(up4.astype(f32), ((0, 1), (0, 0), (0, 0)))
    down = chunk(-2) + down3.astype(f32) + jnp.pad(down4.astype(f32), ((1, 0), (0, 0), (0, 0)))
    others = (from_x(across, 1), from_x(across, -1), from_y(far))
    up, down, next_up, next_down, *others = lax.optimization_barrier(
        (up.astype(bf16), down.astype(bf16), chunk(1).astype(bf16), chunk(-1).astype(bf16), *others)
    )
    far_up, far_down = from_z(up, -2), from_z(down, 2)
    near_up, near_down = from_z(next_up, -1), from_z(next_down, 1)
    total = chunk(0) + near_up.astype(f32) + near_down.astype(f32)
    total = (total + far_up.astype(f32) + far_down.astype(f32)).astype(bf16)

    gram_same = total[0].astype(f32) + from_y_hi(total[0]).astype(f32)
    gram_other = from_y(total[1]).astype(f32) + from_y_both(total[1]).astype(f32)
    gram = jnp.stack([gram_same, gram_other]).astype(bf16)

    up1, down1 = from_z(gram, 1), from_z(gram, -1)
    up2, down2 = from_z(gram, 2), from_z(gram, -2)
    up3, down3 = from_z(up2, 1), from_z(down2, -1)
    up4, down4 = from_z(up2[:1], 2), from_z(down2[1:], -2)
    block = jnp.zeros((2, rows, width), bf16)
    pieces = ((0, gram), (1, up1), (-1, down1), (2, up2), (-2, down2), (3, up3), (-3, down3), (4, cat(up4, down4)))
    for step, piece in pieces:
        block = lax.dynamic_update_slice_in_dim(block, piece, ((z_pos + step) % 8) * unit, 1)
    other = from_core(block)
    low = jnp.where(core == 0, block, other)
    high = jnp.where(core == 0, other, block)
    gram_rows = cat(low[0], high[0], low[1], high[1], axis=1)

    found = dot(gram_rows[:, : 2 * width], same) + dot(gram_rows[:, 2 * width :], cat(across, *others))
    sent = found.astype(bf16)
    right, left, across = gather_first(sent)
    far, across_right, across_left = gather_second(right, left, across)
    across_far = gather_third(far, across_right, across_left)
    three, seven = 3 * rows, 7 * rows
    product = dot(gram_rows[:, :three], cat(sent, right, left))
    product = product + dot(gram_rows[:, three:seven], cat(far, across, across_right, across_left))
    start = coef_a * own.astype(f32) + coef_b * found + coef_c * product
    scale = float(COLS) ** 0.5
    return (scale * (start + coef_c * dot(gram_rows[:, seven:], across_far))).astype(bf16)


def solution(mesh):
    return jax.shard_map(
        local,
        mesh=mesh,
        in_specs=(P("wide", "narrow"),),
        out_specs=P("wide", "narrow"),
        check_vma=False,
    )
```

```python
import jax
import jax.numpy as jnp
from jax import lax
from jax.sharding import PartitionSpec as P

COLS = 18432

coef_a = 3.4445
coef_b = -4.775
coef_c = 2.0315

Z_SIZE = 8
f32, bf16 = jnp.float32, jnp.bfloat16


def from_x(value, step):
    pairs = [(y * 4 + (x + step) % 4, y * 4 + x) for y in range(2) for x in range(4)]
    return lax.ppermute(value, "wide", pairs)


def from_y(value):
    return lax.ppermute(value, "wide", [(w, (w + 4) % 8) for w in range(8)])


def from_z(value, step):
    pairs = [(((z + step) % 8) * 4 + r, z * 4 + r) for z in range(8) for r in range(4)]
    return lax.ppermute(value, "narrow", pairs)


def from_y_hi(value):
    return lax.ppermute(value, "narrow", [(n, n ^ 2) for n in range(32)])


def from_y_both(value):
    pairs = [((w, n), ((w + 4) % 8, n ^ 2)) for w in range(8) for n in range(32)]
    return lax.ppermute(value, ("wide", "narrow"), [(a * 32 + b, c * 32 + d) for (a, b), (c, d) in pairs])


def from_core(value):
    return lax.ppermute(value, "narrow", [(n, n ^ 1) for n in range(32)])


def rows_of(left, right):
    return lax.dot_general(left, right, (((1,), (1,)), ((), ())), preferred_element_type=f32)


def dot(left, right):
    return jnp.dot(left, right, preferred_element_type=f32)


def cat(*parts, axis=0):
    return jnp.concatenate(parts, axis=axis)


def second_parts(right, left, across):
    half = right.shape[0] // 16 * 8
    return cat(right[:half], left[:half]), cat(across[half:], right[:half]), cat(across[half:], left[half:])


def second_blocks(rows, via_y, via_right, via_left):
    half = rows // 16 * 8
    rest = rows - half
    far = cat(via_right[rest:], via_left[rest:])
    return far, cat(via_y[:half], via_right[:rest]), cat(via_y[half:], via_left[:rest])


def third_parts(far, across_right, across_left):
    third = far.shape[0] // 24 * 8
    return far[:third], across_right[third : 2 * third], across_left[2 * third :]


def send(to_y, to_left, to_right):
    return from_y(to_y), from_x(to_left, 1), from_x(to_right, -1)


def send_both(parts_a, parts_b):
    cuts = [part.shape[0] for part in parts_a]
    got = send(*[cat(a, b) for a, b in zip(parts_a, parts_b)])
    return [g[:cut] for g, cut in zip(got, cuts)], [g[cut:] for g, cut in zip(got, cuts)]


def local(own):
    rows = own.shape[0]
    narrow_pos = lax.axis_index("narrow")
    core = narrow_pos % 2
    z_pos = narrow_pos // 4
    unit = rows // Z_SIZE

    across, right, left = send(own, own, own)
    half_rows = rows // 2
    far = cat(from_x(right[:half_rows], 1), from_x(left[half_rows:], -1))
    same = cat(own, right, left, far)

    width = 2 * rows
    both = cat(own, across)
    given = rows_of(both, lax.dynamic_slice_in_dim(same, (1 - core) * width, width, 0)).astype(bf16)
    kept = lax.optimization_barrier(rows_of(both, lax.dynamic_slice_in_dim(same, core * width, width, 0)))
    summed = (kept + from_core(given).astype(f32)).reshape(2, rows, width)

    def chunk(step):
        return lax.dynamic_slice_in_dim(summed, ((z_pos + step) % 8) * unit, unit, 1)

    opposite = chunk(4).astype(bf16)
    up = jnp.pad(from_z(opposite[:1], -1), ((0, 1), (0, 0), (0, 0)))
    down = jnp.pad(from_z(opposite[1:], 1), ((1, 0), (0, 0), (0, 0)))
    for step in (3, 2):
        up = from_z((chunk(step) + up.astype(f32)).astype(bf16), -1)
        down = from_z((chunk(-step) + down.astype(f32)).astype(bf16), 1)
    others = send(far, across, across)
    up, down, *others = lax.optimization_barrier((up, down, *others))
    up = from_z((chunk(1) + up.astype(f32)).astype(bf16), -1)
    down = from_z((chunk(-1) + down.astype(f32)).astype(bf16), 1)
    total = (chunk(0) + up.astype(f32) + down.astype(f32)).astype(bf16)

    gram_same = total[0].astype(f32) + from_y_hi(total[0]).astype(f32)
    gram_other = from_y(total[1]).astype(f32) + from_y_both(total[1]).astype(f32)
    gram = jnp.stack([gram_same, gram_other]).astype(bf16)

    up1, down1 = from_z(gram, 1), from_z(gram, -1)
    up2, down2 = from_z(up1, 1), from_z(down1, -1)
    up3, down3 = from_z(up2, 1), from_z(down2, -1)
    up4, down4 = from_z(up3[:1], 1), from_z(down3[1:], -1)
    near = cat(down2, down1, gram, up1, up2, axis=1)
    distant = cat(up3, cat(up4, down4), down3, axis=1)
    other_first, other_far_y, *other_rest = across, *others
    other = cat(other_first, *other_rest, other_far_y)

    def both_cores(block):
        got = from_core(block)
        low = jnp.where(core == 0, block, got)
        high = jnp.where(core == 0, got, block)
        return cat(low[0], high[0], low[1], high[1], axis=1)

    def found_of(block):
        return dot(block[:, : 2 * width], same) + dot(block[:, 2 * width :], other)

    near = both_cores(near)
    found_near = found_of(near)
    sent_near = found_near.astype(bf16)
    distant, _ = lax.optimization_barrier((distant, sent_near))
    distant = both_cores(distant)
    found_far = found_of(distant)
    sent_far = found_far.astype(bf16)

    def turned(near_part, far_part):
        block = cat(near_part, far_part)
        return lax.dynamic_slice_in_dim(cat(block, block), ((2 - z_pos) % 8) * unit, rows, 0)

    across_n, right_n, left_n = send(sent_near, sent_near, sent_near)
    got_n, got_f = send_both(second_parts(right_n, left_n, across_n), (sent_far,) * 3)
    across_f, right_f, left_f = got_f
    far_n, across_right_n, across_left_n = second_blocks(sent_near.shape[0], *got_n)
    got_n, got_f = send_both(third_parts(far_n, across_right_n, across_left_n), second_parts(right_f, left_f, across_f))
    across_far_n = cat(*got_n)
    far_f, across_right_f, across_left_f = second_blocks(sent_far.shape[0], *got_f)
    across_far_f = cat(*send(*third_parts(far_f, across_right_f, across_left_f)))

    gram_rows = turned(near, distant)
    found = turned(found_near, found_far)
    three, seven = 3 * rows, 7 * rows
    first = cat(turned(sent_near, sent_far), turned(right_n, right_f), turned(left_n, left_f))
    second = cat(
        turned(far_n, far_f),
        turned(across_n, across_f),
        turned(across_right_n, across_right_f),
        turned(across_left_n, across_left_f),
    )
    product = dot(gram_rows[:, :three], first) + dot(gram_rows[:, three:seven], second)
    start = coef_a * own.astype(f32) + coef_b * found + coef_c * product
    scale = float(COLS) ** 0.5
    return (scale * (start + coef_c * dot(gram_rows[:, seven:], turned(across_far_n, across_far_f)))).astype(bf16)


def solution(mesh):
    return jax.shard_map(
        local,
        mesh=mesh,
        in_specs=(P("wide", "narrow"),),
        out_specs=P("wide", "narrow"),
        check_vma=False,
    )
```

```python
import jax
import jax.numpy as jnp
from jax import lax
from jax.sharding import PartitionSpec as P

COLS = 18432

coef_a = 3.4445
coef_b = -4.775
coef_c = 2.0315

Z_SIZE = 8
f32, bf16 = jnp.float32, jnp.bfloat16


def from_x(value, step):
    pairs = [(y * 4 + (x + step) % 4, y * 4 + x) for y in range(2) for x in range(4)]
    return lax.ppermute(value, "wide", pairs)


def from_y(value):
    return lax.ppermute(value, "wide", [(w, (w + 4) % 8) for w in range(8)])


def from_z(value, step):
    pairs = [(((z + step) % 8) * 4 + r, z * 4 + r) for z in range(8) for r in range(4)]
    return lax.ppermute(value, "narrow", pairs)


def from_y_hi(value):
    return lax.ppermute(value, "narrow", [(n, n ^ 2) for n in range(32)])


def from_y_both(value):
    pairs = [((w, n), ((w + 4) % 8, n ^ 2)) for w in range(8) for n in range(32)]
    return lax.ppermute(value, ("wide", "narrow"), [(a * 32 + b, c * 32 + d) for (a, b), (c, d) in pairs])


def from_core(value):
    return lax.ppermute(value, "narrow", [(n, n ^ 1) for n in range(32)])


def rows_of(left, right):
    return lax.dot_general(left, right, (((1,), (1,)), ((), ())), preferred_element_type=f32)


def dot(left, right):
    return jnp.dot(left, right, preferred_element_type=f32)


def cat(*parts, axis=0):
    return jnp.concatenate(parts, axis=axis)


def gather_first(own):
    return from_x(own, 1), from_x(own, -1), from_y(own)


def gather_second(right, left, across):
    half = right.shape[0] // 16 * 8
    via_y = from_y(cat(right[:half], left[:half]))
    via_right = from_x(cat(across[half:], right[:half]), 1)
    via_left = from_x(cat(across[half:], left[half:]), -1)
    rest = right.shape[0] - half
    far = cat(via_right[rest:], via_left[rest:])
    return far, cat(via_y[:half], via_right[:rest]), cat(via_y[half:], via_left[:rest])


def gather_third(far, across_right, across_left):
    third = far.shape[0] // 24 * 8
    part_y = from_y(far[:third])
    part_right = from_x(across_right[third : 2 * third], 1)
    part_left = from_x(across_left[2 * third :], -1)
    return cat(part_y, part_right, part_left)


def local(own):
    rows = own.shape[0]
    narrow_pos = lax.axis_index("narrow")
    core = narrow_pos % 2
    z_pos = narrow_pos // 4
    unit = rows // Z_SIZE

    right, left, across = gather_first(own)
    half_rows = rows // 2
    far = cat(from_x(right[:half_rows], 1), from_x(left[half_rows:], -1))
    same = cat(own, right, left, far)

    width = 2 * rows
    both = cat(own, across)
    given = rows_of(both, lax.dynamic_slice_in_dim(same, (1 - core) * width, width, 0)).astype(bf16)
    kept = rows_of(both, lax.dynamic_slice_in_dim(same, core * width, width, 0))
    kept, other_right = lax.optimization_barrier((kept, from_y(right)))
    summed = (kept + from_core(given).astype(f32)).reshape(2, rows, width)

    def chunk(step):
        return lax.dynamic_slice_in_dim(summed, ((z_pos + step) % 8) * unit, unit, 1)

    up3 = from_z(chunk(3).astype(bf16), -1)
    down3 = from_z(chunk(-3).astype(bf16), 1)
    up4 = from_z(chunk(4)[:1].astype(bf16), -2)
    down4 = from_z(chunk(4)[1:].astype(bf16), 2)
    up = chunk(2) + up3.astype(f32) + jnp.pad(up4.astype(f32), ((0, 1), (0, 0), (0, 0)))
    down = chunk(-2) + down3.astype(f32) + jnp.pad(down4.astype(f32), ((1, 0), (0, 0), (0, 0)))
    up, down, next_up, next_down, other_left = lax.optimization_barrier(
        (up.astype(bf16), down.astype(bf16), chunk(1).astype(bf16), chunk(-1).astype(bf16), from_y(left))
    )
    far_up, far_down = from_z(up, -2), from_z(down, 2)
    near_up, near_down = from_z(next_up, -1), from_z(next_down, 1)
    total = chunk(0) + near_up.astype(f32) + near_down.astype(f32)
    total = (total + far_up.astype(f32) + far_down.astype(f32)).astype(bf16)

    total, other_far = lax.optimization_barrier((total, from_y(far)))

    gram_same = total[0].astype(f32) + from_y_hi(total[0]).astype(f32)
    gram_other = from_y(total[1]).astype(f32) + from_y_both(total[1]).astype(f32)
    gram = jnp.stack([gram_same, gram_other]).astype(bf16)

    up1, down1 = from_z(gram, 1), from_z(gram, -1)
    up2, down2 = from_z(gram, 2), from_z(gram, -2)
    up3, down3 = from_z(up2, 1), from_z(down2, -1)
    up4, down4 = from_z(up2[:1], 2), from_z(down2[1:], -2)
    block = jnp.zeros((2, rows, width), bf16)
    pieces = ((0, gram), (1, up1), (-1, down1), (2, up2), (-2, down2), (3, up3), (-3, down3), (4, cat(up4, down4)))
    for step, piece in pieces:
        block = lax.dynamic_update_slice_in_dim(block, piece, ((z_pos + step) % 8) * unit, 1)
    other = from_core(block)
    low = jnp.where(core == 0, block, other)
    high = jnp.where(core == 0, other, block)
    gram_rows = cat(low[0], high[0], low[1], high[1], axis=1)

    found = dot(gram_rows[:, : 2 * width], same) + dot(gram_rows[:, 2 * width :], cat(across, other_right, other_left, other_far))
    sent = found.astype(bf16)
    right, left, across = gather_first(sent)
    far, across_right, across_left = gather_second(right, left, across)
    across_far = gather_third(far, across_right, across_left)
    three, seven = 3 * rows, 7 * rows
    product = dot(gram_rows[:, :three], cat(sent, right, left))
    product = product + dot(gram_rows[:, three:seven], cat(far, across, across_right, across_left))
    start = coef_a * own.astype(f32) + coef_b * found + coef_c * product
    scale = float(COLS) ** 0.5
    return (scale * (start + coef_c * dot(gram_rows[:, seven:], across_far))).astype(bf16)


def solution(mesh):
    return jax.shard_map(
        local,
        mesh=mesh,
        in_specs=(P("wide", "narrow"),),
        out_specs=P("wide", "narrow"),
        check_vma=False,
    )
```

```python
import jax
import jax.numpy as jnp
from jax import lax
from jax.sharding import PartitionSpec as P

COLS = 18432

coef_a = 3.4445
coef_b = -4.775
coef_c = 2.0315

Z_SIZE = 8
f32, bf16 = jnp.float32, jnp.bfloat16


def from_x(value, step):
    pairs = [(y * 4 + (x + step) % 4, y * 4 + x) for y in range(2) for x in range(4)]
    return lax.ppermute(value, "wide", pairs)


def from_y(value):
    return lax.ppermute(value, "wide", [(w, (w + 4) % 8) for w in range(8)])


def from_z(value, step):
    pairs = [(((z + step) % 8) * 4 + r, z * 4 + r) for z in range(8) for r in range(4)]
    return lax.ppermute(value, "narrow", pairs)


def from_y_hi(value):
    return lax.ppermute(value, "narrow", [(n, n ^ 2) for n in range(32)])


def from_y_both(value):
    pairs = [((w, n), ((w + 4) % 8, n ^ 2)) for w in range(8) for n in range(32)]
    return lax.ppermute(value, ("wide", "narrow"), [(a * 32 + b, c * 32 + d) for (a, b), (c, d) in pairs])


def from_core(value):
    return lax.ppermute(value, "narrow", [(n, n ^ 1) for n in range(32)])


def rows_of(left, right):
    return lax.dot_general(left, right, (((1,), (1,)), ((), ())), preferred_element_type=f32)


def dot(left, right):
    return jnp.dot(left, right, preferred_element_type=f32)


def cat(*parts, axis=0):
    return jnp.concatenate(parts, axis=axis)


def gather_first(own):
    return from_x(own, 1), from_x(own, -1), from_y(own)


def gather_second(right, left, across):
    half = right.shape[0] // 16 * 8
    via_y = from_y(cat(right[:half], left[:half]))
    via_right = from_x(cat(across[half:], right[:half]), 1)
    via_left = from_x(cat(across[half:], left[half:]), -1)
    rest = right.shape[0] - half
    far = cat(via_right[rest:], via_left[rest:])
    return far, cat(via_y[:half], via_right[:rest]), cat(via_y[half:], via_left[:rest])


def gather_third(far, across_right, across_left):
    third = far.shape[0] // 24 * 8
    part_y = from_y(far[:third])
    part_right = from_x(across_right[third : 2 * third], 1)
    part_left = from_x(across_left[2 * third :], -1)
    return cat(part_y, part_right, part_left)


def local(own):
    rows = own.shape[0]
    narrow_pos = lax.axis_index("narrow")
    core = narrow_pos % 2
    z_pos = narrow_pos // 4
    unit = rows // Z_SIZE

    right, left, across = gather_first(own)
    half_rows = rows // 2
    far = cat(from_x(right[:half_rows], 1), from_x(left[half_rows:], -1))
    same = cat(own, right, left, far)

    width = 2 * rows
    both = cat(own, across)
    given = rows_of(both, lax.dynamic_slice_in_dim(same, (1 - core) * width, width, 0)).astype(bf16)
    kept = rows_of(both, lax.dynamic_slice_in_dim(same, core * width, width, 0))
    kept = lax.optimization_barrier(kept)
    summed = (kept + from_core(given).astype(f32)).reshape(2, rows, width)

    def chunk(step):
        return lax.dynamic_slice_in_dim(summed, ((z_pos + step) % 8) * unit, unit, 1)

    up3 = from_z(chunk(3).astype(bf16), -1)
    down3 = from_z(chunk(-3).astype(bf16), 1)
    up4 = from_z(chunk(4)[:1].astype(bf16), -2)
    down4 = from_z(chunk(4)[1:].astype(bf16), 2)
    up = chunk(2) + up3.astype(f32) + jnp.pad(up4.astype(f32), ((0, 1), (0, 0), (0, 0)))
    down = chunk(-2) + down3.astype(f32) + jnp.pad(down4.astype(f32), ((1, 0), (0, 0), (0, 0)))
    up, down, next_up, next_down, other_left = lax.optimization_barrier(
        (up.astype(bf16), down.astype(bf16), chunk(1).astype(bf16), chunk(-1).astype(bf16), from_y(left))
    )
    far_up, far_down = from_z(up, -2), from_z(down, 2)
    near_up, near_down = from_z(next_up, -1), from_z(next_down, 1)
    total = chunk(0) + near_up.astype(f32) + near_down.astype(f32)
    total = (total + far_up.astype(f32) + far_down.astype(f32)).astype(bf16)

    total, other_far = lax.optimization_barrier((total, from_y(far)))

    gram_same = total[0].astype(f32) + from_y_hi(total[0]).astype(f32)
    gram_other = from_y(total[1]).astype(f32) + from_y_both(total[1]).astype(f32)
    gram = jnp.stack([gram_same, gram_other]).astype(bf16)

    up1, down1 = from_z(gram, 1), from_z(gram, -1)
    up2, down2 = from_z(gram, 2), from_z(gram, -2)
    up1, down1, up2, down2, other_right = lax.optimization_barrier((up1, down1, up2, down2, from_y(right)))
    up3, down3 = from_z(up2, 1), from_z(down2, -1)
    up4, down4 = from_z(up3[:1], 1), from_z(down3[1:], -1)
    near = cat(down2, down1, gram, up1, up2, axis=1)
    distant = cat(up3, cat(up4, down4), down3, axis=1)
    other = cat(across, other_right, other_left, other_far)

    def halves(columns):
        mine = lax.dynamic_slice_in_dim(columns, core * width, width, 0)
        return mine, lax.dynamic_slice_in_dim(columns, (1 - core) * width, width, 0)

    (same_mine, same_got), (other_mine, other_got) = halves(same), halves(other)

    def found_of(block, got):
        mine = dot(block[0], same_mine) + dot(block[1], other_mine)
        return mine + (dot(got[0], same_got) + dot(got[1], other_got))

    got_near = from_core(near)
    found_near = found_of(near, got_near)
    sent_near = found_near.astype(bf16)
    got_distant = from_core(distant)
    found_distant = found_of(distant, got_distant)

    near_step = gather_first(sent_near)
    sent_distant, *near_step = lax.optimization_barrier((found_distant.astype(bf16), *near_step))
    right, left, across = [cat(n, d) for n, d in zip(near_step, gather_first(sent_distant))]
    far, across_right, across_left = gather_second(right, left, across)
    across_far = gather_third(far, across_right, across_left)

    def turned(block):
        return lax.dynamic_slice_in_dim(cat(block, block), ((2 - z_pos) % 8) * unit, rows, 0)

    def placed(near_block, distant_block):
        block = jnp.zeros((2, rows, width), bf16)
        for at in range(8):
            piece = near_block[:, at * unit :][:, :unit] if at < 5 else distant_block[:, (at - 5) * unit :][:, :unit]
            block = lax.dynamic_update_slice_in_dim(block, piece, ((z_pos + at - 2) % 8) * unit, 1)
        return block

    block, got = placed(near, distant), placed(got_near, got_distant)
    low = jnp.where(core == 0, block, got)
    high = jnp.where(core == 0, got, block)
    gram_rows = cat(low[0], high[0], low[1], high[1], axis=1)
    found = turned(cat(found_near, found_distant))
    sent = found.astype(bf16)
    three, seven = 3 * rows, 7 * rows
    product = dot(gram_rows[:, :three], cat(sent, turned(right), turned(left)))
    rest = cat(turned(far), turned(across), turned(across_right), turned(across_left))
    product = product + dot(gram_rows[:, three:seven], rest)
    start = coef_a * own.astype(f32) + coef_b * found + coef_c * product
    scale = float(COLS) ** 0.5
    return (scale * (start + coef_c * dot(gram_rows[:, seven:], turned(across_far)))).astype(bf16)


def solution(mesh):
    return jax.shard_map(
        local,
        mesh=mesh,
        in_specs=(P("wide", "narrow"),),
        out_specs=P("wide", "narrow"),
        check_vma=False,
    )
```

```python
import jax
import jax.numpy as jnp
from jax import lax
from jax.sharding import PartitionSpec as P

COLS = 18432

coef_a = 3.4445
coef_b = -4.775
coef_c = 2.0315

Z_SIZE = 8
f32, bf16 = jnp.float32, jnp.bfloat16


def from_x(value, step):
    pairs = [(y * 4 + (x + step) % 4, y * 4 + x) for y in range(2) for x in range(4)]
    return lax.ppermute(value, "wide", pairs)


def from_y(value):
    return lax.ppermute(value, "wide", [(w, (w + 4) % 8) for w in range(8)])


def from_z(value, step):
    pairs = [(((z + step) % 8) * 4 + r, z * 4 + r) for z in range(8) for r in range(4)]
    return lax.ppermute(value, "narrow", pairs)


def from_y_hi(value):
    return lax.ppermute(value, "narrow", [(n, n ^ 2) for n in range(32)])


def from_y_both(value):
    pairs = [((w, n), ((w + 4) % 8, n ^ 2)) for w in range(8) for n in range(32)]
    return lax.ppermute(value, ("wide", "narrow"), [(a * 32 + b, c * 32 + d) for (a, b), (c, d) in pairs])


def from_core(value):
    return lax.ppermute(value, "narrow", [(n, n ^ 1) for n in range(32)])


def rows_of(left, right):
    return lax.dot_general(left, right, (((1,), (1,)), ((), ())), preferred_element_type=f32)


def dot(left, right):
    return jnp.dot(left, right, preferred_element_type=f32)


def cat(*parts, axis=0):
    return jnp.concatenate(parts, axis=axis)


def gather_first(own):
    return from_x(own, 1), from_x(own, -1), from_y(own)


def gather_second(right, left, across):
    half = right.shape[0] // 16 * 8
    via_y = from_y(cat(right[:half], left[:half]))
    via_right = from_x(cat(across[half:], right[:half]), 1)
    via_left = from_x(cat(across[half:], left[half:]), -1)
    rest = right.shape[0] - half
    far = cat(via_right[rest:], via_left[rest:])
    return far, cat(via_y[:half], via_right[:rest]), cat(via_y[half:], via_left[:rest])


def gather_third(far, across_right, across_left):
    third = far.shape[0] // 24 * 8
    part_y = from_y(far[:third])
    part_right = from_x(across_right[third : 2 * third], 1)
    part_left = from_x(across_left[2 * third :], -1)
    return cat(part_y, part_right, part_left)


def local(own):
    rows = own.shape[0]
    narrow_pos = lax.axis_index("narrow")
    core = narrow_pos % 2
    z_pos = narrow_pos // 4
    unit = rows // Z_SIZE

    right, left, across = gather_first(own)
    half_rows = rows // 2
    far = cat(from_x(right[:half_rows], 1), from_x(left[half_rows:], -1))
    same = cat(own, right, left, far)

    width = 2 * rows
    both = cat(own, across)
    given = rows_of(both, lax.dynamic_slice_in_dim(same, (1 - core) * width, width, 0)).astype(bf16)
    kept = rows_of(both, lax.dynamic_slice_in_dim(same, core * width, width, 0))
    kept = lax.optimization_barrier(kept)
    summed = (kept + from_core(given).astype(f32)).reshape(2, rows, width)

    def chunk(step):
        return lax.dynamic_slice_in_dim(summed, ((z_pos + step) % 8) * unit, unit, 1)

    up3 = from_z(chunk(3).astype(bf16), -1)
    down3 = from_z(chunk(-3).astype(bf16), 1)
    up4 = from_z(chunk(4)[:1].astype(bf16), -2)
    down4 = from_z(chunk(4)[1:].astype(bf16), 2)
    up = chunk(2) + up3.astype(f32) + jnp.pad(up4.astype(f32), ((0, 1), (0, 0), (0, 0)))
    down = chunk(-2) + down3.astype(f32) + jnp.pad(down4.astype(f32), ((1, 0), (0, 0), (0, 0)))
    up, down, next_up, next_down, other_left = lax.optimization_barrier(
        (up.astype(bf16), down.astype(bf16), chunk(1).astype(bf16), chunk(-1).astype(bf16), from_y(left))
    )
    far_up, far_down = from_z(up, -2), from_z(down, 2)
    near_up, near_down = from_z(next_up, -1), from_z(next_down, 1)
    total = chunk(0) + near_up.astype(f32) + near_down.astype(f32)
    total = (total + far_up.astype(f32) + far_down.astype(f32)).astype(bf16)

    total, other_far = lax.optimization_barrier((total, from_y(far)))

    gram_same = total[0].astype(f32) + from_y_hi(total[0]).astype(f32)
    gram_other = from_y(total[1]).astype(f32) + from_y_both(total[1]).astype(f32)
    gram = jnp.stack([gram_same, gram_other]).astype(bf16)

    gram, right = lax.optimization_barrier((gram, right))
    up1, down1 = from_z(gram, 1), from_z(gram, -1)
    up2, down2 = from_z(gram, 2), from_z(gram, -2)
    up1, down1, up2, down2, other_right = lax.optimization_barrier((up1, down1, up2, down2, from_y(right)))
    up3, down3 = from_z(up2, 1), from_z(down2, -1)
    up4, down4 = from_z(up2[:1], 2), from_z(down2[1:], -2)
    block = jnp.zeros((2, rows, width), bf16)
    pieces = ((0, gram), (1, up1), (-1, down1), (2, up2), (-2, down2), (3, up3), (-3, down3), (4, cat(up4, down4)))
    for step, piece in pieces:
        block = lax.dynamic_update_slice_in_dim(block, piece, ((z_pos + step) % 8) * unit, 1)
    got = from_core(block)
    low = jnp.where(core == 0, block, got)
    high = jnp.where(core == 0, got, block)
    gram_rows = cat(low[0], high[0], low[1], high[1], axis=1)

    def halves(columns):
        mine = lax.dynamic_slice_in_dim(columns, core * width, width, 0)
        return mine, lax.dynamic_slice_in_dim(columns, (1 - core) * width, width, 0)

    (same_mine, same_got), (other_mine, other_got) = halves(same), halves(cat(across, other_right, other_left, other_far))
    found = dot(block[0], same_mine) + dot(block[1], other_mine)
    found = found + (dot(got[0], same_got) + dot(got[1], other_got))
    sent = found.astype(bf16)
    right, left, across = gather_first(sent)
    far, across_right, across_left = gather_second(right, left, across)
    across_far = gather_third(far, across_right, across_left)
    three, seven = 3 * rows, 7 * rows
    product = dot(gram_rows[:, :three], cat(sent, right, left))
    product = product + dot(gram_rows[:, three:seven], cat(far, across, across_right, across_left))
    start = coef_a * own.astype(f32) + coef_b * found + coef_c * product
    scale = float(COLS) ** 0.5
    return (scale * (start + coef_c * dot(gram_rows[:, seven:], across_far))).astype(bf16)


def solution(mesh):
    return jax.shard_map(
        local,
        mesh=mesh,
        in_specs=(P("wide", "narrow"),),
        out_specs=P("wide", "narrow"),
        check_vma=False,
    )
```

```python
import functools

import jax
import jax.numpy as jnp
from jax import lax
from jax.experimental import pallas as pl
from jax.experimental.pallas import tpu as pltpu
from jax.sharding import PartitionSpec as P

COLS = 18432

coef_a = 3.4445
coef_b = -4.775
coef_c = 2.0315

Z_SIZE = 8
f32, bf16 = jnp.float32, jnp.bfloat16


def from_x(value, step):
    pairs = [(y * 4 + (x + step) % 4, y * 4 + x) for y in range(2) for x in range(4)]
    return lax.ppermute(value, "wide", pairs)


def from_y(value):
    return lax.ppermute(value, "wide", [(w, (w + 4) % 8) for w in range(8)])


def from_z(value, step):
    pairs = [(((z + step) % 8) * 4 + r, z * 4 + r) for z in range(8) for r in range(4)]
    return lax.ppermute(value, "narrow", pairs)


def from_y_hi(value):
    return lax.ppermute(value, "narrow", [(n, n ^ 2) for n in range(32)])


def from_y_both(value):
    pairs = [((w, n), ((w + 4) % 8, n ^ 2)) for w in range(8) for n in range(32)]
    return lax.ppermute(value, ("wide", "narrow"), [(a * 32 + b, c * 32 + d) for (a, b), (c, d) in pairs])


def from_core(value):
    return lax.ppermute(value, "narrow", [(n, n ^ 1) for n in range(32)])


def rows_of(left, right):
    return lax.dot_general(left, right, (((1,), (1,)), ((), ())), preferred_element_type=f32)


def dot(left, right):
    return jnp.dot(left, right, preferred_element_type=f32)


def cat(*parts, axis=0):
    return jnp.concatenate(parts, axis=axis)


def gather_first(own):
    return from_x(own, 1), from_x(own, -1), from_y(own)


def gather_second(right, left, across):
    half = right.shape[0] // 16 * 8
    via_y = from_y(cat(right[:half], left[:half]))
    via_right = from_x(cat(across[half:], right[:half]), 1)
    via_left = from_x(cat(across[half:], left[half:]), -1)
    rest = right.shape[0] - half
    far = cat(via_right[rest:], via_left[rest:])
    return far, cat(via_y[:half], via_right[:rest]), cat(via_y[half:], via_left[:rest])


def gather_third(far, across_right, across_left):
    third = far.shape[0] // 24 * 8
    part_y = from_y(far[:third])
    part_right = from_x(across_right[third : 2 * third], 1)
    part_left = from_x(across_left[2 * third :], -1)
    return cat(part_y, part_right, part_left)


def found_kernel(mine, *refs):
    block_ref, *x_refs = refs[:9]
    if mine:
        found_ref, lhs, rhs, sems = refs[9:]
    else:
        before_ref, found_ref, sent_ref, lhs, rhs, sems = refs[9:]
    rows, cols = x_refs[0].shape
    core = lax.rem(lax.axis_index("narrow"), 2)

    def run(picks):
        copies = [pltpu.make_async_copy(block_ref, lhs, sems.at[4])]
        for at, pick in enumerate(picks):
            copies.append(pltpu.make_async_copy(x_refs[pick], rhs.at[pl.ds(at * rows, rows)], sems.at[at]))
        for copy in copies:
            copy.start()
        for copy in copies:
            copy.wait()

    @pl.when(core == (0 if mine else 1))
    def _():
        run((0, 1, 4, 5))

    @pl.when(core == (1 if mine else 0))
    def _():
        run((2, 3, 6, 7))

    for start in range(0, cols, 256):
        part = pl.ds(start, min(256, cols - start))
        value = dot(lhs[0], rhs[: 2 * rows, part]) + dot(lhs[1], rhs[2 * rows :, part])
        if not mine:
            value = before_ref[:, part] + value
            sent_ref[:, part] = value.astype(bf16)
        found_ref[:, part] = value


def found_part(block, x_blocks, before=None):
    rows, cols = x_blocks[0].shape
    mine = before is None
    found = jax.ShapeDtypeStruct((rows, cols), f32)
    vmem = pl.BlockSpec(memory_space=pltpu.VMEM)
    return pl.pallas_call(
        functools.partial(found_kernel, mine),
        out_shape=found if mine else (found, jax.ShapeDtypeStruct((rows, cols), bf16)),
        in_specs=[pl.BlockSpec(memory_space=pl.ANY)] * 9 + ([] if mine else [vmem]),
        out_specs=vmem if mine else (vmem, vmem),
        scratch_shapes=[
            pltpu.VMEM(block.shape, bf16),
            pltpu.VMEM((4 * rows, cols), bf16),
            pltpu.SemaphoreType.DMA((5,)),
        ],
        compiler_params=pltpu.CompilerParams(vmem_limit_bytes=16 * 2**20),
        cost_estimate=pl.CostEstimate(flops=8 * rows * rows * cols, bytes_accessed=6 * 2**20, transcendentals=0),
    )(block, *x_blocks, *([] if mine else [before]))


def local(own):
    rows = own.shape[0]
    narrow_pos = lax.axis_index("narrow")
    core = narrow_pos % 2
    z_pos = narrow_pos // 4
    unit = rows // Z_SIZE

    right, left, across = gather_first(own)
    half_rows = rows // 2
    far = cat(from_x(right[:half_rows], 1), from_x(left[half_rows:], -1))
    same = cat(own, right, left, far)
    x_right, x_left, x_far = right, left, far

    width = 2 * rows
    both = cat(own, across)
    given = rows_of(both, lax.dynamic_slice_in_dim(same, (1 - core) * width, width, 0)).astype(bf16)
    kept = rows_of(both, lax.dynamic_slice_in_dim(same, core * width, width, 0))
    kept = lax.optimization_barrier(kept)
    summed = (kept + from_core(given).astype(f32)).reshape(2, rows, width)

    def chunk(step):
        return lax.dynamic_slice_in_dim(summed, ((z_pos + step) % 8) * unit, unit, 1)

    three_up, left = lax.optimization_barrier((chunk(3).astype(bf16), left))
    up3 = from_z(three_up, -1)
    down3 = from_z(chunk(-3).astype(bf16), 1)
    up4 = from_z(chunk(4)[:1].astype(bf16), -2)
    down4 = from_z(chunk(4)[1:].astype(bf16), 2)
    up = chunk(2) + up3.astype(f32) + jnp.pad(up4.astype(f32), ((0, 1), (0, 0), (0, 0)))
    down = chunk(-2) + down3.astype(f32) + jnp.pad(down4.astype(f32), ((1, 0), (0, 0), (0, 0)))
    up, down, next_up, next_down, other_left, far = lax.optimization_barrier(
        (up.astype(bf16), down.astype(bf16), chunk(1).astype(bf16), chunk(-1).astype(bf16), from_y(left), far)
    )
    far_up, far_down = from_z(up, -2), from_z(down, 2)
    near_up, near_down = from_z(next_up, -1), from_z(next_down, 1)
    total = chunk(0) + near_up.astype(f32) + near_down.astype(f32)
    total = (total + far_up.astype(f32) + far_down.astype(f32)).astype(bf16)

    total, other_far = lax.optimization_barrier((total, from_y(far)))

    gram_same = total[0].astype(f32) + from_y_hi(total[0]).astype(f32)
    gram_other = from_y(total[1]).astype(f32) + from_y_both(total[1]).astype(f32)
    gram = jnp.stack([gram_same, gram_other]).astype(bf16)

    gram, right = lax.optimization_barrier((gram, right))
    up1, down1 = from_z(gram, 1), from_z(gram, -1)
    up2, down2 = from_z(gram, 2), from_z(gram, -2)
    up1, down1, up2, down2, other_right = lax.optimization_barrier((up1, down1, up2, down2, from_y(right)))
    up3, down3 = from_z(up2, 1), from_z(down2, -1)
    up4, down4 = from_z(up2[:1], 2), from_z(down2[1:], -2)
    block = jnp.zeros((2, rows, width), bf16)
    pieces = ((0, gram), (1, up1), (-1, down1), (2, up2), (-2, down2), (3, up3), (-3, down3), (4, cat(up4, down4)))
    for step, piece in pieces:
        block = lax.dynamic_update_slice_in_dim(block, piece, ((z_pos + step) % 8) * unit, 1)
    got = from_core(block)
    low = jnp.where(core == 0, block, got)
    high = jnp.where(core == 0, got, block)
    gram_rows = cat(low[0], high[0], low[1], high[1], axis=1)

    x_blocks = (own, x_right, x_left, x_far, across, other_right, other_left, other_far)
    found, sent = found_part(got, x_blocks, found_part(block, x_blocks))
    right, left, across = gather_first(sent)
    far, across_right, across_left = gather_second(right, left, across)
    across_far = gather_third(far, across_right, across_left)
    three, seven = 3 * rows, 7 * rows
    product = dot(gram_rows[:, :three], cat(sent, right, left))
    product = product + dot(gram_rows[:, three:seven], cat(far, across, across_right, across_left))
    start = coef_a * own.astype(f32) + coef_b * found + coef_c * product
    scale = float(COLS) ** 0.5
    return (scale * (start + coef_c * dot(gram_rows[:, seven:], across_far))).astype(bf16)


def solution(mesh):
    return jax.shard_map(
        local,
        mesh=mesh,
        in_specs=(P("wide", "narrow"),),
        out_specs=P("wide", "narrow"),
        check_vma=False,
    )
```

```python
import functools

import jax
import jax.numpy as jnp
from jax import lax
from jax.experimental import pallas as pl
from jax.experimental.pallas import tpu as pltpu
from jax.sharding import PartitionSpec as P

COLS = 18432

coef_a = 3.4445
coef_b = -4.775
coef_c = 2.0315

Z_SIZE = 8
f32, bf16 = jnp.float32, jnp.bfloat16


def from_x(value, step):
    pairs = [(y * 4 + (x + step) % 4, y * 4 + x) for y in range(2) for x in range(4)]
    return lax.ppermute(value, "wide", pairs)


def from_y(value):
    return lax.ppermute(value, "wide", [(w, (w + 4) % 8) for w in range(8)])


def from_z(value, step):
    pairs = [(((z + step) % 8) * 4 + r, z * 4 + r) for z in range(8) for r in range(4)]
    return lax.ppermute(value, "narrow", pairs)


def from_y_hi(value):
    return lax.ppermute(value, "narrow", [(n, n ^ 2) for n in range(32)])


def from_y_both(value):
    pairs = [((w, n), ((w + 4) % 8, n ^ 2)) for w in range(8) for n in range(32)]
    return lax.ppermute(value, ("wide", "narrow"), [(a * 32 + b, c * 32 + d) for (a, b), (c, d) in pairs])


def from_core(value):
    return lax.ppermute(value, "narrow", [(n, n ^ 1) for n in range(32)])


def rows_of(left, right):
    return lax.dot_general(left, right, (((1,), (1,)), ((), ())), preferred_element_type=f32)


def dot(left, right):
    return jnp.dot(left, right, preferred_element_type=f32)


def cat(*parts, axis=0):
    return jnp.concatenate(parts, axis=axis)


def gather_first(own):
    return from_x(own, 1), from_x(own, -1), from_y(own)


def gather_second(right, left, across):
    half = right.shape[0] // 16 * 8
    via_y = from_y(cat(right[:half], left[:half]))
    via_right = from_x(cat(across[half:], right[:half]), 1)
    via_left = from_x(cat(across[half:], left[half:]), -1)
    rest = right.shape[0] - half
    far = cat(via_right[rest:], via_left[rest:])
    return far, cat(via_y[:half], via_right[:rest]), cat(via_y[half:], via_left[:rest])


def gather_third(far, across_right, across_left):
    third = far.shape[0] // 24 * 8
    part_y = from_y(far[:third])
    part_right = from_x(across_right[third : 2 * third], 1)
    part_left = from_x(across_left[2 * third :], -1)
    return cat(part_y, part_right, part_left)


def found_kernel(mine, *refs):
    block_ref, whole_ref = refs[:2]
    if mine:
        found_ref, lhs, rhs, sems = refs[2:]
    else:
        before_ref, found_ref, sent_ref, lhs, rhs, sems = refs[2:]
    rows, cols = found_ref.shape
    core = lax.rem(lax.axis_index("narrow"), 2)
    wide_pos = lax.axis_index("wide")
    y_pos, x_pos = wide_pos // 4, lax.rem(wide_pos, 4)

    first = core == (0 if mine else 1)
    copies = [pltpu.make_async_copy(block_ref, lhs, sems.at[4])]
    for at in range(4):
        step = jnp.where(first, (0, 1)[at % 2], (3, 2)[at % 2])
        place = (y_pos if at < 2 else 1 - y_pos) * 4 + lax.rem(x_pos + step, 4)
        source = whole_ref.at[pl.ds(pl.multiple_of(place * rows, rows), rows)]
        copies.append(pltpu.make_async_copy(source, rhs.at[pl.ds(at * rows, rows)], sems.at[at]))
    for copy in copies:
        copy.start()
    for copy in copies:
        copy.wait()

    for start in range(0, cols, 256):
        part = pl.ds(start, min(256, cols - start))
        value = dot(lhs[0], rhs[: 2 * rows, part]) + dot(lhs[1], rhs[2 * rows :, part])
        if not mine:
            value = before_ref[:, part] + value
            sent_ref[:, part] = value.astype(bf16)
        found_ref[:, part] = value


def found_part(block, whole, before=None):
    rows, cols = block.shape[1], whole.shape[1]
    mine = before is None
    found = jax.ShapeDtypeStruct((rows, cols), f32)
    vmem = pl.BlockSpec(memory_space=pltpu.VMEM)
    return pl.pallas_call(
        functools.partial(found_kernel, mine),
        out_shape=found if mine else (found, jax.ShapeDtypeStruct((rows, cols), bf16)),
        in_specs=[pl.BlockSpec(memory_space=pl.ANY)] * 2 + ([] if mine else [vmem]),
        out_specs=vmem if mine else (vmem, vmem),
        scratch_shapes=[
            pltpu.VMEM(block.shape, bf16),
            pltpu.VMEM((4 * rows, cols), bf16),
            pltpu.SemaphoreType.DMA((5,)),
        ],
        compiler_params=pltpu.CompilerParams(vmem_limit_bytes=16 * 2**20),
        cost_estimate=pl.CostEstimate(flops=8 * rows * rows * cols, bytes_accessed=6 * 2**20, transcendentals=0),
    )(block, whole, *([] if mine else [before]))


def local(own):
    rows = own.shape[0]
    narrow_pos = lax.axis_index("narrow")
    core = narrow_pos % 2
    z_pos = narrow_pos // 4
    unit = rows // Z_SIZE

    right, left, across = gather_first(own)
    half_rows = rows // 2
    far = cat(from_x(right[:half_rows], 1), from_x(left[half_rows:], -1))
    same = cat(own, right, left, far)

    width = 2 * rows
    both = cat(own, across)
    given = rows_of(both, lax.dynamic_slice_in_dim(same, (1 - core) * width, width, 0)).astype(bf16)
    kept = rows_of(both, lax.dynamic_slice_in_dim(same, core * width, width, 0))
    kept = lax.optimization_barrier(kept)
    given, gathered = lax.optimization_barrier((given, own))
    whole = lax.all_gather(gathered, "wide", axis=0, tiled=True)
    summed = (kept + from_core(given).astype(f32)).reshape(2, rows, width)

    def chunk(step):
        return lax.dynamic_slice_in_dim(summed, ((z_pos + step) % 8) * unit, unit, 1)

    up3 = from_z(chunk(3).astype(bf16), -1)
    down3 = from_z(chunk(-3).astype(bf16), 1)
    up4 = from_z(chunk(4)[:1].astype(bf16), -2)
    down4 = from_z(chunk(4)[1:].astype(bf16), 2)
    up = chunk(2) + up3.astype(f32) + jnp.pad(up4.astype(f32), ((0, 1), (0, 0), (0, 0)))
    down = chunk(-2) + down3.astype(f32) + jnp.pad(down4.astype(f32), ((1, 0), (0, 0), (0, 0)))
    up, down, next_up, next_down = lax.optimization_barrier(
        (up.astype(bf16), down.astype(bf16), chunk(1).astype(bf16), chunk(-1).astype(bf16))
    )
    far_up, far_down = from_z(up, -2), from_z(down, 2)
    near_up, near_down = from_z(next_up, -1), from_z(next_down, 1)
    total = chunk(0) + near_up.astype(f32) + near_down.astype(f32)
    total = (total + far_up.astype(f32) + far_down.astype(f32)).astype(bf16)

    gram_same = total[0].astype(f32) + from_y_hi(total[0]).astype(f32)
    gram_other = from_y(total[1]).astype(f32) + from_y_both(total[1]).astype(f32)
    gram = jnp.stack([gram_same, gram_other]).astype(bf16)

    up1, down1 = from_z(gram, 1), from_z(gram, -1)
    up2, down2 = from_z(gram, 2), from_z(gram, -2)
    up3, down3 = from_z(up2, 1), from_z(down2, -1)
    up4, down4 = from_z(up2[:1], 2), from_z(down2[1:], -2)
    block = jnp.zeros((2, rows, width), bf16)
    pieces = ((0, gram), (1, up1), (-1, down1), (2, up2), (-2, down2), (3, up3), (-3, down3), (4, cat(up4, down4)))
    for step, piece in pieces:
        block = lax.dynamic_update_slice_in_dim(block, piece, ((z_pos + step) % 8) * unit, 1)
    got = from_core(block)
    low = jnp.where(core == 0, block, got)
    high = jnp.where(core == 0, got, block)
    gram_rows = cat(low[0], high[0], low[1], high[1], axis=1)

    found, sent = found_part(got, whole, found_part(block, whole))
    right, left, across = gather_first(sent)
    far, across_right, across_left = gather_second(right, left, across)
    across_far = gather_third(far, across_right, across_left)
    three, seven = 3 * rows, 7 * rows
    product = dot(gram_rows[:, :three], cat(sent, right, left))
    product = product + dot(gram_rows[:, three:seven], cat(far, across, across_right, across_left))
    start = coef_a * own.astype(f32) + coef_b * found + coef_c * product
    scale = float(COLS) ** 0.5
    return (scale * (start + coef_c * dot(gram_rows[:, seven:], across_far))).astype(bf16)


def solution(mesh):
    return jax.shard_map(
        local,
        mesh=mesh,
        in_specs=(P("wide", "narrow"),),
        out_specs=P("wide", "narrow"),
        check_vma=False,
    )
```

```python
import functools

import jax
import jax.numpy as jnp
from jax import lax
from jax.experimental import pallas as pl
from jax.experimental.pallas import tpu as pltpu
from jax.sharding import PartitionSpec as P

COLS = 18432

coef_a = 3.4445
coef_b = -4.775
coef_c = 2.0315

Z_SIZE = 8
f32, bf16 = jnp.float32, jnp.bfloat16


def from_x(value, step):
    pairs = [(y * 4 + (x + step) % 4, y * 4 + x) for y in range(2) for x in range(4)]
    return lax.ppermute(value, "wide", pairs)


def from_y(value):
    return lax.ppermute(value, "wide", [(w, (w + 4) % 8) for w in range(8)])


def from_y_hi(value):
    return lax.ppermute(value, "narrow", [(n, n ^ 2) for n in range(32)])


def from_y_both(value):
    pairs = [((w, n), ((w + 4) % 8, n ^ 2)) for w in range(8) for n in range(32)]
    return lax.ppermute(value, ("wide", "narrow"), [(a * 32 + b, c * 32 + d) for (a, b), (c, d) in pairs])


def from_core(value):
    return lax.ppermute(value, "narrow", [(n, n ^ 1) for n in range(32)])


def rows_of(left, right):
    return lax.dot_general(left, right, (((1,), (1,)), ((), ())), preferred_element_type=f32)


def dot(left, right):
    return jnp.dot(left, right, preferred_element_type=f32)


def cat(*parts, axis=0):
    return jnp.concatenate(parts, axis=axis)


def gather_first(own):
    return from_x(own, 1), from_x(own, -1), from_y(own)


def gather_second(right, left, across):
    half = right.shape[0] // 16 * 8
    via_y = from_y(cat(right[:half], left[:half]))
    via_right = from_x(cat(across[half:], right[:half]), 1)
    via_left = from_x(cat(across[half:], left[half:]), -1)
    rest = right.shape[0] - half
    far = cat(via_right[rest:], via_left[rest:])
    return far, cat(via_y[:half], via_right[:rest]), cat(via_y[half:], via_left[:rest])


def gather_third(far, across_right, across_left):
    third = far.shape[0] // 24 * 8
    part_y = from_y(far[:third])
    part_right = from_x(across_right[third : 2 * third], 1)
    part_left = from_x(across_left[2 * third :], -1)
    return cat(part_y, part_right, part_left)


def along_z(value, hops):
    pairs = [(z * 4 + r, (z + hops * (1 - 2 * (r % 2))) % 8 * 4 + r) for z in range(8) for r in range(4)]
    return lax.ppermute(value, "narrow", pairs)


def found_kernel(ahead, *refs):
    lhs_ref, *x_refs = refs[:9]
    if ahead:
        found_ref, lhs, rhs, sems = refs[9:]
    else:
        before_ref, found_ref, sent_ref, lhs, rhs, sems = refs[9:]
    rows, cols = x_refs[0].shape
    unit = rows // Z_SIZE
    narrow_pos = lax.axis_index("narrow")
    z_pos, way = narrow_pos // 4, 1 - 2 * lax.rem(narrow_pos, 2)
    steps = [way * at for at in range(4)] if ahead else [-way, -2 * way, -3 * way, 4]

    copies = [pltpu.make_async_copy(lhs_ref, lhs, sems.at[8])]
    for at, x_ref in enumerate(x_refs):
        copies.append(pltpu.make_async_copy(x_ref, rhs.at[pl.ds(at * rows, rows)], sems.at[at]))
    for copy in copies:
        copy.start()
    for copy in copies:
        copy.wait()

    for start in range(0, cols, 256):
        part = pl.ds(start, min(256, cols - start))
        value = dot(lhs[0], rhs[: 4 * rows, part]) + dot(lhs[1], rhs[4 * rows :, part])
        if not ahead:
            found_ref[:, part] = before_ref[:, part]
        for at, step in enumerate(steps):
            place = pl.multiple_of(lax.rem(z_pos + step + 8, 8) * unit, 8)
            found_ref[pl.ds(place, unit), part] = value[at * unit : (at + 1) * unit]
        if not ahead:
            sent_ref[:, part] = found_ref[:, part].astype(bf16)


def found_part(units, x_blocks, before=None):
    rows, cols = x_blocks[0].shape
    ahead = before is None
    found = jax.ShapeDtypeStruct((rows, cols), f32)
    vmem = pl.BlockSpec(memory_space=pltpu.VMEM)
    return pl.pallas_call(
        functools.partial(found_kernel, ahead),
        out_shape=found if ahead else (found, jax.ShapeDtypeStruct((rows, cols), bf16)),
        in_specs=[pl.BlockSpec(memory_space=pl.ANY)] * 9 + ([] if ahead else [vmem]),
        out_specs=vmem if ahead else (vmem, vmem),
        scratch_shapes=[
            pltpu.VMEM(units.shape, bf16),
            pltpu.VMEM((8 * rows, cols), bf16),
            pltpu.SemaphoreType.DMA((9,)),
        ],
        compiler_params=pltpu.CompilerParams(vmem_limit_bytes=20 * 2**20),
        cost_estimate=pl.CostEstimate(flops=8 * rows * rows * cols, bytes_accessed=6 * 2**20, transcendentals=0),
    )(units, *x_blocks, *([] if ahead else [before]))


def local(own):
    rows = own.shape[0]
    narrow_pos = lax.axis_index("narrow")
    core = narrow_pos % 2
    z_pos = narrow_pos // 4
    unit = rows // Z_SIZE

    right, left, across = gather_first(own)
    half_rows = rows // 2
    far = cat(from_x(right[:half_rows], 1), from_x(left[half_rows:], -1))
    same = cat(own, right, left, far)
    x_right, x_left, x_far = right, left, far

    both = cat(own, across)
    order = ((0, 4), (0, 3), (1, 3), (0, 2), (1, 2), (0, 1), (1, 1), (1, 0))

    def units_of(core):
        def place(which, step):
            owner = jnp.where(core == 0, which, 1 - which)
            return owner * rows + ((z_pos + step * (1 - 2 * core)) % 8) * unit

        return cat(*[lax.dynamic_slice_in_dim(both, place(*at), unit, 0) for at in order])

    given = rows_of(units_of(1 - core), same).astype(bf16)
    kept = lax.optimization_barrier(rows_of(units_of(core), same))
    summed = kept + from_core(given).astype(f32)

    def units(start, stop):
        return summed[start * unit : stop * unit]

    three, left = lax.optimization_barrier((units(1, 3).astype(bf16), left))
    passed = along_z(three, 1).astype(f32) + jnp.pad(along_z(units(0, 1).astype(bf16), 2).astype(f32), ((0, unit), (0, 0)))
    two, one, other_left, far = lax.optimization_barrier(
        ((units(3, 5) + passed).astype(bf16), units(5, 7).astype(bf16), from_y(left), far)
    )
    passed = along_z(two, 2).astype(f32) + along_z(one, 1).astype(f32)
    total = (passed + jnp.pad(units(7, 8), ((unit, 0), (0, 0)))).astype(bf16)
    total, other_far = lax.optimization_barrier((total, from_y(far)))
    own_part = jnp.where(core == 0, total[:unit], total[unit:])
    across_part = jnp.where(core == 0, total[unit:], total[:unit])

    gram_same = own_part.astype(f32) + from_y_hi(own_part).astype(f32)
    gram_other = from_y(across_part).astype(f32) + from_y_both(across_part).astype(f32)
    gram = jnp.stack([gram_same, gram_other]).astype(bf16)
    gram = (gram.astype(f32) + from_core(gram).astype(f32)).astype(bf16)

    gram, right = lax.optimization_barrier((gram, right))
    away1, away2, other_right = lax.optimization_barrier((along_z(gram, -1), along_z(gram, -2), from_y(right)))
    away3 = along_z(away2, -1)
    away4 = along_z(lax.dynamic_slice_in_dim(away2, core, 1, 0), -2)
    ahead = cat(gram, away1, away2, away3, axis=1)
    got = from_core(cat(away1.reshape(-1, 4 * rows), away2.reshape(-1, 4 * rows), away3.reshape(-1, 4 * rows), away4[0]))
    got = got.reshape(7, unit, 4 * rows)
    opposite = jnp.where(core == 0, cat(away4, got[6:]), cat(got[6:], away4))
    behind = cat(got[0:2], got[2:4], got[4:6], opposite, axis=1)

    x_blocks = (own, x_right, x_left, x_far, across, other_right, other_left, other_far)
    found, sent = found_part(behind, x_blocks, found_part(ahead, x_blocks))

    gram_rows = jnp.zeros((2, rows, 4 * rows), bf16)
    way = 1 - 2 * core
    for at in range(4):
        for block, step in ((ahead, way * at), (behind, (-way, -2 * way, -3 * way, 4)[at])):
            piece = block[:, at * unit : (at + 1) * unit]
            gram_rows = lax.dynamic_update_slice_in_dim(gram_rows, piece, ((z_pos + step) % 8) * unit, 1)
    gram_rows = cat(gram_rows[0], gram_rows[1], axis=1)

    right, left, across = gather_first(sent)
    far, across_right, across_left = gather_second(right, left, across)
    across_far = gather_third(far, across_right, across_left)
    three, seven = 3 * rows, 7 * rows
    product = dot(gram_rows[:, :three], cat(sent, right, left))
    product = product + dot(gram_rows[:, three:seven], cat(far, across, across_right, across_left))
    start = coef_a * own.astype(f32) + coef_b * found + coef_c * product
    scale = float(COLS) ** 0.5
    return (scale * (start + coef_c * dot(gram_rows[:, seven:], across_far))).astype(bf16)


def solution(mesh):
    return jax.shard_map(
        local,
        mesh=mesh,
        in_specs=(P("wide", "narrow"),),
        out_specs=P("wide", "narrow"),
        check_vma=False,
    )
```

```python
import functools

import jax
import jax.numpy as jnp
from jax import lax
from jax.experimental import pallas as pl
from jax.experimental.pallas import tpu as pltpu
from jax.sharding import PartitionSpec as P

COLS = 18432

coef_a = 3.4445
coef_b = -4.775
coef_c = 2.0315

Z_SIZE = 8
f32, bf16 = jnp.float32, jnp.bfloat16


def from_x(value, step):
    pairs = [(y * 4 + (x + step) % 4, y * 4 + x) for y in range(2) for x in range(4)]
    return lax.ppermute(value, "wide", pairs)


def from_y(value):
    return lax.ppermute(value, "wide", [(w, (w + 4) % 8) for w in range(8)])


def from_z(value, step):
    pairs = [(((z + step) % 8) * 4 + r, z * 4 + r) for z in range(8) for r in range(4)]
    return lax.ppermute(value, "narrow", pairs)


def from_y_hi(value):
    return lax.ppermute(value, "narrow", [(n, n ^ 2) for n in range(32)])


def from_y_both(value):
    pairs = [((w, n), ((w + 4) % 8, n ^ 2)) for w in range(8) for n in range(32)]
    return lax.ppermute(value, ("wide", "narrow"), [(a * 32 + b, c * 32 + d) for (a, b), (c, d) in pairs])


def from_core(value):
    return lax.ppermute(value, "narrow", [(n, n ^ 1) for n in range(32)])


def rows_of(left, right):
    return lax.dot_general(left, right, (((1,), (1,)), ((), ())), preferred_element_type=f32)


def dot(left, right):
    return jnp.dot(left, right, preferred_element_type=f32)


def cat(*parts, axis=0):
    return jnp.concatenate(parts, axis=axis)


def gather_first(own):
    return from_x(own, 1), from_x(own, -1), from_y(own)


def gather_second(right, left, across):
    half = right.shape[0] // 16 * 8
    via_y = from_y(cat(right[:half], left[:half]))
    via_right = from_x(cat(across[half:], right[:half]), 1)
    via_left = from_x(cat(across[half:], left[half:]), -1)
    rest = right.shape[0] - half
    far = cat(via_right[rest:], via_left[rest:])
    return far, cat(via_y[:half], via_right[:rest]), cat(via_y[half:], via_left[:rest])


def gather_third(far, across_right, across_left):
    third = far.shape[0] // 24 * 8
    part_y = from_y(far[:third])
    part_right = from_x(across_right[third : 2 * third], 1)
    part_left = from_x(across_left[2 * third :], -1)
    return cat(part_y, part_right, part_left)


def along_z(value, hops):
    pairs = [(z * 4 + r, (z + hops * (1 - 2 * (r % 2))) % 8 * 4 + r) for z in range(8) for r in range(4)]
    return lax.ppermute(value, "narrow", pairs)


def found_kernel(mine, *refs):
    block_ref, *x_refs = refs[:9]
    if mine:
        found_ref, lhs, rhs, sems = refs[9:]
    else:
        before_ref, found_ref, sent_ref, lhs, rhs, sems = refs[9:]
    rows, cols = x_refs[0].shape
    core = lax.rem(lax.axis_index("narrow"), 2)

    def run(picks):
        copies = [pltpu.make_async_copy(block_ref, lhs, sems.at[4])]
        for at, pick in enumerate(picks):
            copies.append(pltpu.make_async_copy(x_refs[pick], rhs.at[pl.ds(at * rows, rows)], sems.at[at]))
        for copy in copies:
            copy.start()
        for copy in copies:
            copy.wait()

    @pl.when(core == (0 if mine else 1))
    def _():
        run((0, 1, 4, 5))

    @pl.when(core == (1 if mine else 0))
    def _():
        run((2, 3, 6, 7))

    for start in range(0, cols, 256):
        part = pl.ds(start, min(256, cols - start))
        value = dot(lhs[0], rhs[: 2 * rows, part]) + dot(lhs[1], rhs[2 * rows :, part])
        if not mine:
            value = before_ref[:, part] + value
            sent_ref[:, part] = value.astype(bf16)
        found_ref[:, part] = value


def found_part(block, x_blocks, before=None):
    rows, cols = x_blocks[0].shape
    mine = before is None
    found = jax.ShapeDtypeStruct((rows, cols), f32)
    vmem = pl.BlockSpec(memory_space=pltpu.VMEM)
    return pl.pallas_call(
        functools.partial(found_kernel, mine),
        out_shape=found if mine else (found, jax.ShapeDtypeStruct((rows, cols), bf16)),
        in_specs=[pl.BlockSpec(memory_space=pl.ANY)] * 9 + ([] if mine else [vmem]),
        out_specs=vmem if mine else (vmem, vmem),
        scratch_shapes=[
            pltpu.VMEM(block.shape, bf16),
            pltpu.VMEM((4 * rows, cols), bf16),
            pltpu.SemaphoreType.DMA((5,)),
        ],
        compiler_params=pltpu.CompilerParams(vmem_limit_bytes=16 * 2**20),
        cost_estimate=pl.CostEstimate(flops=8 * rows * rows * cols, bytes_accessed=6 * 2**20, transcendentals=0),
    )(block, *x_blocks, *([] if mine else [before]))


def local(own):
    rows = own.shape[0]
    narrow_pos = lax.axis_index("narrow")
    core = narrow_pos % 2
    z_pos = narrow_pos // 4
    unit = rows // Z_SIZE

    right, left, across = gather_first(own)
    half_rows = rows // 2
    far = cat(from_x(right[:half_rows], 1), from_x(left[half_rows:], -1))
    same = cat(own, right, left, far)
    x_right, x_left, x_far = right, left, far

    both = cat(own, across)
    order = ((0, 4), (0, 3), (1, 3), (0, 2), (1, 2), (0, 1), (1, 1), (1, 0))

    def units_of(core):
        def place(which, step):
            owner = jnp.where(core == 0, which, 1 - which)
            return owner * rows + ((z_pos + step * (1 - 2 * core)) % 8) * unit

        return cat(*[lax.dynamic_slice_in_dim(both, place(*at), unit, 0) for at in order])

    given = rows_of(units_of(1 - core), same).astype(bf16)
    kept = lax.optimization_barrier(rows_of(units_of(core), same))
    summed = kept + from_core(given).astype(f32)

    def units(start, stop):
        return summed[start * unit : stop * unit]

    three, left = lax.optimization_barrier((units(1, 3).astype(bf16), left))
    passed = along_z(three, 1).astype(f32) + jnp.pad(along_z(units(0, 1).astype(bf16), 2).astype(f32), ((0, unit), (0, 0)))
    two, one, far = lax.optimization_barrier(((units(3, 5) + passed).astype(bf16), units(5, 7).astype(bf16), far))
    passed = along_z(two, 2).astype(f32) + along_z(one, 1).astype(f32)
    total = passed + jnp.pad(units(7, 8), ((unit, 0), (0, 0)))
    total, other_left, other_far = lax.optimization_barrier((total, from_y(left), from_y(far)))

    width = 2 * rows
    total = jnp.where(core == 0, total, cat(total[unit:], total[:unit])).reshape(2, unit, 2 * width)
    given = lax.dynamic_slice_in_dim(total, (1 - core) * width, width, 2).astype(bf16)
    total = (lax.dynamic_slice_in_dim(total, core * width, width, 2) + from_core(given).astype(f32)).astype(bf16)

    gram_same = total[0].astype(f32) + from_y_hi(total[0]).astype(f32)
    gram_other = from_y(total[1]).astype(f32) + from_y_both(total[1]).astype(f32)
    gram = jnp.stack([gram_same, gram_other]).astype(bf16)

    gram, right = lax.optimization_barrier((gram, right))
    up1, down1 = from_z(gram, 1), from_z(gram, -1)
    up2, down2 = from_z(gram, 2), from_z(gram, -2)
    up1, down1, up2, down2, other_right = lax.optimization_barrier((up1, down1, up2, down2, from_y(right)))
    up3, down3 = from_z(up2, 1), from_z(down2, -1)
    up4, down4 = from_z(up2[:1], 2), from_z(down2[1:], -2)
    block = jnp.zeros((2, rows, width), bf16)
    pieces = ((0, gram), (1, up1), (-1, down1), (2, up2), (-2, down2), (3, up3), (-3, down3), (4, cat(up4, down4)))
    for step, piece in pieces:
        block = lax.dynamic_update_slice_in_dim(block, piece, ((z_pos + step) % 8) * unit, 1)
    got = from_core(block)
    low = jnp.where(core == 0, block, got)
    high = jnp.where(core == 0, got, block)
    gram_rows = cat(low[0], high[0], low[1], high[1], axis=1)

    x_blocks = (own, x_right, x_left, x_far, across, other_right, other_left, other_far)
    found, sent = found_part(got, x_blocks, found_part(block, x_blocks))
    right, left, across = gather_first(sent)
    far, across_right, across_left = gather_second(right, left, across)
    across_far = gather_third(far, across_right, across_left)
    three, seven = 3 * rows, 7 * rows
    product = dot(gram_rows[:, :three], cat(sent, right, left))
    product = product + dot(gram_rows[:, three:seven], cat(far, across, across_right, across_left))
    start = coef_a * own.astype(f32) + coef_b * found + coef_c * product
    scale = float(COLS) ** 0.5
    return (scale * (start + coef_c * dot(gram_rows[:, seven:], across_far))).astype(bf16)


def solution(mesh):
    return jax.shard_map(
        local,
        mesh=mesh,
        in_specs=(P("wide", "narrow"),),
        out_specs=P("wide", "narrow"),
        check_vma=False,
    )
```

```python
import functools

import jax
import jax.numpy as jnp
from jax import lax
from jax.experimental import pallas as pl
from jax.experimental.pallas import tpu as pltpu
from jax.sharding import PartitionSpec as P

COLS = 18432

coef_a = 3.4445
coef_b = -4.775
coef_c = 2.0315

Z_SIZE = 8
f32, bf16 = jnp.float32, jnp.bfloat16


def from_x(value, step):
    pairs = [(y * 4 + (x + step) % 4, y * 4 + x) for y in range(2) for x in range(4)]
    return lax.ppermute(value, "wide", pairs)


def from_y(value):
    return lax.ppermute(value, "wide", [(w, (w + 4) % 8) for w in range(8)])


def from_z(value, step):
    pairs = [(((z + step) % 8) * 4 + r, z * 4 + r) for z in range(8) for r in range(4)]
    return lax.ppermute(value, "narrow", pairs)


def from_y_hi(value):
    return lax.ppermute(value, "narrow", [(n, n ^ 2) for n in range(32)])


def from_y_both(value):
    pairs = [((w, n), ((w + 4) % 8, n ^ 2)) for w in range(8) for n in range(32)]
    return lax.ppermute(value, ("wide", "narrow"), [(a * 32 + b, c * 32 + d) for (a, b), (c, d) in pairs])


def from_core(value):
    return lax.ppermute(value, "narrow", [(n, n ^ 1) for n in range(32)])


def rows_of(left, right):
    return lax.dot_general(left, right, (((1,), (1,)), ((), ())), preferred_element_type=f32)


def dot(left, right):
    return jnp.dot(left, right, preferred_element_type=f32)


def cat(*parts, axis=0):
    return jnp.concatenate(parts, axis=axis)


def gather_first(own):
    return from_x(own, 1), from_x(own, -1), from_y(own)


def gather_second(right, left, across):
    half = right.shape[0] // 16 * 8
    via_y = from_y(cat(right[:half], left[:half]))
    via_right = from_x(cat(across[half:], right[:half]), 1)
    via_left = from_x(cat(across[half:], left[half:]), -1)
    rest = right.shape[0] - half
    far = cat(via_right[rest:], via_left[rest:])
    return far, cat(via_y[:half], via_right[:rest]), cat(via_y[half:], via_left[:rest])


def gather_third(far, across_right, across_left):
    third = far.shape[0] // 24 * 8
    part_y = from_y(far[:third])
    part_right = from_x(across_right[third : 2 * third], 1)
    part_left = from_x(across_left[2 * third :], -1)
    return cat(part_y, part_right, part_left)


def along_z(value, hops):
    pairs = [(z * 4 + r, (z + hops * (1 - 2 * (r % 2))) % 8 * 4 + r) for z in range(8) for r in range(4)]
    return lax.ppermute(value, "narrow", pairs)


def found_kernel(mine, *refs):
    block_ref, *x_refs = refs[:9]
    if mine:
        found_ref, lhs, rhs, sems = refs[9:]
    else:
        before_ref, found_ref, sent_ref, lhs, rhs, sems = refs[9:]
    rows, cols = x_refs[0].shape
    core = lax.rem(lax.axis_index("narrow"), 2)

    def run(picks):
        copies = [pltpu.make_async_copy(block_ref, lhs, sems.at[4])]
        for at, pick in enumerate(picks):
            copies.append(pltpu.make_async_copy(x_refs[pick], rhs.at[pl.ds(at * rows, rows)], sems.at[at]))
        for copy in copies:
            copy.start()
        for copy in copies:
            copy.wait()

    @pl.when(core == (0 if mine else 1))
    def _():
        run((0, 1, 4, 5))

    @pl.when(core == (1 if mine else 0))
    def _():
        run((2, 3, 6, 7))

    for start in range(0, cols, 256):
        part = pl.ds(start, min(256, cols - start))
        value = dot(lhs[0], rhs[: 2 * rows, part]) + dot(lhs[1], rhs[2 * rows :, part])
        if not mine:
            value = before_ref[:, part] + value
            sent_ref[:, part] = value.astype(bf16)
        found_ref[:, part] = value


def found_part(block, x_blocks, before=None):
    rows, cols = x_blocks[0].shape
    mine = before is None
    found = jax.ShapeDtypeStruct((rows, cols), f32)
    vmem = pl.BlockSpec(memory_space=pltpu.VMEM)
    return pl.pallas_call(
        functools.partial(found_kernel, mine),
        out_shape=found if mine else (found, jax.ShapeDtypeStruct((rows, cols), bf16)),
        in_specs=[pl.BlockSpec(memory_space=pl.ANY)] * 9 + ([] if mine else [vmem]),
        out_specs=vmem if mine else (vmem, vmem),
        scratch_shapes=[
            pltpu.VMEM(block.shape, bf16),
            pltpu.VMEM((4 * rows, cols), bf16),
            pltpu.SemaphoreType.DMA((5,)),
        ],
        compiler_params=pltpu.CompilerParams(vmem_limit_bytes=16 * 2**20),
        cost_estimate=pl.CostEstimate(flops=8 * rows * rows * cols, bytes_accessed=6 * 2**20, transcendentals=0),
    )(block, *x_blocks, *([] if mine else [before]))


def local(own):
    rows = own.shape[0]
    narrow_pos = lax.axis_index("narrow")
    core = narrow_pos % 2
    z_pos = narrow_pos // 4
    unit = rows // Z_SIZE

    right, left, across = gather_first(own)
    half_rows = rows // 2
    far = cat(from_x(right[:half_rows], 1), from_x(left[half_rows:], -1))
    same = cat(own, right, left, far)
    x_right, x_left, x_far = right, left, far

    both = cat(own, across)
    order = ((0, 4), (0, 3), (1, 3), (0, 2), (1, 2), (0, 1), (1, 1), (1, 0))

    def units_of(core):
        def place(which, step):
            owner = jnp.where(core == 0, which, 1 - which)
            return owner * rows + ((z_pos + step * (1 - 2 * core)) % 8) * unit

        return cat(*[lax.dynamic_slice_in_dim(both, place(*at), unit, 0) for at in order])

    given = rows_of(units_of(1 - core), same).astype(bf16)
    kept = lax.optimization_barrier(rows_of(units_of(core), same))
    summed = kept + from_core(given).astype(f32)

    def units(start, stop):
        return summed[start * unit : stop * unit]

    passed = along_z(units(1, 3).astype(bf16), 1).astype(f32) + jnp.pad(along_z(units(0, 1).astype(bf16), 2).astype(f32), ((0, unit), (0, 0)))
    two, one, other_left = lax.optimization_barrier(
        ((units(3, 5) + passed).astype(bf16), units(5, 7).astype(bf16), from_y(left))
    )
    passed = along_z(two, 2).astype(f32) + along_z(one, 1).astype(f32)
    total = passed + jnp.pad(units(7, 8), ((unit, 0), (0, 0)))
    total, other_far = lax.optimization_barrier((total, from_y(far)))

    width = 2 * rows
    total = jnp.where(core == 0, total, cat(total[unit:], total[:unit])).reshape(2, unit, 2 * width)
    given = lax.dynamic_slice_in_dim(total, (1 - core) * width, width, 2).astype(bf16)
    total = (lax.dynamic_slice_in_dim(total, core * width, width, 2) + from_core(given).astype(f32)).astype(bf16)

    gram_same = total[0].astype(f32) + from_y_hi(total[0]).astype(f32)
    gram_other = from_y(total[1]).astype(f32) + from_y_both(total[1]).astype(f32)
    gram = jnp.stack([gram_same, gram_other]).astype(bf16)

    gram, right = lax.optimization_barrier((gram, right))
    up1, down1 = from_z(gram, 1), from_z(gram, -1)
    up2, down2 = from_z(gram, 2), from_z(gram, -2)
    up1, down1, up2, down2, other_right = lax.optimization_barrier((up1, down1, up2, down2, from_y(right)))
    up3, down3 = from_z(up2, 1), from_z(down2, -1)
    up4, down4 = from_z(up2[:1], 2), from_z(down2[1:], -2)
    block = jnp.zeros((2, rows, width), bf16)
    pieces = ((0, gram), (1, up1), (-1, down1), (2, up2), (-2, down2), (3, up3), (-3, down3), (4, cat(up4, down4)))
    for step, piece in pieces:
        block = lax.dynamic_update_slice_in_dim(block, piece, ((z_pos + step) % 8) * unit, 1)
    got = from_core(block)
    low = jnp.where(core == 0, block, got)
    high = jnp.where(core == 0, got, block)
    gram_rows = cat(low[0], high[0], low[1], high[1], axis=1)

    x_blocks = (own, x_right, x_left, x_far, across, other_right, other_left, other_far)
    found, sent = found_part(got, x_blocks, found_part(block, x_blocks))
    right, left, across = gather_first(sent)
    far, across_right, across_left = gather_second(right, left, across)
    across_far = gather_third(far, across_right, across_left)
    three, seven = 3 * rows, 7 * rows
    product = dot(gram_rows[:, :three], cat(sent, right, left))
    product = product + dot(gram_rows[:, three:seven], cat(far, across, across_right, across_left))
    start = coef_a * own.astype(f32) + coef_b * found + coef_c * product
    scale = float(COLS) ** 0.5
    return (scale * (start + coef_c * dot(gram_rows[:, seven:], across_far))).astype(bf16)


def solution(mesh):
    return jax.shard_map(
        local,
        mesh=mesh,
        in_specs=(P("wide", "narrow"),),
        out_specs=P("wide", "narrow"),
        check_vma=False,
    )
```

```python
import functools

import jax
import jax.numpy as jnp
from jax import lax
from jax.experimental import pallas as pl
from jax.experimental.pallas import tpu as pltpu
from jax.sharding import PartitionSpec as P

COLS = 18432

coef_a = 3.4445
coef_b = -4.775
coef_c = 2.0315

Z_SIZE = 8
f32, bf16 = jnp.float32, jnp.bfloat16


def from_x(value, step):
    pairs = [(y * 4 + (x + step) % 4, y * 4 + x) for y in range(2) for x in range(4)]
    return lax.ppermute(value, "wide", pairs)


def from_y(value):
    return lax.ppermute(value, "wide", [(w, (w + 4) % 8) for w in range(8)])


def from_z(value, step):
    pairs = [(((z + step) % 8) * 4 + r, z * 4 + r) for z in range(8) for r in range(4)]
    return lax.ppermute(value, "narrow", pairs)


def from_y_hi(value):
    return lax.ppermute(value, "narrow", [(n, n ^ 2) for n in range(32)])


def from_y_both(value):
    pairs = [((w, n), ((w + 4) % 8, n ^ 2)) for w in range(8) for n in range(32)]
    return lax.ppermute(value, ("wide", "narrow"), [(a * 32 + b, c * 32 + d) for (a, b), (c, d) in pairs])


def from_core(value):
    return lax.ppermute(value, "narrow", [(n, n ^ 1) for n in range(32)])


def rows_of(left, right):
    return lax.dot_general(left, right, (((1,), (1,)), ((), ())), preferred_element_type=f32)


def dot(left, right):
    return jnp.dot(left, right, preferred_element_type=f32)


def cat(*parts, axis=0):
    return jnp.concatenate(parts, axis=axis)


def gather_first(own):
    return from_x(own, 1), from_x(own, -1), from_y(own)


def along_z(value, hops):
    pairs = [(z * 4 + r, (z + hops * (1 - 2 * (r % 2))) % 8 * 4 + r) for z in range(8) for r in range(4)]
    return lax.ppermute(value, "narrow", pairs)


def found_kernel(mine, *refs):
    block_ref, *x_refs = refs[:9]
    if mine:
        found_ref, lhs, rhs, sems = refs[9:]
    else:
        before_ref, found_ref, sent_ref, lhs, rhs, sems = refs[9:]
    rows, cols = x_refs[0].shape
    core = lax.rem(lax.axis_index("narrow"), 2)

    def run(picks):
        copies = [pltpu.make_async_copy(block_ref, lhs, sems.at[4])]
        for at, pick in enumerate(picks):
            copies.append(pltpu.make_async_copy(x_refs[pick], rhs.at[pl.ds(at * rows, rows)], sems.at[at]))
        for copy in copies:
            copy.start()
        for copy in copies:
            copy.wait()

    @pl.when(core == (0 if mine else 1))
    def _():
        run((0, 1, 4, 5))

    @pl.when(core == (1 if mine else 0))
    def _():
        run((2, 3, 6, 7))

    for start in range(0, cols, 256):
        part = pl.ds(start, min(256, cols - start))
        value = dot(lhs[0], rhs[: 2 * rows, part]) + dot(lhs[1], rhs[2 * rows :, part])
        if not mine:
            value = before_ref[:, part] + value
            sent_ref[:, part] = value.astype(bf16)
        found_ref[:, part] = value


def found_part(block, x_blocks, before=None):
    rows, cols = x_blocks[0].shape
    mine = before is None
    found = jax.ShapeDtypeStruct((rows, cols), f32)
    vmem = pl.BlockSpec(memory_space=pltpu.VMEM)
    return pl.pallas_call(
        functools.partial(found_kernel, mine),
        out_shape=found if mine else (found, jax.ShapeDtypeStruct((rows, cols), bf16)),
        in_specs=[pl.BlockSpec(memory_space=pl.ANY)] * 9 + ([] if mine else [vmem]),
        out_specs=vmem if mine else (vmem, vmem),
        scratch_shapes=[
            pltpu.VMEM(block.shape, bf16),
            pltpu.VMEM((4 * rows, cols), bf16),
            pltpu.SemaphoreType.DMA((5,)),
        ],
        compiler_params=pltpu.CompilerParams(vmem_limit_bytes=9 * 2**20),
        cost_estimate=pl.CostEstimate(flops=8 * rows * rows * cols, bytes_accessed=6 * 2**20, transcendentals=0),
    )(block, *x_blocks, *([] if mine else [before]))


def local(own):
    rows = own.shape[0]
    narrow_pos = lax.axis_index("narrow")
    core = narrow_pos % 2
    z_pos = narrow_pos // 4
    unit = rows // Z_SIZE

    right, left, across = gather_first(own)
    half_rows = rows // 2
    far = cat(from_x(right[:half_rows], 1), from_x(left[half_rows:], -1))
    same = cat(own, right, left, far)
    x_right, x_left, x_far = right, left, far

    both = cat(own, across)
    order = ((0, 4), (0, 3), (1, 3), (0, 2), (1, 2), (0, 1), (1, 1), (1, 0))

    def units_of(core):
        def place(which, step):
            owner = jnp.where(core == 0, which, 1 - which)
            return owner * rows + ((z_pos + step * (1 - 2 * core)) % 8) * unit

        return cat(*[lax.dynamic_slice_in_dim(both, place(*at), unit, 0) for at in order])

    given = rows_of(units_of(1 - core), same).astype(bf16)
    kept = lax.optimization_barrier(rows_of(units_of(core), same))
    summed = kept + from_core(given).astype(f32)

    def units(start, stop):
        return summed[start * unit : stop * unit]

    passed = along_z(units(1, 3).astype(bf16), 1).astype(f32) + jnp.pad(along_z(units(0, 1).astype(bf16), 2).astype(f32), ((0, unit), (0, 0)))
    two, one, late_across, late_far = lax.optimization_barrier(
        ((units(3, 5) + passed).astype(bf16), units(5, 7).astype(bf16), across, far)
    )
    passed = along_z(two, 2).astype(f32) + along_z(one, 1).astype(f32)
    total = passed + jnp.pad(units(7, 8), ((unit, 0), (0, 0)))
    others = (from_x(late_across, 1), from_x(late_across, -1), from_y(late_far))
    total, other_right, other_left, other_far = lax.optimization_barrier((total, *others))

    width = 2 * rows
    total = jnp.where(core == 0, total, cat(total[unit:], total[:unit])).reshape(2, unit, 2 * width)
    given = lax.dynamic_slice_in_dim(total, (1 - core) * width, width, 2).astype(bf16)
    total = (lax.dynamic_slice_in_dim(total, core * width, width, 2) + from_core(given).astype(f32)).astype(bf16)

    gram_same = total[0].astype(f32) + from_y_hi(total[0]).astype(f32)
    gram_other = from_y(total[1]).astype(f32) + from_y_both(total[1]).astype(f32)
    gram = jnp.stack([gram_same, gram_other]).astype(bf16)

    up1, down1 = from_z(gram, 1), from_z(gram, -1)
    up2, down2 = from_z(gram, 2), from_z(gram, -2)
    up3, down3 = from_z(up2, 1), from_z(down2, -1)
    up4, down4 = from_z(up2[:1], 2), from_z(down2[1:], -2)
    block = jnp.zeros((2, rows, width), bf16)
    pieces = ((0, gram), (1, up1), (-1, down1), (2, up2), (-2, down2), (3, up3), (-3, down3), (4, cat(up4, down4)))
    for step, piece in pieces:
        block = lax.dynamic_update_slice_in_dim(block, piece, ((z_pos + step) % 8) * unit, 1)
    got = from_core(block)
    low = jnp.where(core == 0, block, got)
    high = jnp.where(core == 0, got, block)
    gram_rows = cat(low[0], high[0], low[1], high[1], axis=1)

    x_blocks = (own, x_right, x_left, x_far, across, other_right, other_left, other_far)
    found, sent = found_part(got, x_blocks, found_part(block, x_blocks))
    right, left, across = gather_first(sent)
    half, few = rows // 2, rows // 48 * 8
    via_y = from_y(cat(right[few:], left[few:]))
    via_right = from_x(cat(right[:half], across[:few]), 1)
    via_left = from_x(cat(left[half:], across[:few]), -1)
    across_far = from_x(across, 2)
    far = cat(via_right[:half], via_left[:half])
    across_right = cat(via_right[half:], via_y[: rows - few])
    across_left = cat(via_left[half:], via_y[rows - few :])

    three, four, five = 3 * rows, 4 * rows, 5 * rows
    product = dot(gram_rows[:, :three], cat(sent, right, left)) + dot(gram_rows[:, four:five], across)
    start = coef_a * own.astype(f32) + coef_b * found + coef_c * product
    scale = float(COLS) ** 0.5
    last = dot(gram_rows[:, three:four], far) + dot(gram_rows[:, five:], cat(across_right, across_left, across_far))
    return (scale * (start + coef_c * last)).astype(bf16)


def solution(mesh):
    return jax.shard_map(
        local,
        mesh=mesh,
        in_specs=(P("wide", "narrow"),),
        out_specs=P("wide", "narrow"),
        check_vma=False,
    )
```

```python
import functools

import jax
import jax.numpy as jnp
from jax import lax
from jax.experimental import pallas as pl
from jax.experimental.pallas import tpu as pltpu
from jax.sharding import PartitionSpec as P

COLS = 18432

coef_a = 3.4445
coef_b = -4.775
coef_c = 2.0315

Z_SIZE = 8
f32, bf16 = jnp.float32, jnp.bfloat16


def from_x(value, step):
    pairs = [(y * 4 + (x + step) % 4, y * 4 + x) for y in range(2) for x in range(4)]
    return lax.ppermute(value, "wide", pairs)


def from_y(value):
    return lax.ppermute(value, "wide", [(w, (w + 4) % 8) for w in range(8)])


def from_z(value, step):
    pairs = [(((z + step) % 8) * 4 + r, z * 4 + r) for z in range(8) for r in range(4)]
    return lax.ppermute(value, "narrow", pairs)


def from_y_hi(value):
    return lax.ppermute(value, "narrow", [(n, n ^ 2) for n in range(32)])


def from_y_both(value):
    pairs = [((w, n), ((w + 4) % 8, n ^ 2)) for w in range(8) for n in range(32)]
    return lax.ppermute(value, ("wide", "narrow"), [(a * 32 + b, c * 32 + d) for (a, b), (c, d) in pairs])


def from_core(value):
    return lax.ppermute(value, "narrow", [(n, n ^ 1) for n in range(32)])


def rows_of(left, right):
    return lax.dot_general(left, right, (((1,), (1,)), ((), ())), preferred_element_type=f32)


def dot(left, right):
    return jnp.dot(left, right, preferred_element_type=f32)


def cat(*parts, axis=0):
    return jnp.concatenate(parts, axis=axis)


def gather_first(own):
    return from_x(own, 1), from_x(own, -1), from_y(own)


def along_z(value, hops):
    pairs = [(z * 4 + r, (z + hops * (1 - 2 * (r % 2))) % 8 * 4 + r) for z in range(8) for r in range(4)]
    return lax.ppermute(value, "narrow", pairs)


def found_kernel(mine, *refs):
    block_ref, *x_refs = refs[:9]
    if mine:
        found_ref, lhs, rhs, sems = refs[9:]
    else:
        before_ref, found_ref, sent_ref, lhs, rhs, sems = refs[9:]
    rows, cols = x_refs[0].shape
    core = lax.rem(lax.axis_index("narrow"), 2)

    def run(picks):
        copies = [pltpu.make_async_copy(block_ref, lhs, sems.at[4])]
        for at, pick in enumerate(picks):
            copies.append(pltpu.make_async_copy(x_refs[pick], rhs.at[pl.ds(at * rows, rows)], sems.at[at]))
        for copy in copies:
            copy.start()
        for copy in copies:
            copy.wait()

    @pl.when(core == (0 if mine else 1))
    def _():
        run((0, 1, 4, 5))

    @pl.when(core == (1 if mine else 0))
    def _():
        run((2, 3, 6, 7))

    for start in range(0, cols, 256):
        part = pl.ds(start, min(256, cols - start))
        value = dot(lhs[0], rhs[: 2 * rows, part]) + dot(lhs[1], rhs[2 * rows :, part])
        if not mine:
            value = before_ref[:, part] + value
            sent_ref[:, part] = value.astype(bf16)
        found_ref[:, part] = value


def found_part(block, x_blocks, before=None):
    rows, cols = x_blocks[0].shape
    mine = before is None
    found = jax.ShapeDtypeStruct((rows, cols), f32)
    vmem = pl.BlockSpec(memory_space=pltpu.VMEM)
    return pl.pallas_call(
        functools.partial(found_kernel, mine),
        out_shape=found if mine else (found, jax.ShapeDtypeStruct((rows, cols), bf16)),
        in_specs=[pl.BlockSpec(memory_space=pl.ANY)] * 9 + ([] if mine else [vmem]),
        out_specs=vmem if mine else (vmem, vmem),
        scratch_shapes=[
            pltpu.VMEM(block.shape, bf16),
            pltpu.VMEM((4 * rows, cols), bf16),
            pltpu.SemaphoreType.DMA((5,)),
        ],
        compiler_params=pltpu.CompilerParams(vmem_limit_bytes=9 * 2**20),
        cost_estimate=pl.CostEstimate(flops=8 * rows * rows * cols, bytes_accessed=6 * 2**20, transcendentals=0),
    )(block, *x_blocks, *([] if mine else [before]))


def close_kernel(few, block_ref, got_ref, *refs):
    own_y, right, left, across, via_y, via_right, via_left, across_far = refs[:8]
    found_ref, own_ref, out_ref, lhs, rhs, total, sems = refs[8:]
    rows, cols = own_ref.shape
    half, more = rows // 2, rows - few
    core = lax.rem(lax.axis_index("narrow"), 2)

    pieces = [
        (block_ref, lhs.at[core]),
        (got_ref, lhs.at[1 - core]),
        (own_y, 0),
        (right, rows),
        (left, 2 * rows),
        (via_right.at[pl.ds(0, half)], 3 * rows),
        (via_left.at[pl.ds(0, half)], 3 * rows + half),
        (across, 4 * rows),
        (via_right.at[pl.ds(half, few)], 5 * rows),
        (via_y.at[pl.ds(0, more)], 5 * rows + few),
        (via_left.at[pl.ds(half, few)], 6 * rows),
        (via_y.at[pl.ds(more, more)], 6 * rows + few),
        (across_far, 7 * rows),
    ]
    copies = []
    for at, (source, place) in enumerate(pieces):
        target = rhs.at[pl.ds(place, source.shape[0])] if isinstance(place, int) else place
        copies.append(pltpu.make_async_copy(source, target, sems.at[at]))
    for copy in copies:
        copy.start()
    parts = [pl.ds(start, min(256, cols - start)) for start in range(0, cols, 256)]
    width = 2 * rows
    for copy in copies[:7]:
        copy.wait()
    for part in parts:
        total[:, part] = dot(lhs[0, 0], rhs[:width, part]) + dot(lhs[1, 0], rhs[width : 2 * width, part])
    for copy in copies[7:]:
        copy.wait()
    scale = float(COLS) ** 0.5
    for part in parts:
        value = dot(lhs[0, 1], rhs[2 * width : 3 * width, part]) + dot(lhs[1, 1], rhs[3 * width :, part])
        value = coef_b * found_ref[:, part] + coef_c * (total[:, part] + value)
        out_ref[:, part] = (scale * (coef_a * own_ref[:, part].astype(f32) + value)).astype(bf16)


def close(few, block, got, blocks, found, own):
    rows, cols = own.shape
    vmem = pl.BlockSpec(memory_space=pltpu.VMEM)
    return pl.pallas_call(
        functools.partial(close_kernel, few),
        out_shape=jax.ShapeDtypeStruct((rows, cols), bf16),
        in_specs=[pl.BlockSpec(memory_space=pl.ANY)] * 10 + [vmem, vmem],
        out_specs=vmem,
        scratch_shapes=[
            pltpu.VMEM((2, *block.shape), bf16),
            pltpu.VMEM((8 * rows, cols), bf16),
            pltpu.VMEM((rows, cols), f32),
            pltpu.SemaphoreType.DMA((13,)),
        ],
        compiler_params=pltpu.CompilerParams(vmem_limit_bytes=16 * 2**20),
        cost_estimate=pl.CostEstimate(flops=16 * rows * rows * cols, bytes_accessed=10 * 2**20, transcendentals=0),
    )(block, got, *blocks, found, own)


def local(own):
    rows = own.shape[0]
    narrow_pos = lax.axis_index("narrow")
    core = narrow_pos % 2
    z_pos = narrow_pos // 4
    unit = rows // Z_SIZE

    right, left, across = gather_first(own)
    half_rows = rows // 2
    far = cat(from_x(right[:half_rows], 1), from_x(left[half_rows:], -1))
    same = cat(own, right, left, far)
    x_right, x_left, x_far = right, left, far

    both = cat(own, across)
    order = ((0, 4), (0, 3), (1, 3), (0, 2), (1, 2), (0, 1), (1, 1), (1, 0))

    def units_of(core):
        def place(which, step):
            owner = jnp.where(core == 0, which, 1 - which)
            return owner * rows + ((z_pos + step * (1 - 2 * core)) % 8) * unit

        return cat(*[lax.dynamic_slice_in_dim(both, place(*at), unit, 0) for at in order])

    given = rows_of(units_of(1 - core), same).astype(bf16)
    kept = lax.optimization_barrier(rows_of(units_of(core), same))
    summed = kept + from_core(given).astype(f32)

    def units(start, stop):
        return summed[start * unit : stop * unit]

    passed = along_z(units(1, 3).astype(bf16), 1).astype(f32) + jnp.pad(along_z(units(0, 1).astype(bf16), 2).astype(f32), ((0, unit), (0, 0)))
    two, one, late_across, late_far = lax.optimization_barrier(
        ((units(3, 5) + passed).astype(bf16), units(5, 7).astype(bf16), across, far)
    )
    passed = along_z(two, 2).astype(f32) + along_z(one, 1).astype(f32)
    total = passed + jnp.pad(units(7, 8), ((unit, 0), (0, 0)))
    others = (from_x(late_across, 1), from_x(late_across, -1), from_y(late_far))
    total, other_right, other_left, other_far = lax.optimization_barrier((total, *others))

    width = 2 * rows
    total = jnp.where(core == 0, total, cat(total[unit:], total[:unit])).reshape(2, unit, 2 * width)
    given = lax.dynamic_slice_in_dim(total, (1 - core) * width, width, 2).astype(bf16)
    total = (lax.dynamic_slice_in_dim(total, core * width, width, 2) + from_core(given).astype(f32)).astype(bf16)

    gram_same = total[0].astype(f32) + from_y_hi(total[0]).astype(f32)
    gram_other = from_y(total[1]).astype(f32) + from_y_both(total[1]).astype(f32)
    gram = jnp.stack([gram_same, gram_other]).astype(bf16)

    up1, down1 = from_z(gram, 1), from_z(gram, -1)
    up2, down2 = from_z(gram, 2), from_z(gram, -2)
    up3, down3 = from_z(up2, 1), from_z(down2, -1)
    up4, down4 = from_z(up2[:1], 2), from_z(down2[1:], -2)
    block = jnp.zeros((2, rows, width), bf16)
    pieces = ((0, gram), (1, up1), (-1, down1), (2, up2), (-2, down2), (3, up3), (-3, down3), (4, cat(up4, down4)))
    for step, piece in pieces:
        block = lax.dynamic_update_slice_in_dim(block, piece, ((z_pos + step) % 8) * unit, 1)
    got = from_core(block)
    x_blocks = (own, x_right, x_left, x_far, across, other_right, other_left, other_far)
    found, sent = found_part(got, x_blocks, found_part(block, x_blocks))
    right, left, across = gather_first(sent)
    half, few = rows // 2, 80
    via_y = from_y(cat(right[few:], left[few:]))
    via_right = from_x(cat(right[:half], across[:few]), 1)
    via_left = from_x(cat(left[half:], across[:few]), -1)
    across_far = from_x(across, 2)
    return close(few, block, got, (sent, right, left, across, via_y, via_right, via_left, across_far), found, own)


def solution(mesh):
    return jax.shard_map(
        local,
        mesh=mesh,
        in_specs=(P("wide", "narrow"),),
        out_specs=P("wide", "narrow"),
        check_vma=False,
    )
```

```python
import functools

import jax
import jax.numpy as jnp
from jax import lax
from jax.experimental import pallas as pl
from jax.experimental.pallas import tpu as pltpu
from jax.sharding import PartitionSpec as P

COLS = 18432

coef_a = 3.4445
coef_b = -4.775
coef_c = 2.0315

Z_SIZE = 8
f32, bf16 = jnp.float32, jnp.bfloat16


def from_x(value, step):
    pairs = [(y * 4 + (x + step) % 4, y * 4 + x) for y in range(2) for x in range(4)]
    return lax.ppermute(value, "wide", pairs)


def from_y(value):
    return lax.ppermute(value, "wide", [(w, (w + 4) % 8) for w in range(8)])


def from_z(value, step):
    pairs = [(((z + step) % 8) * 4 + r, z * 4 + r) for z in range(8) for r in range(4)]
    return lax.ppermute(value, "narrow", pairs)


def from_y_hi(value):
    return lax.ppermute(value, "narrow", [(n, n ^ 2) for n in range(32)])


def from_y_both(value):
    pairs = [((w, n), ((w + 4) % 8, n ^ 2)) for w in range(8) for n in range(32)]
    return lax.ppermute(value, ("wide", "narrow"), [(a * 32 + b, c * 32 + d) for (a, b), (c, d) in pairs])


def from_core(value):
    return lax.ppermute(value, "narrow", [(n, n ^ 1) for n in range(32)])


def rows_of(left, right):
    return lax.dot_general(left, right, (((1,), (1,)), ((), ())), preferred_element_type=f32)


def dot(left, right):
    return jnp.dot(left, right, preferred_element_type=f32)


def cat(*parts, axis=0):
    return jnp.concatenate(parts, axis=axis)


def gather_first(own):
    return from_x(own, 1), from_x(own, -1), from_y(own)


def along_z(value, hops):
    pairs = [(z * 4 + r, (z + hops * (1 - 2 * (r % 2))) % 8 * 4 + r) for z in range(8) for r in range(4)]
    return lax.ppermute(value, "narrow", pairs)


def found_kernel(mine, *refs):
    block_ref, *x_refs = refs[:9]
    if mine:
        found_ref, lhs, rhs, sems = refs[9:]
    else:
        before_ref, found_ref, sent_ref, lhs, rhs, sems = refs[9:]
    rows, cols = x_refs[0].shape
    core = lax.rem(lax.axis_index("narrow"), 2)

    def run(picks):
        copies = [pltpu.make_async_copy(block_ref, lhs, sems.at[4])]
        for at, pick in enumerate(picks):
            copies.append(pltpu.make_async_copy(x_refs[pick], rhs.at[pl.ds(at * rows, rows)], sems.at[at]))
        for copy in copies:
            copy.start()

    @pl.when(core == (0 if mine else 1))
    def _():
        run((0, 1, 4, 5))

    @pl.when(core == (1 if mine else 0))
    def _():
        run((2, 3, 6, 7))

    def wait(at):
        pltpu.make_async_copy(x_refs[at], rhs.at[pl.ds(at * rows, rows)], sems.at[at]).wait()

    parts = [pl.ds(start, min(256, cols - start)) for start in range(0, cols, 256)]
    pltpu.make_async_copy(block_ref, lhs, sems.at[4]).wait()
    wait(0)
    wait(1)
    for part in parts:
        found_ref[:, part] = dot(lhs[0], rhs[: 2 * rows, part])
    wait(2)
    wait(3)
    for part in parts:
        value = found_ref[:, part] + dot(lhs[1], rhs[2 * rows :, part])
        if not mine:
            value = before_ref[:, part] + value
            sent_ref[:, part] = value.astype(bf16)
        found_ref[:, part] = value


def found_part(block, x_blocks, before=None):
    rows, cols = x_blocks[0].shape
    mine = before is None
    found = jax.ShapeDtypeStruct((rows, cols), f32)
    vmem = pl.BlockSpec(memory_space=pltpu.VMEM)
    return pl.pallas_call(
        functools.partial(found_kernel, mine),
        out_shape=found if mine else (found, jax.ShapeDtypeStruct((rows, cols), bf16)),
        in_specs=[pl.BlockSpec(memory_space=pl.ANY)] * 9 + ([] if mine else [vmem]),
        out_specs=vmem if mine else (vmem, vmem),
        scratch_shapes=[
            pltpu.VMEM(block.shape, bf16),
            pltpu.VMEM((4 * rows, cols), bf16),
            pltpu.SemaphoreType.DMA((5,)),
        ],
        compiler_params=pltpu.CompilerParams(vmem_limit_bytes=9 * 2**20),
        cost_estimate=pl.CostEstimate(flops=8 * rows * rows * cols, bytes_accessed=6 * 2**20, transcendentals=0),
    )(block, *x_blocks, *([] if mine else [before]))


def open_kernel(block_ref, got_ref, own_y, right, found_ref, own_ref, begun_ref, lhs, rhs, sems):
    rows, cols = own_ref.shape
    core = lax.rem(lax.axis_index("narrow"), 2)
    copies = [
        pltpu.make_async_copy(block_ref.at[0], lhs.at[core], sems.at[0]),
        pltpu.make_async_copy(got_ref.at[0], lhs.at[1 - core], sems.at[1]),
        pltpu.make_async_copy(own_y, rhs.at[pl.ds(0, rows)], sems.at[2]),
        pltpu.make_async_copy(right, rhs.at[pl.ds(rows, rows)], sems.at[3]),
    ]
    for copy in copies:
        copy.start()
    for copy in copies:
        copy.wait()
    for start in range(0, cols, 256):
        part = pl.ds(start, min(256, cols - start))
        value = coef_a * own_ref[:, part].astype(f32) + coef_b * found_ref[:, part]
        begun_ref[:, part] = value + coef_c * dot(lhs[0], rhs[:, part])


def close_kernel(few, block_ref, got_ref, *refs):
    left, across, via_y, via_right, via_left, across_far = refs[:6]
    begun_ref, out_ref, lhs, rhs, total, sems = refs[6:]
    rows, cols = out_ref.shape
    half, more = rows // 2, rows - few
    core = lax.rem(lax.axis_index("narrow"), 2)

    pieces = [
        (block_ref, lhs.at[core]),
        (got_ref, lhs.at[1 - core]),
        (left, 0),
        (via_right.at[pl.ds(0, half)], rows),
        (via_left.at[pl.ds(0, half)], rows + half),
        (across, 2 * rows),
        (via_right.at[pl.ds(half, few)], 3 * rows),
        (via_y.at[pl.ds(0, more)], 3 * rows + few),
        (via_left.at[pl.ds(half, few)], 4 * rows),
        (via_y.at[pl.ds(more, more)], 4 * rows + few),
        (across_far, 5 * rows),
    ]
    copies = []
    for at, (source, place) in enumerate(pieces):
        target = rhs.at[pl.ds(place, source.shape[0])] if isinstance(place, int) else place
        copies.append(pltpu.make_async_copy(source, target, sems.at[at]))
    for copy in copies:
        copy.start()
    parts = [pl.ds(start, min(256, cols - start)) for start in range(0, cols, 256)]
    width = 2 * rows
    for copy in copies[:5]:
        copy.wait()
    for part in parts:
        total[:, part] = dot(lhs[1, 0], rhs[:width, part])
    for copy in copies[5:]:
        copy.wait()
    scale = float(COLS) ** 0.5
    for part in parts:
        value = dot(lhs[0, 1], rhs[width : 2 * width, part]) + dot(lhs[1, 1], rhs[2 * width :, part])
        out_ref[:, part] = (scale * (begun_ref[:, part] + coef_c * (total[:, part] + value))).astype(bf16)


def open_product(block, got, own_y, right, found, own):
    rows, cols = own.shape
    vmem = pl.BlockSpec(memory_space=pltpu.VMEM)
    return pl.pallas_call(
        open_kernel,
        out_shape=jax.ShapeDtypeStruct((rows, cols), f32),
        in_specs=[pl.BlockSpec(memory_space=pl.ANY)] * 4 + [vmem, vmem],
        out_specs=vmem,
        scratch_shapes=[
            pltpu.VMEM(block.shape, bf16),
            pltpu.VMEM((2 * rows, cols), bf16),
            pltpu.SemaphoreType.DMA((4,)),
        ],
        compiler_params=pltpu.CompilerParams(vmem_limit_bytes=12 * 2**20),
        cost_estimate=pl.CostEstimate(flops=4 * rows * rows * cols, bytes_accessed=5 * 2**20, transcendentals=0),
    )(block, got, own_y, right, found, own)


def close_product(few, block, got, blocks, begun):
    rows, cols = begun.shape
    vmem = pl.BlockSpec(memory_space=pltpu.VMEM)
    return pl.pallas_call(
        functools.partial(close_kernel, few),
        out_shape=jax.ShapeDtypeStruct((rows, cols), bf16),
        in_specs=[pl.BlockSpec(memory_space=pltpu.HBM)] * 8 + [vmem],
        out_specs=vmem,
        scratch_shapes=[
            pltpu.VMEM((2, *block.shape), bf16),
            pltpu.VMEM((6 * rows, cols), bf16),
            pltpu.VMEM((rows, cols), f32),
            pltpu.SemaphoreType.DMA((11,)),
        ],
        compiler_params=pltpu.CompilerParams(vmem_limit_bytes=16 * 2**20),
        cost_estimate=pl.CostEstimate(flops=12 * rows * rows * cols, bytes_accessed=9 * 2**20, transcendentals=0),
    )(block, got, *blocks, begun)


def local(own):
    rows = own.shape[0]
    narrow_pos = lax.axis_index("narrow")
    core = narrow_pos % 2
    z_pos = narrow_pos // 4
    unit = rows // Z_SIZE

    right, left, across = gather_first(own)
    half_rows = rows // 2
    far = cat(from_x(right[:half_rows], 1), from_x(left[half_rows:], -1))
    same = cat(own, right, left, far)
    x_right, x_left, x_far = right, left, far

    both = cat(own, across)
    order = ((0, 4), (0, 3), (1, 3), (0, 2), (1, 2), (0, 1), (1, 1), (1, 0))

    def units_of(core):
        def place(which, step):
            owner = jnp.where(core == 0, which, 1 - which)
            return owner * rows + ((z_pos + step * (1 - 2 * core)) % 8) * unit

        return cat(*[lax.dynamic_slice_in_dim(both, place(*at), unit, 0) for at in order])

    given = rows_of(units_of(1 - core), same).astype(bf16)
    kept = lax.optimization_barrier(rows_of(units_of(core), same))
    summed = kept + from_core(given).astype(f32)

    def units(start, stop):
        return summed[start * unit : stop * unit]

    passed = along_z(units(1, 3).astype(bf16), 1).astype(f32) + jnp.pad(along_z(units(0, 1).astype(bf16), 2).astype(f32), ((0, unit), (0, 0)))
    two, one, late_across, late_far = lax.optimization_barrier(
        ((units(3, 5) + passed).astype(bf16), units(5, 7).astype(bf16), across, far)
    )
    passed = along_z(two, 2).astype(f32) + along_z(one, 1).astype(f32)
    total = passed + jnp.pad(units(7, 8), ((unit, 0), (0, 0)))
    others = (from_x(late_across, 1), from_x(late_across, -1), from_y(late_far))
    total, other_right, other_left, other_far = lax.optimization_barrier((total, *others))

    width = 2 * rows
    total = jnp.where(core == 0, total, cat(total[unit:], total[:unit])).reshape(2, unit, 2 * width)
    given = lax.dynamic_slice_in_dim(total, (1 - core) * width, width, 2).astype(bf16)
    total = (lax.dynamic_slice_in_dim(total, core * width, width, 2) + from_core(given).astype(f32)).astype(bf16)

    gram_same = total[0].astype(f32) + from_y_hi(total[0]).astype(f32)
    gram_other = from_y(total[1]).astype(f32) + from_y_both(total[1]).astype(f32)
    gram = jnp.stack([gram_same, gram_other]).astype(bf16)

    up1, down1 = from_z(gram, 1), from_z(gram, -1)
    up2, down2 = from_z(gram, 2), from_z(gram, -2)
    up3, down3 = from_z(up2, 1), from_z(down2, -1)
    up4, down4 = from_z(up2[:1], 2), from_z(down2[1:], -2)
    block = jnp.zeros((2, rows, width), bf16)
    pieces = ((0, gram), (1, up1), (-1, down1), (2, up2), (-2, down2), (3, up3), (-3, down3), (4, cat(up4, down4)))
    for step, piece in pieces:
        block = lax.dynamic_update_slice_in_dim(block, piece, ((z_pos + step) % 8) * unit, 1)
    got = from_core(block)
    x_blocks = (own, x_right, x_left, x_far, across, other_right, other_left, other_far)
    found, sent = found_part(got, x_blocks, found_part(block, x_blocks))
    right, left, across = gather_first(sent)
    half, few = rows // 2, rows // 4
    via_y = from_y(cat(right[few:], left[few:]))
    via_right = from_x(cat(right[:half], across[:few]), 1)
    via_left = from_x(cat(left[half:], across[:few]), -1)
    across_far = from_x(across, 2)
    begun = open_product(block, got, sent, right, found, own)
    return close_product(few, block, got, (left, across, via_y, via_right, via_left, across_far), begun)


def solution(mesh):
    return jax.shard_map(
        local,
        mesh=mesh,
        in_specs=(P("wide", "narrow"),),
        out_specs=P("wide", "narrow"),
        check_vma=False,
    )
```

```python
import functools

import jax
import jax.numpy as jnp
from jax import lax
from jax.experimental import pallas as pl
from jax.experimental.pallas import tpu as pltpu
from jax.sharding import PartitionSpec as P

COLS = 18432

coef_a = 3.4445
coef_b = -4.775
coef_c = 2.0315

Z_SIZE = 8
f32, bf16 = jnp.float32, jnp.bfloat16


def from_x(value, step):
    pairs = [(y * 4 + (x + step) % 4, y * 4 + x) for y in range(2) for x in range(4)]
    return lax.ppermute(value, "wide", pairs)


def from_y(value):
    return lax.ppermute(value, "wide", [(w, (w + 4) % 8) for w in range(8)])


def from_z(value, step):
    pairs = [(((z + step) % 8) * 4 + r, z * 4 + r) for z in range(8) for r in range(4)]
    return lax.ppermute(value, "narrow", pairs)


def from_y_hi(value):
    return lax.ppermute(value, "narrow", [(n, n ^ 2) for n in range(32)])


def from_y_both(value):
    pairs = [((w, n), ((w + 4) % 8, n ^ 2)) for w in range(8) for n in range(32)]
    return lax.ppermute(value, ("wide", "narrow"), [(a * 32 + b, c * 32 + d) for (a, b), (c, d) in pairs])


def from_core(value):
    return lax.ppermute(value, "narrow", [(n, n ^ 1) for n in range(32)])


def rows_of(left, right):
    return lax.dot_general(left, right, (((1,), (1,)), ((), ())), preferred_element_type=f32)


def dot(left, right):
    return jnp.dot(left, right, preferred_element_type=f32)


def cat(*parts, axis=0):
    return jnp.concatenate(parts, axis=axis)


def gather_first(own):
    return from_x(own, 1), from_x(own, -1), from_y(own)


def along_z(value, hops):
    pairs = [(z * 4 + r, (z + hops * (1 - 2 * (r % 2))) % 8 * 4 + r) for z in range(8) for r in range(4)]
    return lax.ppermute(value, "narrow", pairs)


def found_kernel(mine, *refs):
    block_ref, *x_refs = refs[:9]
    if mine:
        found_ref, lhs, rhs, sems = refs[9:]
    else:
        before_ref, found_ref, sent_ref, lhs, rhs, sems = refs[9:]
    rows, cols = x_refs[0].shape
    core = lax.rem(lax.axis_index("narrow"), 2)

    def run(picks):
        copies = [pltpu.make_async_copy(block_ref, lhs, sems.at[4])]
        for at, pick in enumerate(picks):
            copies.append(pltpu.make_async_copy(x_refs[pick], rhs.at[pl.ds(at * rows, rows)], sems.at[at]))
        for copy in copies:
            copy.start()

    @pl.when(core == (0 if mine else 1))
    def _():
        run((0, 1, 4, 5))

    @pl.when(core == (1 if mine else 0))
    def _():
        run((2, 3, 6, 7))

    def wait(at):
        pltpu.make_async_copy(x_refs[at], rhs.at[pl.ds(at * rows, rows)], sems.at[at]).wait()

    parts = [pl.ds(start, min(256, cols - start)) for start in range(0, cols, 256)]
    pltpu.make_async_copy(block_ref, lhs, sems.at[4]).wait()
    wait(0)
    wait(1)
    for part in parts:
        found_ref[:, part] = dot(lhs[0], rhs[: 2 * rows, part])
    wait(2)
    wait(3)
    for part in parts:
        value = found_ref[:, part] + dot(lhs[1], rhs[2 * rows :, part])
        if not mine:
            value = before_ref[:, part] + value
            sent_ref[:, part] = value.astype(bf16)
        found_ref[:, part] = value


def found_part(block, x_blocks, before=None):
    rows, cols = x_blocks[0].shape
    mine = before is None
    found = jax.ShapeDtypeStruct((rows, cols), f32)
    vmem = pl.BlockSpec(memory_space=pltpu.VMEM)
    return pl.pallas_call(
        functools.partial(found_kernel, mine),
        out_shape=found if mine else (found, jax.ShapeDtypeStruct((rows, cols), bf16)),
        in_specs=[pl.BlockSpec(memory_space=pl.ANY)] * 9 + ([] if mine else [vmem]),
        out_specs=vmem if mine else (vmem, vmem),
        scratch_shapes=[
            pltpu.VMEM(block.shape, bf16),
            pltpu.VMEM((4 * rows, cols), bf16),
            pltpu.SemaphoreType.DMA((5,)),
        ],
        compiler_params=pltpu.CompilerParams(vmem_limit_bytes=9 * 2**20),
        cost_estimate=pl.CostEstimate(flops=8 * rows * rows * cols, bytes_accessed=6 * 2**20, transcendentals=0),
    )(block, *x_blocks, *([] if mine else [before]))


def open_kernel(lhs_ref, own_y, right, left, across, found_ref, own_ref, begun_ref, lhs, rhs, sems):
    rows, cols = own_ref.shape
    copies = [pltpu.make_async_copy(lhs_ref, lhs, sems.at[4])]
    for at, block in enumerate((own_y, right, left, across)):
        copies.append(pltpu.make_async_copy(block, rhs.at[pl.ds(at * rows, rows)], sems.at[at]))
    for copy in copies:
        copy.start()
    for copy in copies:
        copy.wait()
    for start in range(0, cols, 256):
        part = pl.ds(start, min(256, cols - start))
        value = coef_a * own_ref[:, part].astype(f32) + coef_b * found_ref[:, part]
        begun_ref[:, part] = value + coef_c * dot(lhs[...], rhs[:, part])


def close_kernel(few, lhs_ref, via_y, via_right, via_left, across_far, begun_ref, out_ref, lhs, rhs, begun, sems):
    rows, cols = out_ref.shape
    half, more = rows // 2, rows - few
    pieces = [
        (via_right.at[pl.ds(0, half)], 0),
        (via_left.at[pl.ds(0, half)], half),
        (via_right.at[pl.ds(half, few)], rows),
        (via_y.at[pl.ds(0, more)], rows + few),
        (via_left.at[pl.ds(half, few)], 2 * rows),
        (via_y.at[pl.ds(more, more)], 2 * rows + few),
        (across_far, 3 * rows),
    ]
    copies = [pltpu.make_async_copy(lhs_ref, lhs, sems.at[7])]
    for at, (source, place) in enumerate(pieces):
        copies.append(pltpu.make_async_copy(source, rhs.at[pl.ds(place, source.shape[0])], sems.at[at]))
    copies.append(pltpu.make_async_copy(begun_ref, begun, sems.at[8]))
    for copy in copies:
        copy.start()
    parts = [pl.ds(start, min(256, cols - start)) for start in range(0, cols, 256)]
    for copy in copies:
        copy.wait()
    scale = float(COLS) ** 0.5
    for part in parts:
        value = begun[:, part] + coef_c * dot(lhs[...], rhs[:, part])
        out_ref[:, part] = (scale * value).astype(bf16)


def open_product(lhs, blocks, found, own):
    rows, cols = own.shape
    vmem = pl.BlockSpec(memory_space=pltpu.VMEM)
    return pl.pallas_call(
        open_kernel,
        out_shape=jax.ShapeDtypeStruct((rows, cols), f32),
        in_specs=[pl.BlockSpec(memory_space=pl.ANY)] * 5 + [vmem, vmem],
        out_specs=vmem,
        scratch_shapes=[
            pltpu.VMEM(lhs.shape, bf16),
            pltpu.VMEM((4 * rows, cols), bf16),
            pltpu.SemaphoreType.DMA((5,)),
        ],
        compiler_params=pltpu.CompilerParams(vmem_limit_bytes=12 * 2**20),
        cost_estimate=pl.CostEstimate(flops=8 * rows * rows * cols, bytes_accessed=6 * 2**20, transcendentals=0),
    )(lhs, *blocks, found, own)


def close_product(few, lhs, blocks, begun):
    rows, cols = begun.shape
    return pl.pallas_call(
        functools.partial(close_kernel, few),
        out_shape=jax.ShapeDtypeStruct((rows, cols), bf16),
        in_specs=[pl.BlockSpec(memory_space=pltpu.HBM)] * 6,
        out_specs=pl.BlockSpec(memory_space=pltpu.VMEM),
        scratch_shapes=[
            pltpu.VMEM(lhs.shape, bf16),
            pltpu.VMEM((4 * rows, cols), bf16),
            pltpu.VMEM((rows, cols), f32),
            pltpu.SemaphoreType.DMA((9,)),
        ],
        compiler_params=pltpu.CompilerParams(vmem_limit_bytes=12 * 2**20),
        cost_estimate=pl.CostEstimate(flops=8 * rows * rows * cols, bytes_accessed=6 * 2**20, transcendentals=0),
    )(lhs, *blocks, begun)


def local(own):
    rows = own.shape[0]
    narrow_pos = lax.axis_index("narrow")
    core = narrow_pos % 2
    z_pos = narrow_pos // 4
    unit = rows // Z_SIZE

    right, left, across = gather_first(own)
    half_rows = rows // 2
    far = cat(from_x(right[:half_rows], 1), from_x(left[half_rows:], -1))
    same = cat(own, right, left, far)
    x_right, x_left, x_far = right, left, far

    both = cat(own, across)
    order = ((0, 4), (0, 3), (1, 3), (0, 2), (1, 2), (0, 1), (1, 1), (1, 0))

    def units_of(core):
        def place(which, step):
            owner = jnp.where(core == 0, which, 1 - which)
            return owner * rows + ((z_pos + step * (1 - 2 * core)) % 8) * unit

        return cat(*[lax.dynamic_slice_in_dim(both, place(*at), unit, 0) for at in order])

    given = rows_of(units_of(1 - core), same).astype(bf16)
    kept = lax.optimization_barrier(rows_of(units_of(core), same))
    summed = kept + from_core(given).astype(f32)

    def units(start, stop):
        return summed[start * unit : stop * unit]

    passed = along_z(units(1, 3).astype(bf16), 1).astype(f32) + jnp.pad(along_z(units(0, 1).astype(bf16), 2).astype(f32), ((0, unit), (0, 0)))
    two, one, late_across, late_far = lax.optimization_barrier(
        ((units(3, 5) + passed).astype(bf16), units(5, 7).astype(bf16), across, far)
    )
    passed = along_z(two, 2).astype(f32) + along_z(one, 1).astype(f32)
    total = passed + jnp.pad(units(7, 8), ((unit, 0), (0, 0)))
    others = (from_x(late_across, 1), from_x(late_across, -1), from_y(late_far))
    total, other_right, other_left, other_far = lax.optimization_barrier((total, *others))

    width = 2 * rows
    total = total.astype(bf16)
    kept_part = jnp.where(core == 0, total[:unit], total[unit:])
    given_part = jnp.where(core == 0, total[unit:], total[:unit])
    gram_same = kept_part.astype(f32) + from_y_hi(kept_part).astype(f32)
    gram_other = from_y(given_part).astype(f32) + from_y_both(given_part).astype(f32)
    gram = jnp.stack([gram_same, gram_other])
    given = lax.dynamic_slice_in_dim(gram, (1 - core) * width, width, 2).astype(bf16)
    gram = (lax.dynamic_slice_in_dim(gram, core * width, width, 2) + from_core(given).astype(f32)).astype(bf16)

    up1, down1 = from_z(gram, 1), from_z(gram, -1)
    up2, down2 = from_z(gram, 2), from_z(gram, -2)
    up3, down3 = from_z(up2, 1), from_z(down2, -1)
    up4, down4 = from_z(up2[:1], 2), from_z(down2[1:], -2)
    block = jnp.zeros((2, rows, width), bf16)
    pieces = ((0, gram), (1, up1), (-1, down1), (2, up2), (-2, down2), (3, up3), (-3, down3), (4, cat(up4, down4)))
    for step, piece in pieces:
        block = lax.dynamic_update_slice_in_dim(block, piece, ((z_pos + step) % 8) * unit, 1)
    got = from_core(block)
    x_blocks = (own, x_right, x_left, x_far, across, other_right, other_left, other_far)
    found, sent = found_part(got, x_blocks, found_part(block, x_blocks))
    right, left, across = gather_first(sent)
    half, few = rows // 2, rows // 4
    via_y = from_y(cat(right[few:], left[few:]))
    via_right = from_x(cat(right[:half], across[:few]), 1)
    via_left = from_x(cat(left[half:], across[:few]), -1)
    across_far = from_x(across, 2)
    block, got, _ = lax.optimization_barrier((block, got, right))
    low = jnp.where(core == 0, block, got)
    high = jnp.where(core == 0, got, block)
    early = cat(low[0], high[0, :, :rows], low[1, :, :rows], axis=1)
    late = cat(high[0, :, rows:], low[1, :, rows:], high[1], axis=1)
    begun = open_product(early, (sent, right, left, across), found, own)
    return close_product(few, late, (via_y, via_right, via_left, across_far), begun)


def solution(mesh):
    return jax.shard_map(
        local,
        mesh=mesh,
        in_specs=(P("wide", "narrow"),),
        out_specs=P("wide", "narrow"),
        check_vma=False,
    )
```

```python
import functools

import jax
import jax.numpy as jnp
from jax import lax
from jax.experimental import pallas as pl
from jax.experimental.pallas import tpu as pltpu
from jax.sharding import PartitionSpec as P

COLS = 18432

coef_a = 3.4445
coef_b = -4.775
coef_c = 2.0315

Z_SIZE = 8
f32, bf16 = jnp.float32, jnp.bfloat16


def from_x(value, step):
    pairs = [(y * 4 + (x + step) % 4, y * 4 + x) for y in range(2) for x in range(4)]
    return lax.ppermute(value, "wide", pairs)


def from_y(value):
    return lax.ppermute(value, "wide", [(w, (w + 4) % 8) for w in range(8)])


def from_z(value, step):
    pairs = [(((z + step) % 8) * 4 + r, z * 4 + r) for z in range(8) for r in range(4)]
    return lax.ppermute(value, "narrow", pairs)


def from_y_first(value):
    pairs = [((w, n ^ 2) if n % 2 == 0 else ((w + 4) % 8, n), (w, n)) for w in range(8) for n in range(32)]
    return lax.ppermute(value, ("wide", "narrow"), [(a * 32 + b, c * 32 + d) for (a, b), (c, d) in pairs])


def from_y_second(value):
    pairs = [(((w + 4) % 8, n ^ 2), (w, n)) for w in range(8) for n in range(1, 32, 2)]
    return lax.ppermute(value, ("wide", "narrow"), [(a * 32 + b, c * 32 + d) for (a, b), (c, d) in pairs])


def from_core(value):
    return lax.ppermute(value, "narrow", [(n, n ^ 1) for n in range(32)])


def rows_of(left, right):
    return lax.dot_general(left, right, (((1,), (1,)), ((), ())), preferred_element_type=f32)


def dot(left, right):
    return jnp.dot(left, right, preferred_element_type=f32)


def cat(*parts, axis=0):
    return jnp.concatenate(parts, axis=axis)


def gather_first(own):
    return from_x(own, 1), from_x(own, -1), from_y(own)


def along_z(value, hops):
    pairs = [(z * 4 + r, (z + hops * (1 - 2 * (r % 2))) % 8 * 4 + r) for z in range(8) for r in range(4)]
    return lax.ppermute(value, "narrow", pairs)


def found_kernel(mine, *refs):
    block_ref, *x_refs = refs[:9]
    if mine:
        found_ref, lhs, rhs, sems = refs[9:]
    else:
        before_ref, found_ref, sent_ref, lhs, rhs, sems = refs[9:]
    rows, cols = x_refs[0].shape
    core = lax.rem(lax.axis_index("narrow"), 2)

    def run(picks):
        copies = [pltpu.make_async_copy(block_ref, lhs, sems.at[4])]
        for at, pick in enumerate(picks):
            copies.append(pltpu.make_async_copy(x_refs[pick], rhs.at[pl.ds(at * rows, rows)], sems.at[at]))
        for copy in copies:
            copy.start()

    @pl.when(core == (0 if mine else 1))
    def _():
        run((0, 1, 2, 3))

    @pl.when(core == (1 if mine else 0))
    def _():
        run((4, 5, 6, 7))

    def wait(at):
        pltpu.make_async_copy(x_refs[at], rhs.at[pl.ds(at * rows, rows)], sems.at[at]).wait()

    parts = [pl.ds(start, min(256, cols - start)) for start in range(0, cols, 256)]
    pltpu.make_async_copy(block_ref, lhs, sems.at[4]).wait()
    wait(0)
    wait(1)
    for part in parts:
        found_ref[:, part] = dot(lhs[:, : 2 * rows], rhs[: 2 * rows, part])
    wait(2)
    wait(3)
    for part in parts:
        value = found_ref[:, part] + dot(lhs[:, 2 * rows :], rhs[2 * rows :, part])
        if not mine:
            value = before_ref[:, part] + value
            sent_ref[:, part] = value.astype(bf16)
        found_ref[:, part] = value


def found_part(block, x_blocks, before=None):
    rows, cols = x_blocks[0].shape
    mine = before is None
    found = jax.ShapeDtypeStruct((rows, cols), f32)
    vmem = pl.BlockSpec(memory_space=pltpu.VMEM)
    return pl.pallas_call(
        functools.partial(found_kernel, mine),
        out_shape=found if mine else (found, jax.ShapeDtypeStruct((rows, cols), bf16)),
        in_specs=[pl.BlockSpec(memory_space=pl.ANY)] * 9 + ([] if mine else [vmem]),
        out_specs=vmem if mine else (vmem, vmem),
        scratch_shapes=[
            pltpu.VMEM(block.shape, bf16),
            pltpu.VMEM((4 * rows, cols), bf16),
            pltpu.SemaphoreType.DMA((5,)),
        ],
        compiler_params=pltpu.CompilerParams(vmem_limit_bytes=9 * 2**20),
        cost_estimate=pl.CostEstimate(flops=8 * rows * rows * cols, bytes_accessed=6 * 2**20, transcendentals=0),
    )(block, *x_blocks, *([] if mine else [before]))


def open_kernel(block_ref, got_ref, own_y, right, found_ref, own_ref, begun_ref, lhs, rhs, sems):
    rows, cols = own_ref.shape
    core = lax.rem(lax.axis_index("narrow"), 2)
    copies = [
        pltpu.make_async_copy(block_ref, lhs.at[core], sems.at[0]),
        pltpu.make_async_copy(got_ref, lhs.at[1 - core], sems.at[1]),
        pltpu.make_async_copy(own_y, rhs.at[pl.ds(0, rows)], sems.at[2]),
        pltpu.make_async_copy(right, rhs.at[pl.ds(rows, rows)], sems.at[3]),
    ]
    for copy in copies:
        copy.start()
    for copy in copies:
        copy.wait()
    for start in range(0, cols, 256):
        part = pl.ds(start, min(256, cols - start))
        value = coef_a * own_ref[:, part].astype(f32) + coef_b * found_ref[:, part]
        begun_ref[:, part] = value + coef_c * dot(lhs[0, :, : 2 * rows], rhs[:, part])


def close_kernel(few, block_ref, got_ref, *refs):
    left, across, via_y, via_right, via_left, across_far = refs[:6]
    begun_ref, out_ref, lhs, rhs, total, sems = refs[6:]
    rows, cols = out_ref.shape
    half, more = rows // 2, rows - few
    core = lax.rem(lax.axis_index("narrow"), 2)

    pieces = [
        (block_ref, lhs.at[core]),
        (got_ref, lhs.at[1 - core]),
        (left, 0),
        (via_right.at[pl.ds(0, half)], rows),
        (via_left.at[pl.ds(0, half)], rows + half),
        (across, 2 * rows),
        (via_right.at[pl.ds(half, few)], 3 * rows),
        (via_y.at[pl.ds(0, more)], 3 * rows + few),
        (via_left.at[pl.ds(half, few)], 4 * rows),
        (via_y.at[pl.ds(more, more)], 4 * rows + few),
        (across_far, 5 * rows),
    ]
    copies = []
    for at, (source, place) in enumerate(pieces):
        target = rhs.at[pl.ds(place, source.shape[0])] if isinstance(place, int) else place
        copies.append(pltpu.make_async_copy(source, target, sems.at[at]))
    for copy in copies:
        copy.start()
    parts = [pl.ds(start, min(256, cols - start)) for start in range(0, cols, 256)]
    width = 2 * rows
    for copy in copies[:5]:
        copy.wait()
    for part in parts:
        total[:, part] = dot(lhs[0, :, width:], rhs[:width, part])
    for copy in copies[5:]:
        copy.wait()
    scale = float(COLS) ** 0.5
    for part in parts:
        value = dot(lhs[1], rhs[width:, part])
        out_ref[:, part] = (scale * (begun_ref[:, part] + coef_c * (total[:, part] + value))).astype(bf16)


def open_product(block, got, own_y, right, found, own):
    rows, cols = own.shape
    vmem = pl.BlockSpec(memory_space=pltpu.VMEM)
    return pl.pallas_call(
        open_kernel,
        out_shape=jax.ShapeDtypeStruct((rows, cols), f32),
        in_specs=[pl.BlockSpec(memory_space=pl.ANY)] * 4 + [vmem, vmem],
        out_specs=vmem,
        scratch_shapes=[
            pltpu.VMEM((2, *block.shape), bf16),
            pltpu.VMEM((2 * rows, cols), bf16),
            pltpu.SemaphoreType.DMA((4,)),
        ],
        compiler_params=pltpu.CompilerParams(vmem_limit_bytes=12 * 2**20),
        cost_estimate=pl.CostEstimate(flops=4 * rows * rows * cols, bytes_accessed=5 * 2**20, transcendentals=0),
    )(block, got, own_y, right, found, own)


def close_product(few, block, got, blocks, begun):
    rows, cols = begun.shape
    vmem = pl.BlockSpec(memory_space=pltpu.VMEM)
    return pl.pallas_call(
        functools.partial(close_kernel, few),
        out_shape=jax.ShapeDtypeStruct((rows, cols), bf16),
        in_specs=[pl.BlockSpec(memory_space=pltpu.HBM)] * 8 + [vmem],
        out_specs=vmem,
        scratch_shapes=[
            pltpu.VMEM((2, *block.shape), bf16),
            pltpu.VMEM((6 * rows, cols), bf16),
            pltpu.VMEM((rows, cols), f32),
            pltpu.SemaphoreType.DMA((11,)),
        ],
        compiler_params=pltpu.CompilerParams(vmem_limit_bytes=16 * 2**20),
        cost_estimate=pl.CostEstimate(flops=12 * rows * rows * cols, bytes_accessed=9 * 2**20, transcendentals=0),
    )(block, got, *blocks, begun)


def local(own):
    rows = own.shape[0]
    narrow_pos = lax.axis_index("narrow")
    core = narrow_pos % 2
    z_pos = narrow_pos // 4
    unit = rows // Z_SIZE

    right, left, across = gather_first(own)
    half_rows = rows // 2
    far = cat(from_x(right[:half_rows], 1), from_x(left[half_rows:], -1))
    same = cat(own, right, left, far)
    x_right, x_left, x_far = right, left, far

    both = cat(own, across)
    order = ((0, 4), (0, 3), (1, 3), (0, 2), (1, 2), (0, 1), (1, 1), (1, 0))

    def units_of(core):
        def place(which, step):
            owner = jnp.where(core == 0, which, 1 - which)
            return owner * rows + ((z_pos + step * (1 - 2 * core)) % 8) * unit

        return cat(*[lax.dynamic_slice_in_dim(both, place(*at), unit, 0) for at in order])

    given = rows_of(units_of(1 - core), same).astype(bf16)
    kept = lax.optimization_barrier(rows_of(units_of(core), same))
    summed = kept + from_core(given).astype(f32)

    def units(start, stop):
        return summed[start * unit : stop * unit]

    passed = along_z(units(1, 3).astype(bf16), 1).astype(f32) + jnp.pad(along_z(units(0, 1).astype(bf16), 2).astype(f32), ((0, unit), (0, 0)))
    two, one, late_across, late_far = lax.optimization_barrier(
        ((units(3, 5) + passed).astype(bf16), units(5, 7).astype(bf16), across, far)
    )
    passed = along_z(two, 2).astype(f32) + along_z(one, 1).astype(f32)
    total = passed + jnp.pad(units(7, 8), ((unit, 0), (0, 0)))
    others = (from_x(late_across, 1), from_x(late_across, -1), from_y(late_far))
    total, other_right, other_left, other_far = lax.optimization_barrier((total, *others))

    total = total[:unit] + from_core(total[unit:].astype(bf16)).astype(f32)
    total = total.astype(bf16)

    first, second = from_y_first(total).astype(f32), from_y_second(total).astype(f32)
    gram = (jnp.where(core == 0, total.astype(f32), second) + first).astype(bf16)

    up1, down1 = from_z(gram, 1), from_z(gram, -1)
    up2, down2 = from_z(gram, 2), from_z(gram, -2)
    up3, down3 = from_z(up2, 1), from_z(down2, -1)
    four = along_z(jnp.where(core == 0, up2, down2), -2)
    block = jnp.zeros((rows, 4 * rows), bf16)
    pieces = ((0, gram), (1, up1), (-1, down1), (2, up2), (-2, down2), (3, up3), (-3, down3), (4, four))
    for step, piece in pieces:
        block = lax.dynamic_update_slice_in_dim(block, piece, ((z_pos + step) % 8) * unit, 0)
    got = from_core(block)

    x_blocks = (own, x_right, x_left, x_far, across, other_right, other_left, other_far)
    found, sent = found_part(got, x_blocks, found_part(block, x_blocks))
    right, left, across = gather_first(sent)
    half, few = rows // 2, rows // 4
    via_y = from_y(cat(right[few:], left[few:]))
    via_right = from_x(cat(right[:half], across[:few]), 1)
    via_left = from_x(cat(left[half:], across[:few]), -1)
    across_far = from_x(across, 2)
    begun = open_product(block, got, sent, right, found, own)
    return close_product(few, block, got, (left, across, via_y, via_right, via_left, across_far), begun)


def solution(mesh):
    return jax.shard_map(
        local,
        mesh=mesh,
        in_specs=(P("wide", "narrow"),),
        out_specs=P("wide", "narrow"),
        check_vma=False,
    )
```

```python
import functools

import jax
import jax.numpy as jnp
from jax import lax
from jax.experimental import pallas as pl
from jax.experimental.pallas import tpu as pltpu
from jax.sharding import PartitionSpec as P

COLS = 18432

coef_a = 3.4445
coef_b = -4.775
coef_c = 2.0315

Z_SIZE = 8
f32, bf16 = jnp.float32, jnp.bfloat16


def from_x(value, step):
    pairs = [(y * 4 + (x + step) % 4, y * 4 + x) for y in range(2) for x in range(4)]
    return lax.ppermute(value, "wide", pairs)


def from_y(value):
    return lax.ppermute(value, "wide", [(w, (w + 4) % 8) for w in range(8)])


def from_z(value, step):
    pairs = [(((z + step) % 8) * 4 + r, z * 4 + r) for z in range(8) for r in range(4)]
    return lax.ppermute(value, "narrow", pairs)


def from_y_hi(value):
    return lax.ppermute(value, "narrow", [(n, n ^ 2) for n in range(32)])


def from_y_both(value):
    pairs = [((w, n), ((w + 4) % 8, n ^ 2)) for w in range(8) for n in range(32)]
    return lax.ppermute(value, ("wide", "narrow"), [(a * 32 + b, c * 32 + d) for (a, b), (c, d) in pairs])


def from_core(value):
    return lax.ppermute(value, "narrow", [(n, n ^ 1) for n in range(32)])


def rows_of(left, right):
    return lax.dot_general(left, right, (((1,), (1,)), ((), ())), preferred_element_type=f32)


def dot(left, right):
    return jnp.dot(left, right, preferred_element_type=f32)


def cat(*parts, axis=0):
    return jnp.concatenate(parts, axis=axis)


def gather_first(own):
    return from_x(own, 1), from_x(own, -1), from_y(own)


def along_z(value, hops):
    pairs = [(z * 4 + r, (z + hops * (1 - 2 * (r % 2))) % 8 * 4 + r) for z in range(8) for r in range(4)]
    return lax.ppermute(value, "narrow", pairs)


def found_kernel(mine, *refs):
    block_ref, *x_refs = refs[:9]
    if mine:
        found_ref, lhs, rhs, sems = refs[9:]
    else:
        before_ref, found_ref, sent_ref, lhs, rhs, sems = refs[9:]
    rows, cols = x_refs[0].shape
    core = lax.rem(lax.axis_index("narrow"), 2)

    def run(picks):
        copies = [pltpu.make_async_copy(block_ref, lhs, sems.at[4])]
        for at, pick in enumerate(picks):
            copies.append(pltpu.make_async_copy(x_refs[pick], rhs.at[pl.ds(at * rows, rows)], sems.at[at]))
        for copy in copies:
            copy.start()

    @pl.when(core == (0 if mine else 1))
    def _():
        run((0, 1, 4, 5))

    @pl.when(core == (1 if mine else 0))
    def _():
        run((2, 3, 6, 7))

    def wait(at):
        pltpu.make_async_copy(x_refs[at], rhs.at[pl.ds(at * rows, rows)], sems.at[at]).wait()

    parts = [pl.ds(start, min(256, cols - start)) for start in range(0, cols, 256)]
    pltpu.make_async_copy(block_ref, lhs, sems.at[4]).wait()
    wait(0)
    wait(1)
    for part in parts:
        found_ref[:, part] = dot(lhs[0], rhs[: 2 * rows, part])
    wait(2)
    wait(3)
    for part in parts:
        value = found_ref[:, part] + dot(lhs[1], rhs[2 * rows :, part])
        if not mine:
            value = before_ref[:, part] + value
            sent_ref[:, part] = value.astype(bf16)
        found_ref[:, part] = value


def found_part(block, x_blocks, before=None):
    rows, cols = x_blocks[0].shape
    mine = before is None
    found = jax.ShapeDtypeStruct((rows, cols), f32)
    vmem = pl.BlockSpec(memory_space=pltpu.VMEM)
    return pl.pallas_call(
        functools.partial(found_kernel, mine),
        out_shape=found if mine else (found, jax.ShapeDtypeStruct((rows, cols), bf16)),
        in_specs=[pl.BlockSpec(memory_space=pl.ANY)] * 9 + ([] if mine else [vmem]),
        out_specs=vmem if mine else (vmem, vmem),
        scratch_shapes=[
            pltpu.VMEM(block.shape, bf16),
            pltpu.VMEM((4 * rows, cols), bf16),
            pltpu.SemaphoreType.DMA((5,)),
        ],
        compiler_params=pltpu.CompilerParams(vmem_limit_bytes=9 * 2**20),
        cost_estimate=pl.CostEstimate(flops=8 * rows * rows * cols, bytes_accessed=6 * 2**20, transcendentals=0),
    )(block, *x_blocks, *([] if mine else [before]))


def open_kernel(block_ref, got_ref, own_y, right, found_ref, own_ref, begun_ref, lhs, rhs, sems):
    rows, cols = own_ref.shape
    core = lax.rem(lax.axis_index("narrow"), 2)
    copies = [
        pltpu.make_async_copy(block_ref.at[0], lhs.at[core], sems.at[0]),
        pltpu.make_async_copy(got_ref.at[0], lhs.at[1 - core], sems.at[1]),
        pltpu.make_async_copy(own_y, rhs.at[pl.ds(0, rows)], sems.at[2]),
        pltpu.make_async_copy(right, rhs.at[pl.ds(rows, rows)], sems.at[3]),
    ]
    for copy in copies:
        copy.start()
    for copy in copies:
        copy.wait()
    for start in range(0, cols, 256):
        part = pl.ds(start, min(256, cols - start))
        value = coef_a * own_ref[:, part].astype(f32) + coef_b * found_ref[:, part]
        begun_ref[:, part] = value + coef_c * dot(lhs[0], rhs[:, part])


def close_kernel(few, block_ref, got_ref, *refs):
    left, across, via_y, via_right, via_left, across_far = refs[:6]
    begun_ref, out_ref, lhs, rhs, total, begun, sems = refs[6:]
    rows, cols = out_ref.shape
    half, more = rows // 2, rows - few
    core = lax.rem(lax.axis_index("narrow"), 2)

    pieces = [
        (block_ref, lhs.at[core]),
        (got_ref, lhs.at[1 - core]),
        (left, 0),
        (via_right.at[pl.ds(0, half)], rows),
        (via_left.at[pl.ds(0, half)], rows + half),
        (across, 2 * rows),
        (via_right.at[pl.ds(half, few)], 3 * rows),
        (via_y.at[pl.ds(0, more)], 3 * rows + few),
        (via_left.at[pl.ds(half, few)], 4 * rows),
        (via_y.at[pl.ds(more, more)], 4 * rows + few),
        (across_far, 5 * rows),
    ]
    copies = []
    for at, (source, place) in enumerate(pieces):
        target = rhs.at[pl.ds(place, source.shape[0])] if isinstance(place, int) else place
        copies.append(pltpu.make_async_copy(source, target, sems.at[at]))
    copies.append(pltpu.make_async_copy(begun_ref, begun, sems.at[11]))
    for copy in copies:
        copy.start()
    parts = [pl.ds(start, min(256, cols - start)) for start in range(0, cols, 256)]
    width = 2 * rows
    for copy in copies[:5]:
        copy.wait()
    for part in parts:
        total[:, part] = dot(lhs[1, 0], rhs[:width, part])
    for copy in copies[5:]:
        copy.wait()
    scale = float(COLS) ** 0.5
    for part in parts:
        value = dot(lhs[0, 1], rhs[width : 2 * width, part]) + dot(lhs[1, 1], rhs[2 * width :, part])
        out_ref[:, part] = (scale * (begun[:, part] + coef_c * (total[:, part] + value))).astype(bf16)


def open_product(block, got, own_y, right, found, own):
    rows, cols = own.shape
    vmem = pl.BlockSpec(memory_space=pltpu.VMEM)
    return pl.pallas_call(
        open_kernel,
        out_shape=jax.ShapeDtypeStruct((rows, cols), f32),
        in_specs=[pl.BlockSpec(memory_space=pl.ANY)] * 4 + [vmem, vmem],
        out_specs=vmem,
        scratch_shapes=[
            pltpu.VMEM(block.shape, bf16),
            pltpu.VMEM((2 * rows, cols), bf16),
            pltpu.SemaphoreType.DMA((4,)),
        ],
        compiler_params=pltpu.CompilerParams(vmem_limit_bytes=12 * 2**20),
        cost_estimate=pl.CostEstimate(flops=4 * rows * rows * cols, bytes_accessed=5 * 2**20, transcendentals=0),
    )(block, got, own_y, right, found, own)


def close_product(few, block, got, blocks, begun):
    rows, cols = begun.shape
    vmem = pl.BlockSpec(memory_space=pltpu.VMEM)
    return pl.pallas_call(
        functools.partial(close_kernel, few),
        out_shape=jax.ShapeDtypeStruct((rows, cols), bf16),
        in_specs=[pl.BlockSpec(memory_space=pltpu.HBM)] * 9,
        out_specs=vmem,
        scratch_shapes=[
            pltpu.VMEM((2, *block.shape), bf16),
            pltpu.VMEM((6 * rows, cols), bf16),
            pltpu.VMEM((rows, cols), f32),
            pltpu.VMEM((rows, cols), f32),
            pltpu.SemaphoreType.DMA((12,)),
        ],
        compiler_params=pltpu.CompilerParams(vmem_limit_bytes=16 * 2**20),
        cost_estimate=pl.CostEstimate(flops=12 * rows * rows * cols, bytes_accessed=9 * 2**20, transcendentals=0),
    )(block, got, *blocks, begun)


def local(own):
    rows = own.shape[0]
    narrow_pos = lax.axis_index("narrow")
    core = narrow_pos % 2
    z_pos = narrow_pos // 4
    unit = rows // Z_SIZE

    right, left, across = gather_first(own)
    half_rows = rows // 2
    far = cat(from_x(right[:half_rows], 1), from_x(left[half_rows:], -1))
    same = cat(own, right, left, far)
    x_right, x_left, x_far = right, left, far

    both = cat(own, across)
    order = ((0, 4), (0, 3), (1, 3), (0, 2), (1, 2), (0, 1), (1, 1), (1, 0))

    def units_of(core):
        def place(which, step):
            owner = jnp.where(core == 0, which, 1 - which)
            return owner * rows + ((z_pos + step * (1 - 2 * core)) % 8) * unit

        return cat(*[lax.dynamic_slice_in_dim(both, place(*at), unit, 0) for at in order])

    given = rows_of(units_of(1 - core), same).astype(bf16)
    kept = lax.optimization_barrier(rows_of(units_of(core), same))
    summed = kept + from_core(given).astype(f32)

    def units(start, stop):
        return summed[start * unit : stop * unit]

    passed = along_z(units(1, 3).astype(bf16), 1).astype(f32) + jnp.pad(along_z(units(0, 1).astype(bf16), 2).astype(f32), ((0, unit), (0, 0)))
    two, one, late_across, late_far = lax.optimization_barrier(
        ((units(3, 5) + passed).astype(bf16), units(5, 7).astype(bf16), across, far)
    )
    passed = along_z(two, 2).astype(f32) + along_z(one, 1).astype(f32)
    total = passed + jnp.pad(units(7, 8), ((unit, 0), (0, 0)))
    others = (from_x(late_across, 1), from_x(late_across, -1), from_y(late_far))
    total, other_right, other_left, other_far = lax.optimization_barrier((total, *others))

    width = 2 * rows
    total = total.reshape(2, unit, 2 * width)
    given = from_core(lax.dynamic_slice_in_dim(total, (1 - core) * width, width, 2).astype(bf16))
    total = lax.dynamic_slice_in_dim(total, core * width, width, 2) + cat(given[1:], given[:1]).astype(f32)
    total = total.astype(bf16)
    kept = jnp.where(core == 0, total[0], total[1])
    given = jnp.where(core == 0, total[1], total[0])

    gram_same = kept.astype(f32) + from_y_hi(kept).astype(f32)
    gram_other = from_y(given).astype(f32) + from_y_both(given).astype(f32)
    gram = jnp.stack([gram_same, gram_other]).astype(bf16)

    up1, down1 = from_z(gram, 1), from_z(gram, -1)
    up2, down2 = from_z(gram, 2), from_z(gram, -2)
    up3, down3 = from_z(up2, 1), from_z(down2, -1)
    four = along_z(jnp.where(core == 0, up2, down2), -2)
    block = jnp.zeros((2, rows, width), bf16)
    pieces = ((0, gram), (1, up1), (-1, down1), (2, up2), (-2, down2), (3, up3), (-3, down3), (4, four))
    for step, piece in pieces:
        block = lax.dynamic_update_slice_in_dim(block, piece, ((z_pos + step) % 8) * unit, 1)
    got = from_core(block)
    x_blocks = (own, x_right, x_left, x_far, across, other_right, other_left, other_far)
    found, sent = found_part(got, x_blocks, found_part(block, x_blocks))
    right, left, across = gather_first(sent)
    half, few = rows // 2, rows // 4
    via_y = from_y(cat(right[few:], left[few:]))
    via_right = from_x(cat(right[:half], across[:few]), 1)
    via_left = from_x(cat(left[half:], across[:few]), -1)
    across_far = from_x(across, 2)
    begun = open_product(block, got, sent, right, found, own)
    return close_product(few, block, got, (left, across, via_y, via_right, via_left, across_far), begun)


def solution(mesh):
    return jax.shard_map(
        local,
        mesh=mesh,
        in_specs=(P("wide", "narrow"),),
        out_specs=P("wide", "narrow"),
        check_vma=False,
    )
```

```python
import functools

import jax
import jax.numpy as jnp
from jax import lax
from jax.experimental import pallas as pl
from jax.experimental.pallas import tpu as pltpu
from jax.sharding import PartitionSpec as P

COLS = 18432

coef_a = 3.4445
coef_b = -4.775
coef_c = 2.0315

Z_SIZE = 8
f32, bf16 = jnp.float32, jnp.bfloat16


def from_x(value, step):
    pairs = [(y * 4 + (x + step) % 4, y * 4 + x) for y in range(2) for x in range(4)]
    return lax.ppermute(value, "wide", pairs)


def from_y(value):
    return lax.ppermute(value, "wide", [(w, (w + 4) % 8) for w in range(8)])


def from_z(value, step):
    pairs = [(((z + step) % 8) * 4 + r, z * 4 + r) for z in range(8) for r in range(4)]
    return lax.ppermute(value, "narrow", pairs)


def from_y_hi(value):
    return lax.ppermute(value, "narrow", [(n, n ^ 2) for n in range(32)])


def from_y_both(value):
    pairs = [((w, n), ((w + 4) % 8, n ^ 2)) for w in range(8) for n in range(32)]
    return lax.ppermute(value, ("wide", "narrow"), [(a * 32 + b, c * 32 + d) for (a, b), (c, d) in pairs])


def from_core(value):
    return lax.ppermute(value, "narrow", [(n, n ^ 1) for n in range(32)])


def rows_of(left, right):
    return lax.dot_general(left, right, (((1,), (1,)), ((), ())), preferred_element_type=f32)


def dot(left, right):
    return jnp.dot(left, right, preferred_element_type=f32)


def cat(*parts, axis=0):
    return jnp.concatenate(parts, axis=axis)


def gather_first(own):
    return from_x(own, 1), from_x(own, -1), from_y(own)


def along_z(value, hops):
    pairs = [(z * 4 + r, (z + hops * (1 - 2 * (r % 2))) % 8 * 4 + r) for z in range(8) for r in range(4)]
    return lax.ppermute(value, "narrow", pairs)


def found_kernel(mine, *refs):
    block_ref, *x_refs = refs[:9]
    if mine:
        found_ref, lhs, rhs, sems = refs[9:]
    else:
        before_ref, found_ref, sent_ref, lhs, rhs, sems = refs[9:]
    rows, cols = x_refs[0].shape
    core = lax.rem(lax.axis_index("narrow"), 2)

    def run(picks):
        copies = [pltpu.make_async_copy(block_ref, lhs, sems.at[4])]
        for at, pick in enumerate(picks):
            copies.append(pltpu.make_async_copy(x_refs[pick], rhs.at[pl.ds(at * rows, rows)], sems.at[at]))
        for copy in copies:
            copy.start()

    @pl.when(core == (0 if mine else 1))
    def _():
        run((0, 1, 4, 5))

    @pl.when(core == (1 if mine else 0))
    def _():
        run((2, 3, 6, 7))

    def wait(at):
        pltpu.make_async_copy(x_refs[at], rhs.at[pl.ds(at * rows, rows)], sems.at[at]).wait()

    parts = [pl.ds(start, min(256, cols - start)) for start in range(0, cols, 256)]
    pltpu.make_async_copy(block_ref, lhs, sems.at[4]).wait()
    wait(0)
    wait(1)
    for part in parts:
        found_ref[:, part] = dot(lhs[0], rhs[: 2 * rows, part])
    wait(2)
    wait(3)
    for part in parts:
        value = found_ref[:, part] + dot(lhs[1], rhs[2 * rows :, part])
        if not mine:
            value = before_ref[:, part] + value
            sent_ref[:, part] = value.astype(bf16)
        found_ref[:, part] = value


def found_part(block, x_blocks, before=None):
    rows, cols = x_blocks[0].shape
    mine = before is None
    found = jax.ShapeDtypeStruct((rows, cols), f32)
    vmem = pl.BlockSpec(memory_space=pltpu.VMEM)
    return pl.pallas_call(
        functools.partial(found_kernel, mine),
        out_shape=found if mine else (found, jax.ShapeDtypeStruct((rows, cols), bf16)),
        in_specs=[pl.BlockSpec(memory_space=pl.ANY)] * 9 + ([] if mine else [vmem]),
        out_specs=vmem if mine else (vmem, vmem),
        scratch_shapes=[
            pltpu.VMEM(block.shape, bf16),
            pltpu.VMEM((4 * rows, cols), bf16),
            pltpu.SemaphoreType.DMA((5,)),
        ],
        compiler_params=pltpu.CompilerParams(vmem_limit_bytes=9 * 2**20),
        cost_estimate=pl.CostEstimate(flops=8 * rows * rows * cols, bytes_accessed=6 * 2**20, transcendentals=0),
    )(block, *x_blocks, *([] if mine else [before]))


def open_kernel(block_ref, got_ref, own_y, right, found_ref, own_ref, begun_ref, lhs, rhs, sems):
    rows, cols = own_ref.shape
    core = lax.rem(lax.axis_index("narrow"), 2)
    copies = [
        pltpu.make_async_copy(block_ref.at[0], lhs.at[core], sems.at[0]),
        pltpu.make_async_copy(got_ref.at[0], lhs.at[1 - core], sems.at[1]),
        pltpu.make_async_copy(own_y, rhs.at[pl.ds(0, rows)], sems.at[2]),
        pltpu.make_async_copy(right, rhs.at[pl.ds(rows, rows)], sems.at[3]),
    ]
    for copy in copies:
        copy.start()
    for copy in copies:
        copy.wait()
    for start in range(0, cols, 256):
        part = pl.ds(start, min(256, cols - start))
        value = coef_a * own_ref[:, part].astype(f32) + coef_b * found_ref[:, part]
        begun_ref[:, part] = value + coef_c * dot(lhs[0], rhs[:, part])


def close_kernel(few, block_ref, got_ref, *refs):
    left, across, via_y, via_right, via_left, across_far = refs[:6]
    begun_ref, out_ref, lhs, rhs, total, sems = refs[6:]
    rows, cols = out_ref.shape
    half, more = rows // 2, rows - few
    core = lax.rem(lax.axis_index("narrow"), 2)

    @pl.when(core == 0)
    def _():
        pltpu.make_async_copy(got_ref.at[0], lhs.at[0], sems.at[0]).start()

    @pl.when(core == 1)
    def _():
        pltpu.make_async_copy(block_ref.at[0], lhs.at[0], sems.at[0]).start()

    pieces = [
        (left, 0),
        (via_right.at[pl.ds(0, half)], rows),
        (via_left.at[pl.ds(0, half)], rows + half),
        (block_ref.at[1], lhs.at[1 + core]),
        (got_ref.at[1], lhs.at[2 - core]),
        (across, 2 * rows),
        (via_right.at[pl.ds(half, few)], 3 * rows),
        (via_y.at[pl.ds(0, more)], 3 * rows + few),
        (via_left.at[pl.ds(half, few)], 4 * rows),
        (via_y.at[pl.ds(more, more)], 4 * rows + few),
        (across_far, 5 * rows),
    ]
    copies = []
    for at, (source, place) in enumerate(pieces):
        target = rhs.at[pl.ds(place, source.shape[0])] if isinstance(place, int) else place
        copies.append(pltpu.make_async_copy(source, target, sems.at[1 + at]))
    for copy in copies:
        copy.start()
    parts = [pl.ds(start, min(256, cols - start)) for start in range(0, cols, 256)]
    width = 2 * rows
    pltpu.make_async_copy(block_ref.at[0], lhs.at[0], sems.at[0]).wait()
    for copy in copies[:3]:
        copy.wait()
    for part in parts:
        total[:, part] = dot(lhs[0], rhs[:width, part])
    for copy in copies[3:8]:
        copy.wait()
    for part in parts:
        total[:, part] += dot(lhs[1], rhs[width : 2 * width, part])
    for copy in copies[8:]:
        copy.wait()
    scale = float(COLS) ** 0.5
    for part in parts:
        value = total[:, part] + dot(lhs[2], rhs[2 * width :, part])
        out_ref[:, part] = (scale * (begun_ref[:, part] + coef_c * value)).astype(bf16)


def open_product(block, got, own_y, right, found, own):
    rows, cols = own.shape
    vmem = pl.BlockSpec(memory_space=pltpu.VMEM)
    return pl.pallas_call(
        open_kernel,
        out_shape=jax.ShapeDtypeStruct((rows, cols), f32),
        in_specs=[pl.BlockSpec(memory_space=pl.ANY)] * 4 + [vmem, vmem],
        out_specs=vmem,
        scratch_shapes=[
            pltpu.VMEM(block.shape, bf16),
            pltpu.VMEM((2 * rows, cols), bf16),
            pltpu.SemaphoreType.DMA((4,)),
        ],
        compiler_params=pltpu.CompilerParams(vmem_limit_bytes=12 * 2**20),
        cost_estimate=pl.CostEstimate(flops=4 * rows * rows * cols, bytes_accessed=5 * 2**20, transcendentals=0),
    )(block, got, own_y, right, found, own)


def close_product(few, block, got, blocks, begun):
    rows, cols = begun.shape
    vmem = pl.BlockSpec(memory_space=pltpu.VMEM)
    return pl.pallas_call(
        functools.partial(close_kernel, few),
        out_shape=jax.ShapeDtypeStruct((rows, cols), bf16),
        in_specs=[pl.BlockSpec(memory_space=pltpu.HBM)] * 8 + [vmem],
        out_specs=vmem,
        scratch_shapes=[
            pltpu.VMEM((3, *block.shape[1:]), bf16),
            pltpu.VMEM((6 * rows, cols), bf16),
            pltpu.VMEM((rows, cols), f32),
            pltpu.SemaphoreType.DMA((12,)),
        ],
        compiler_params=pltpu.CompilerParams(vmem_limit_bytes=16 * 2**20),
        cost_estimate=pl.CostEstimate(flops=12 * rows * rows * cols, bytes_accessed=9 * 2**20, transcendentals=0),
    )(block, got, *blocks, begun)


def local(own):
    rows = own.shape[0]
    narrow_pos = lax.axis_index("narrow")
    core = narrow_pos % 2
    z_pos = narrow_pos // 4
    unit = rows // Z_SIZE

    right, left, across = gather_first(own)
    half_rows = rows // 2
    far = cat(from_x(right[:half_rows], 1), from_x(left[half_rows:], -1))
    same = cat(own, right, left, far)
    x_right, x_left, x_far = right, left, far

    both = cat(own, across)
    order = ((0, 4), (0, 3), (1, 3), (0, 2), (1, 2), (0, 1), (1, 1), (1, 0))

    def units_of(core):
        def place(which, step):
            owner = jnp.where(core == 0, which, 1 - which)
            return owner * rows + ((z_pos + step * (1 - 2 * core)) % 8) * unit

        return cat(*[lax.dynamic_slice_in_dim(both, place(*at), unit, 0) for at in order])

    given = rows_of(units_of(1 - core), same).astype(bf16)
    kept = lax.optimization_barrier(rows_of(units_of(core), same))
    summed = kept + from_core(given).astype(f32)

    def units(start, stop):
        return summed[start * unit : stop * unit]

    passed = along_z(units(1, 3).astype(bf16), 1).astype(f32) + jnp.pad(along_z(units(0, 1).astype(bf16), 2).astype(f32), ((0, unit), (0, 0)))
    two, one, late_across, late_far = lax.optimization_barrier(
        ((units(3, 5) + passed).astype(bf16), units(5, 7).astype(bf16), across, far)
    )
    passed = along_z(two, 2).astype(f32) + along_z(one, 1).astype(f32)
    total = passed + jnp.pad(units(7, 8), ((unit, 0), (0, 0)))
    others = (from_x(late_across, 1), from_x(late_across, -1), from_y(late_far))
    total, other_right, other_left, other_far = lax.optimization_barrier((total, *others))

    width = 2 * rows
    total = total.reshape(2, unit, 2 * width)
    given = from_core(lax.dynamic_slice_in_dim(total, (1 - core) * width, width, 2).astype(bf16))
    total = lax.dynamic_slice_in_dim(total, core * width, width, 2) + cat(given[1:], given[:1]).astype(f32)
    total = total.astype(bf16)
    kept = jnp.where(core == 0, total[0], total[1])
    given = jnp.where(core == 0, total[1], total[0])

    gram_same = kept.astype(f32) + from_y_hi(kept).astype(f32)
    gram_other = from_y(given).astype(f32) + from_y_both(given).astype(f32)
    gram = jnp.stack([gram_same, gram_other]).astype(bf16)

    up1, down1 = from_z(gram, 1), from_z(gram, -1)
    up2, down2 = from_z(gram, 2), from_z(gram, -2)
    up3, down3 = from_z(up2, 1), from_z(down2, -1)
    up4, down4 = from_z(up2[:1], 2), from_z(down2[1:], -2)
    block = jnp.zeros((2, rows, width), bf16)
    pieces = ((0, gram), (1, up1), (-1, down1), (2, up2), (-2, down2), (3, up3), (-3, down3), (4, cat(up4, down4)))
    for step, piece in pieces:
        block = lax.dynamic_update_slice_in_dim(block, piece, ((z_pos + step) % 8) * unit, 1)
    got = from_core(block)
    x_blocks = (own, x_right, x_left, x_far, across, other_right, other_left, other_far)
    found, sent = found_part(got, x_blocks, found_part(block, x_blocks))
    right, left, across = gather_first(sent)
    half, few = rows // 2, rows // 4
    via_y = from_y(cat(right[few:], left[few:]))
    via_right = from_x(cat(right[:half], across[:few]), 1)
    via_left = from_x(cat(left[half:], across[:few]), -1)
    across_far = from_x(across, 2)
    begun = open_product(block, got, sent, right, found, own)
    return close_product(few, block, got, (left, across, via_y, via_right, via_left, across_far), begun)


def solution(mesh):
    return jax.shard_map(
        local,
        mesh=mesh,
        in_specs=(P("wide", "narrow"),),
        out_specs=P("wide", "narrow"),
        check_vma=False,
    )
```

```python
import functools

import jax
import jax.numpy as jnp
from jax import lax
from jax.experimental import pallas as pl
from jax.experimental.pallas import tpu as pltpu
from jax.sharding import PartitionSpec as P

COLS = 18432

coef_a = 3.4445
coef_b = -4.775
coef_c = 2.0315

Z_SIZE = 8
f32, bf16 = jnp.float32, jnp.bfloat16


def from_x(value, step):
    pairs = [(y * 4 + (x + step) % 4, y * 4 + x) for y in range(2) for x in range(4)]
    return lax.ppermute(value, "wide", pairs)


def from_y(value):
    return lax.ppermute(value, "wide", [(w, (w + 4) % 8) for w in range(8)])


def from_z(value, step):
    pairs = [(((z + step) % 8) * 4 + r, z * 4 + r) for z in range(8) for r in range(4)]
    return lax.ppermute(value, "narrow", pairs)


def from_y_hi(value):
    return lax.ppermute(value, "narrow", [(n, n ^ 2) for n in range(32)])


def from_y_both(value):
    pairs = [((w, n), ((w + 4) % 8, n ^ 2)) for w in range(8) for n in range(32)]
    return lax.ppermute(value, ("wide", "narrow"), [(a * 32 + b, c * 32 + d) for (a, b), (c, d) in pairs])


def from_core(value):
    return lax.ppermute(value, "narrow", [(n, n ^ 1) for n in range(32)])


def rows_of(left, right):
    return lax.dot_general(left, right, (((1,), (1,)), ((), ())), preferred_element_type=f32)


def dot(left, right):
    return jnp.dot(left, right, preferred_element_type=f32)


def cat(*parts, axis=0):
    return jnp.concatenate(parts, axis=axis)


def gather_first(own):
    return from_x(own, 1), from_x(own, -1), from_y(own)


def along_z(value, hops):
    pairs = [(z * 4 + r, (z + hops * (1 - 2 * (r % 2))) % 8 * 4 + r) for z in range(8) for r in range(4)]
    return lax.ppermute(value, "narrow", pairs)


def found_kernel(mine, *refs):
    block_ref, *x_refs = refs[:9]
    if mine:
        found_ref, lhs, rhs, sems = refs[9:]
    else:
        before_ref, found_ref, sent_ref, lhs, rhs, sems = refs[9:]
    rows, cols = x_refs[0].shape
    core = lax.rem(lax.axis_index("narrow"), 2)

    def run(picks):
        copies = [pltpu.make_async_copy(block_ref, lhs, sems.at[4])]
        for at, pick in enumerate(picks):
            copies.append(pltpu.make_async_copy(x_refs[pick], rhs.at[pl.ds(at * rows, rows)], sems.at[at]))
        for copy in copies:
            copy.start()

    @pl.when(core == (0 if mine else 1))
    def _():
        run((0, 1, 4, 5))

    @pl.when(core == (1 if mine else 0))
    def _():
        run((2, 3, 6, 7))

    def wait(at):
        pltpu.make_async_copy(x_refs[at], rhs.at[pl.ds(at * rows, rows)], sems.at[at]).wait()

    parts = [pl.ds(start, min(256, cols - start)) for start in range(0, cols, 256)]
    pltpu.make_async_copy(block_ref, lhs, sems.at[4]).wait()
    wait(0)
    wait(1)
    for part in parts:
        found_ref[:, part] = dot(lhs[0], rhs[: 2 * rows, part])
    wait(2)
    wait(3)
    for part in parts:
        value = found_ref[:, part] + dot(lhs[1], rhs[2 * rows :, part])
        if not mine:
            value = before_ref[:, part] + value
            sent_ref[:, part] = value.astype(bf16)
        found_ref[:, part] = value


def found_part(block, x_blocks, before=None):
    rows, cols = x_blocks[0].shape
    mine = before is None
    found = jax.ShapeDtypeStruct((rows, cols), f32)
    vmem = pl.BlockSpec(memory_space=pltpu.VMEM)
    return pl.pallas_call(
        functools.partial(found_kernel, mine),
        out_shape=found if mine else (found, jax.ShapeDtypeStruct((rows, cols), bf16)),
        in_specs=[pl.BlockSpec(memory_space=pl.ANY)] * 9 + ([] if mine else [vmem]),
        out_specs=vmem if mine else (vmem, vmem),
        scratch_shapes=[
            pltpu.VMEM(block.shape, bf16),
            pltpu.VMEM((4 * rows, cols), bf16),
            pltpu.SemaphoreType.DMA((5,)),
        ],
        compiler_params=pltpu.CompilerParams(vmem_limit_bytes=9 * 2**20),
        cost_estimate=pl.CostEstimate(flops=8 * rows * rows * cols, bytes_accessed=6 * 2**20, transcendentals=0),
    )(block, *x_blocks, *([] if mine else [before]))


def open_kernel(block_ref, got_ref, own_y, right, found_ref, own_ref, begun_ref, lhs, rhs, sems):
    rows, cols = own_ref.shape
    core = lax.rem(lax.axis_index("narrow"), 2)
    copies = [
        pltpu.make_async_copy(block_ref.at[0], lhs.at[core], sems.at[0]),
        pltpu.make_async_copy(got_ref.at[0], lhs.at[1 - core], sems.at[1]),
        pltpu.make_async_copy(own_y, rhs.at[pl.ds(0, rows)], sems.at[2]),
        pltpu.make_async_copy(right, rhs.at[pl.ds(rows, rows)], sems.at[3]),
    ]
    for copy in copies:
        copy.start()
    for copy in copies:
        copy.wait()
    for start in range(0, cols, 256):
        part = pl.ds(start, min(256, cols - start))
        value = coef_a * own_ref[:, part].astype(f32) + coef_b * found_ref[:, part]
        begun_ref[:, part] = value + coef_c * dot(lhs[0], rhs[:, part])


def close_kernel(few, block_ref, got_ref, *refs):
    left, across, via_y, via_right, via_left, across_far = refs[:6]
    begun_ref, out_ref, lhs, rhs, total, sems = refs[6:]
    rows, cols = out_ref.shape
    half, more = rows // 2, rows - few
    core = lax.rem(lax.axis_index("narrow"), 2)

    @pl.when(core == 0)
    def _():
        pltpu.make_async_copy(got_ref.at[0], lhs.at[0], sems.at[0]).start()

    @pl.when(core == 1)
    def _():
        pltpu.make_async_copy(block_ref.at[0], lhs.at[0], sems.at[0]).start()

    pieces = [
        (left, 0),
        (via_right.at[pl.ds(0, half)], rows),
        (via_left.at[pl.ds(0, half)], rows + half),
        (block_ref.at[1], lhs.at[1 + core]),
        (got_ref.at[1], lhs.at[2 - core]),
        (across, 2 * rows),
        (via_right.at[pl.ds(half, few)], 3 * rows),
        (via_y.at[pl.ds(0, more)], 3 * rows + few),
        (via_left.at[pl.ds(half, few)], 4 * rows),
        (via_y.at[pl.ds(more, more)], 4 * rows + few),
        (across_far, 5 * rows),
    ]
    copies = []
    for at, (source, place) in enumerate(pieces):
        target = rhs.at[pl.ds(place, source.shape[0])] if isinstance(place, int) else place
        copies.append(pltpu.make_async_copy(source, target, sems.at[1 + at]))
    for copy in copies:
        copy.start()
    parts = [pl.ds(start, min(256, cols - start)) for start in range(0, cols, 256)]
    width = 2 * rows
    pltpu.make_async_copy(block_ref.at[0], lhs.at[0], sems.at[0]).wait()
    for copy in copies[:3]:
        copy.wait()
    for part in parts:
        total[:, part] = dot(lhs[0], rhs[:width, part])
    for copy in copies[3:8]:
        copy.wait()
    for part in parts:
        total[:, part] += dot(lhs[1], rhs[width : 2 * width, part])
    for copy in copies[8:]:
        copy.wait()
    scale = float(COLS) ** 0.5
    for part in parts:
        value = total[:, part] + dot(lhs[2], rhs[2 * width :, part])
        out_ref[:, part] = (scale * (begun_ref[:, part] + coef_c * value)).astype(bf16)


def open_product(block, got, own_y, right, found, own):
    rows, cols = own.shape
    vmem = pl.BlockSpec(memory_space=pltpu.VMEM)
    return pl.pallas_call(
        open_kernel,
        out_shape=jax.ShapeDtypeStruct((rows, cols), f32),
        in_specs=[pl.BlockSpec(memory_space=pl.ANY)] * 4 + [vmem, vmem],
        out_specs=vmem,
        scratch_shapes=[
            pltpu.VMEM(block.shape, bf16),
            pltpu.VMEM((2 * rows, cols), bf16),
            pltpu.SemaphoreType.DMA((4,)),
        ],
        compiler_params=pltpu.CompilerParams(vmem_limit_bytes=12 * 2**20),
        cost_estimate=pl.CostEstimate(flops=4 * rows * rows * cols, bytes_accessed=5 * 2**20, transcendentals=0),
    )(block, got, own_y, right, found, own)


def close_product(few, block, got, blocks, begun):
    rows, cols = begun.shape
    vmem = pl.BlockSpec(memory_space=pltpu.VMEM)
    return pl.pallas_call(
        functools.partial(close_kernel, few),
        out_shape=jax.ShapeDtypeStruct((rows, cols), bf16),
        in_specs=[pl.BlockSpec(memory_space=pltpu.HBM)] * 8 + [vmem],
        out_specs=vmem,
        scratch_shapes=[
            pltpu.VMEM((3, *block.shape[1:]), bf16),
            pltpu.VMEM((6 * rows, cols), bf16),
            pltpu.VMEM((rows, cols), f32),
            pltpu.SemaphoreType.DMA((12,)),
        ],
        compiler_params=pltpu.CompilerParams(vmem_limit_bytes=16 * 2**20),
        cost_estimate=pl.CostEstimate(flops=12 * rows * rows * cols, bytes_accessed=9 * 2**20, transcendentals=0),
    )(block, got, *blocks, begun)


def local(own):
    rows = own.shape[0]
    narrow_pos = lax.axis_index("narrow")
    core = narrow_pos % 2
    z_pos = narrow_pos // 4
    unit = rows // Z_SIZE

    right, left, across = gather_first(own)
    half_rows = rows // 2
    far = cat(from_x(right[:half_rows], 1), from_x(left[half_rows:], -1))
    same = cat(own, right, left, far)
    x_right, x_left, x_far = right, left, far

    both = cat(own, across)
    order = ((0, 4), (0, 3), (1, 3), (0, 2), (1, 2), (0, 1), (1, 1), (1, 0))

    def units_of(core):
        def place(which, step):
            owner = jnp.where(core == 0, which, 1 - which)
            return owner * rows + ((z_pos + step * (1 - 2 * core)) % 8) * unit

        return cat(*[lax.dynamic_slice_in_dim(both, place(*at), unit, 0) for at in order])

    given = rows_of(units_of(1 - core), same).astype(bf16)
    kept = lax.optimization_barrier(rows_of(units_of(core), same))
    summed = kept + from_core(given).astype(f32)

    def units(start, stop):
        return summed[start * unit : stop * unit]

    passed = along_z(units(1, 3).astype(bf16), 1).astype(f32) + jnp.pad(along_z(units(0, 1).astype(bf16), 2).astype(f32), ((0, unit), (0, 0)))
    two, one, late_across, late_far = lax.optimization_barrier(
        ((units(3, 5) + passed).astype(bf16), units(5, 7).astype(bf16), across, far)
    )
    passed = along_z(two, 2).astype(f32) + along_z(one, 1).astype(f32)
    total = passed + jnp.pad(units(7, 8), ((unit, 0), (0, 0)))
    others = (from_x(late_across, 1), from_x(late_across, -1), from_y(late_far))

    width = 2 * rows
    total = total.reshape(2, unit, 2 * width)
    given = from_core(lax.dynamic_slice_in_dim(total, (1 - core) * width, width, 2).astype(bf16))
    total = lax.dynamic_slice_in_dim(total, core * width, width, 2) + cat(given[1:], given[:1]).astype(f32)
    total = total.astype(bf16)
    kept = jnp.where(core == 0, total[0], total[1])
    given = jnp.where(core == 0, total[1], total[0])

    gram_same = kept.astype(f32) + from_y_hi(kept).astype(f32)
    gram_other = from_y(given).astype(f32) + from_y_both(given).astype(f32)
    gram = jnp.stack([gram_same, gram_other]).astype(bf16)

    gram, other_right, other_left, other_far = lax.optimization_barrier((gram, *others))

    up1, down1 = from_z(gram, 1), from_z(gram, -1)
    up2, down2 = from_z(gram, 2), from_z(gram, -2)
    up3, down3 = from_z(up2, 1), from_z(down2, -1)
    up4, down4 = from_z(up2[:1], 2), from_z(down2[1:], -2)
    block = jnp.zeros((2, rows, width), bf16)
    pieces = ((0, gram), (1, up1), (-1, down1), (2, up2), (-2, down2), (3, up3), (-3, down3), (4, cat(up4, down4)))
    for step, piece in pieces:
        block = lax.dynamic_update_slice_in_dim(block, piece, ((z_pos + step) % 8) * unit, 1)
    got = from_core(block)
    x_blocks = (own, x_right, x_left, x_far, across, other_right, other_left, other_far)
    found, sent = found_part(got, x_blocks, found_part(block, x_blocks))
    right, left, across = gather_first(sent)
    half, few = rows // 2, rows // 4
    via_y = from_y(cat(right[few:], left[few:]))
    via_right = from_x(cat(right[:half], across[:few]), 1)
    via_left = from_x(cat(left[half:], across[:few]), -1)
    across_far = from_x(across, 2)
    begun = open_product(block, got, sent, right, found, own)
    return close_product(few, block, got, (left, across, via_y, via_right, via_left, across_far), begun)


def solution(mesh):
    return jax.shard_map(
        local,
        mesh=mesh,
        in_specs=(P("wide", "narrow"),),
        out_specs=P("wide", "narrow"),
        check_vma=False,
    )
```
